32 devices in a mesh: replica: 4 (over z), shard: 4 (over y, core), tensor: 2 (over x).
Axes of the slice: x: 2, y: 2, z: 4, core: 2. Of those that a mesh axis runs over, the one named last changes fastest.
Arguments:
- trained_up: bfloat16 [4, 1024, 4096], P('replica', None, 'tensor'), may hold values from -6 to 6
- trained_down: bfloat16 [4, 4096, 1024], P('replica', 'tensor'), may hold values from -6 to 6
- trained_embed: bfloat16 [4, 8192, 1024], P('replica', ('shard', 'tensor')), may hold values from -6 to 6
- trained_norm: bfloat16 [4, 2, 1024], P('replica'), may hold values from 0.099609375 to 1.8984375
- master_up: float32 [1024, 4096], P(('replica', 'shard', 'tensor')), may hold values from -6 to 6
- moment_up: float32 [1024, 4096], P(('replica', 'shard', 'tensor')), may hold values from -4 to 4
- master_down: float32 [2, 2048, 1024], P('tensor', ('replica', 'shard')), may hold values from -6 to 6
- moment_down: float32 [2, 2048, 1024], P('tensor', ('replica', 'shard')), may hold values from -4 to 4
- master_embed: float32 [8, 1024, 1024], P(('shard', 'tensor'), 'replica'), may hold values from -6 to 6
- moment_embed: float32 [8, 1024, 64], P(('shard', 'tensor'), 'replica'), may hold values from -4 to 4
- master_norm: float32 [2, 1024], replicated, may hold values from 0.1 to 1.9
- moment_norm: float32 [2, 1024], replicated, may hold values from -2 to 2
- embed_basis: float32 [1024, 64], replicated, may hold values from -0.1875 to 0.1875
Outputs:
- recast_up: bfloat16 [1024, 4096], P(None, 'tensor')
- recast_down: bfloat16 [4096, 1024], P('tensor')
- recast_embed: bfloat16 [8192, 1024], P(('shard', 'tensor'))
- recast_norm: bfloat16 [2, 1024], replicated
- stored_up: float32 [1024, 4096], P(('replica', 'shard', 'tensor'))
- velocity_up: float32 [1024, 4096], P(('replica', 'shard', 'tensor'))
- stored_down: float32 [2, 2048, 1024], P('tensor', ('replica', 'shard'))
- velocity_down: float32 [2, 2048, 1024], P('tensor', ('replica', 'shard'))
- stored_embed: float32 [8, 1024, 1024], P(('shard', 'tensor'), 'replica')
- velocity_embed: float32 [8, 1024, 64], P(('shard', 'tensor'), 'replica')
- stored_norm: float32 [2, 1024], replicated
- velocity_norm: float32 [2, 1024], replicated
The draws below stay inside these ranges and needn't reach their ends.
All inputs are finite; a program needn't handle non-finite values.
Results may differ from the reference program's by a relative error of at most 0.012.
Values may be sent and summed in bfloat16 or wider, within the bound.
No kernel may reach another device: no remote copies, remote signals or barrier semaphores. Data moves between devices by JAX's collectives and lax.ppermute only.
A program may use at most 128 MiB of HBM per device.

```python
import jax
import jax.numpy as jnp
from jax import lax

D = 1024
FF = 4096
RANK = 64
EMB_DEV = 256
EMB_ROWS = 8192
N_REPLICA = 4
N_SHARD = 4
N_TENSOR = 2


def shard_levels(rng, dims, split, smallest, top_value):
    factor_of, own = 1.0, jax.random.fold_in(rng, 6)
    for dim, shards_of in split:
        heights = jnp.exp(jax.random.uniform(jax.random.fold_in(own, dim), (shards_of,), jnp.float32, smallest / len(split), top_value / len(split)))
        factor_of = factor_of * jnp.repeat(heights, dims[dim] // shards_of).reshape([-1 if axis == dim else 1 for axis in range(len(dims))])
    return factor_of


def noise(stream_key, dims, spread, limit, cuts=(), dtype=jnp.bfloat16):
    values = jax.random.normal(stream_key, dims, jnp.float32) * spread
    if len(cuts) > 0:
        values = shard_levels(stream_key, dims, cuts, -0.22, 0.18) * values
    return jnp.clip(values, min=-limit, max=limit).astype(dtype)


def setup_inputs(seed: int = 0) -> dict:
    keys = jax.random.split(jax.random.key(seed), 14)
    return {
        "trained_up": noise(keys[0], (N_REPLICA, D, FF), 1.0, 6.0, ((0, 4), (2, 2))),
        "trained_down": noise(keys[1], (N_REPLICA, FF, D), 1.0, 6.0, ((0, 4), (1, 2))),
        "trained_embed": noise(keys[2], (N_REPLICA, EMB_ROWS, D), 1.0, 6.0, ((0, 4), (1, 8))),
        "trained_norm": jnp.clip(1.0 + 0.18 * jax.random.normal(keys[3], (N_REPLICA, 2, D), jnp.float32), 0.099609375, 1.8984375).astype(jnp.bfloat16),
        "master_up": noise(keys[4], (D, FF), 1.0, 6.0, ((0, 32),), jnp.float32),
        "moment_up": noise(keys[5], (D, FF), 0.5, 4.0, ((0, 32),), jnp.float32),
        "master_down": noise(keys[6], (N_TENSOR, FF // N_TENSOR, D), 1.0, 6.0, ((0, 2), (1, 16)), jnp.float32),
        "moment_down": noise(keys[7], (N_TENSOR, FF // N_TENSOR, D), 0.5, 4.0, ((0, 2), (1, 16)), jnp.float32),
        "master_embed": noise(keys[8], (N_SHARD * N_TENSOR, N_REPLICA * EMB_DEV, D), 1.0, 6.0, ((0, 8), (1, 4)), jnp.float32),
        "moment_embed": noise(keys[9], (N_SHARD * N_TENSOR, N_REPLICA * EMB_DEV, RANK), 0.5, 4.0, ((0, 8), (1, 4)), jnp.float32),
        "master_norm": jnp.clip(1.0 + 0.18 * jax.random.normal(keys[10], (2, D), jnp.float32), 0.1, 1.9),
        "moment_norm": noise(keys[11], (2, D), 0.2, 2.0, (), jnp.float32),
        "embed_basis": noise(keys[12], (D, RANK), D ** -0.5, 0.1875, (), jnp.float32),
    }


def outer_step(master, moment, summed, groups):
    difference = master - summed / groups
    velocity = 0.5 * moment + difference
    return master - 0.7 * (difference + 0.5 * velocity), velocity


def reference(trained_up, trained_down, trained_embed, trained_norm, master_up, moment_up, master_down, moment_down, master_embed, moment_embed, master_norm, moment_norm, embed_basis):
    up_total = jnp.sum(trained_up.astype(jnp.float32), axis=0)
    stored_up, velocity_up = outer_step(master_up, moment_up, up_total, N_REPLICA)
    down_total = jnp.sum(trained_down.astype(jnp.float32), axis=0).reshape(N_TENSOR, FF // N_TENSOR, D)
    stored_down, velocity_down = outer_step(master_down, moment_down, down_total, N_REPLICA)
    norm_total = jnp.sum(trained_norm.astype(jnp.float32), axis=0)
    stored_norm, velocity_norm = outer_step(master_norm, moment_norm, norm_total, N_REPLICA)
    embed_total = jnp.zeros((EMB_ROWS, D), jnp.float32)
    for group in range(N_REPLICA):
        embed_total = embed_total + trained_embed[group].astype(jnp.float32)
    flat_master = master_embed.reshape(EMB_ROWS, D)
    coefficient = jnp.dot(flat_master - embed_total / N_REPLICA, embed_basis, precision=lax.Precision.HIGHEST)
    velocity_flat = 0.5 * moment_embed.reshape(EMB_ROWS, RANK) + coefficient
    stored_flat = flat_master - 0.7 * jnp.dot(coefficient + 0.5 * velocity_flat, embed_basis.T, precision=lax.Precision.HIGHEST)
    return (stored_up.astype(jnp.bfloat16), stored_down.reshape(FF, D).astype(jnp.bfloat16), stored_flat.astype(jnp.bfloat16), stored_norm.astype(jnp.bfloat16), stored_up, velocity_up, stored_down, velocity_down, stored_flat.reshape(master_embed.shape), velocity_flat.reshape(moment_embed.shape), stored_norm, velocity_norm)
```

```python
import functools

import jax
import jax.numpy as jnp
from jax import lax
from jax.experimental import pallas as pl
from jax.experimental.pallas import tpu as pltpu
from jax.sharding import PartitionSpec as P

F32 = jnp.float32
BF16 = jnp.bfloat16


def outer_step(master, moment, summed, groups):
    difference = master - summed / groups
    velocity = 0.5 * moment + difference
    return (master - 0.7 * (difference + 0.5 * velocity), velocity)


def line_reduce(block, replicas, pos):
    right = left = None
    for step in range(1, replicas):
        ahead = block(jnp.minimum(pos + replicas - step, replicas - 1))
        behind = block(jnp.maximum(pos - replicas + step, 0))
        if right is not None:
            ahead = (ahead.astype(F32) + right.astype(F32)).astype(BF16)
            behind = (behind.astype(F32) + left.astype(F32)).astype(BF16)
        right = lax.ppermute(ahead, "replica", [(i, i + 1) for i in range(step)])
        left = lax.ppermute(
            behind, "replica", [(i, i - 1) for i in range(replicas - step, replicas)]
        )
    return block(pos).astype(F32) + right.astype(F32) + left.astype(F32)


def gather_pieces(piece, replicas, shards, pos):
    top = shards // 2

    def across(x, valid):
        pairs = [(i * shards + j, i * shards + (j ^ top)) for i in valid for j in range(shards)]
        return lax.ppermute(x, ("replica", "shard"), pairs)

    rights, lefts, far_rights, far_lefts = [None], [None], [None], [None]
    right = left = piece
    far = across(piece, range(replicas))
    for step in range(1, replicas):
        right = lax.ppermute(right, "replica", [(i, i + 1) for i in range(step - 1, replicas - 1)])
        left = lax.ppermute(left, "replica", [(i, i - 1) for i in range(1, replicas - step + 1)])
        rights.append(right)
        lefts.append(left)
        far_rights.append(across(right, range(step, replicas)))
        far_lefts.append(across(left, range(replicas - step)))
    pairs = {(0, 0): jnp.stack([piece, far])}
    for slot in range(1, replicas):
        below = pos >= slot
        pairs[slot, 0] = jnp.stack(
            [
                jnp.where(below, rights[slot], lefts[replicas - slot]),
                jnp.where(below, far_rights[slot], far_lefts[replicas - slot]),
            ]
        )
    bit = top // 2
    while bit:
        for (slot, mask), pair in list(pairs.items()):
            swapped = lax.ppermute(pair, "shard", [(j, j ^ bit) for j in range(shards)])
            pairs[slot, mask ^ bit] = swapped
        bit //= 2
    return pairs


def place_kernel(keys, replicas, top, *refs):
    sources, out, sem = refs[: len(keys)], refs[len(keys)], refs[len(keys) + 1]
    pos, me = lax.axis_index("replica"), lax.axis_index("shard")
    copies = []
    for source, (slot, mask) in zip(sources, keys):
        owner = lax.rem(pos + replicas - slot, replicas)
        for half in range(2):
            shard = jnp.bitwise_xor(me, mask ^ (top * half))
            copy = pltpu.make_async_copy(
                source.at[half], out.at[owner, shard], sem.at[len(copies)]
            )
            copy.start()
            copies.append(copy)
    for copy in copies:
        copy.wait()


def place(pairs, replicas, shards):
    keys = list(pairs)
    sources = [pairs[key] for key in keys]
    piece = sources[0].shape[1:]
    size = 2 * len(keys) * sources[0].size
    return pl.pallas_call(
        functools.partial(place_kernel, keys, replicas, shards // 2),
        out_shape=jax.ShapeDtypeStruct((replicas, shards) + piece, BF16),
        in_specs=[pl.BlockSpec(memory_space=pl.ANY)] * len(keys),
        out_specs=pl.BlockSpec(memory_space=pl.ANY),
        scratch_shapes=[pltpu.SemaphoreType.DMA((2 * len(keys),))],
        cost_estimate=pl.CostEstimate(flops=0, bytes_accessed=2 * size, transcendentals=0),
        name="place_pieces",
    )(*sources)


def body(
    trained_up,
    trained_down,
    trained_embed,
    trained_norm,
    master_up,
    moment_up,
    master_down,
    moment_down,
    master_embed,
    moment_embed,
    master_norm,
    moment_norm,
    embed_basis,
):
    replicas = lax.axis_size("replica")
    shards = lax.axis_size("shard")
    tensors = lax.axis_size("tensor")
    pos = lax.axis_index("replica")
    shard_pos = lax.axis_index("shard")
    tensor_pos = lax.axis_index("tensor")
    width, rank = embed_basis.shape
    rows_up = master_up.shape[0]
    half_cols = trained_up.shape[2]
    rows_down = master_down.shape[1]
    rows_embed = master_embed.shape[1]

    high = lax.reduce_precision(embed_basis, 8, 7)
    middle = lax.reduce_precision(embed_basis - high, 8, 7)
    low = embed_basis - high - middle
    split = jnp.concatenate([high, middle, low], axis=1).astype(BF16)
    projected = lax.dot_general(
        split, trained_embed[0], (((0,), (1,)), ((), ())), preferred_element_type=F32
    )
    projected = projected[:rank] + projected[rank : 2 * rank] + projected[2 * rank :]
    norm_own = trained_norm[0].astype(F32).reshape(-1, rows_embed)

    def packet(owner):
        block = lax.dynamic_slice_in_dim(projected, owner * rows_embed, rows_embed, axis=1)
        return jnp.concatenate([block, norm_own], axis=0)

    packets = packet(pos)
    for shift in range(1, replicas):
        packets = packets + lax.ppermute(
            packet(lax.rem(pos + shift, replicas)),
            "replica",
            [(i, (i + shift) % replicas) for i in range(replicas)],
        )
    norm_summed = packets[rank:].reshape(master_norm.shape)
    stored_norm, velocity_norm = outer_step(master_norm, moment_norm, norm_summed, replicas)
    embed_own = master_embed[0]
    coefficient = (
        lax.dot_general(
            embed_basis, embed_own, (((0,), (1,)), ((), ())), precision=lax.Precision.HIGHEST
        )
        - packets[:rank] / replicas
    )
    velocity_rows = 0.5 * moment_embed[0].T + coefficient
    stored_rows = embed_own - 0.7 * lax.dot_general(
        coefficient + 0.5 * velocity_rows,
        embed_basis,
        (((0,), (1,)), ((), ())),
        precision=lax.Precision.HIGHEST,
    )
    recast_embed = lax.all_gather(stored_rows.astype(BF16), "replica", axis=0, tiled=True)

    down_blocks = trained_down[0].reshape(replicas, shards, rows_down, width)

    def down_block(owner):
        return lax.dynamic_slice(
            down_blocks, (owner, shard_pos, 0, 0), (1, 1, rows_down, width)
        ).reshape(rows_down, width)

    down_summed = line_reduce(down_block, replicas, pos)
    stored_down, velocity_down = outer_step(master_down, moment_down, down_summed[None], replicas)
    recast_down = place(
        gather_pieces(stored_down[0].astype(BF16), replicas, shards, pos), replicas, shards
    ).reshape(-1, width)

    up_blocks = trained_up[0].reshape(replicas, shards, tensors, rows_up, half_cols)

    def up_rows(tensor):
        return lax.dynamic_slice(
            up_blocks,
            (0, shard_pos, tensor, 0, 0),
            (replicas, 1, 1, rows_up, half_cols),
        ).reshape(replicas, 1, rows_up, half_cols)

    halves = jnp.arange(tensors).reshape(1, tensors, 1, 1)
    up_whole = up_rows(tensor_pos)
    for shift in range(1, tensors):
        came = lax.ppermute(
            up_rows(lax.rem(tensor_pos + shift, tensors)),
            "tensor",
            [(i, (i + shift) % tensors) for i in range(tensors)],
        )
        source = lax.rem(tensor_pos + tensors - shift, tensors)
        up_whole = jnp.where(halves == source, came, up_whole)

    def up_block(owner):
        return lax.dynamic_index_in_dim(up_whole, owner, 0, keepdims=False)

    up_summed = line_reduce(up_block, replicas, pos)
    up_summed = jnp.concatenate([up_summed[i] for i in range(tensors)], axis=1)
    stored_up, velocity_up = outer_step(master_up, moment_up, up_summed, replicas)
    up_recast = stored_up.astype(BF16)

    def up_cols(tensor):
        return lax.dynamic_slice_in_dim(up_recast, tensor * half_cols, half_cols, axis=1)[None]

    up_piece = up_cols(tensor_pos)
    for shift in range(1, tensors):
        came = lax.ppermute(
            up_cols(lax.rem(tensor_pos + shift, tensors)),
            "tensor",
            [(i, (i + shift) % tensors) for i in range(tensors)],
        )
        source = lax.rem(tensor_pos + tensors - shift, tensors)
        up_piece = jnp.where(halves[0] == source, came, up_piece)
    up_piece = up_piece.reshape(tensors * rows_up, half_cols)
    recast_up = place(
        gather_pieces(up_piece, replicas, shards, pos), replicas, shards
    ).reshape(-1, half_cols)

    return (
        recast_up,
        recast_down,
        recast_embed,
        stored_norm.astype(BF16),
        stored_up,
        velocity_up,
        stored_down,
        velocity_down,
        stored_rows[None],
        velocity_rows.T[None],
        stored_norm,
        velocity_norm,
    )


def solution(mesh):
    in_specs = (
        P("replica", None, "tensor"),
        P("replica", "tensor", None),
        P("replica", ("shard", "tensor"), None),
        P("replica", None, None),
        P(("replica", "shard", "tensor"), None),
        P(("replica", "shard", "tensor"), None),
        P("tensor", ("replica", "shard"), None),
        P("tensor", ("replica", "shard"), None),
        P(("shard", "tensor"), "replica", None),
        P(("shard", "tensor"), "replica", None),
        P(),
        P(),
        P(),
    )
    out_specs = (
        P(None, "tensor"),
        P("tensor", None),
        P(("shard", "tensor"), None),
        P(),
        P(("replica", "shard", "tensor"), None),
        P(("replica", "shard", "tensor"), None),
        P("tensor", ("replica", "shard"), None),
        P("tensor", ("replica", "shard"), None),
        P(("shard", "tensor"), "replica", None),
        P(("shard", "tensor"), "replica", None),
        P(),
        P(),
    )
    return jax.shard_map(body, mesh=mesh, in_specs=in_specs, out_specs=out_specs, check_vma=False)
```

```python
import functools

import jax
import jax.numpy as jnp
from jax import lax
from jax.experimental import pallas as pl
from jax.experimental.pallas import tpu as pltpu
from jax.sharding import PartitionSpec as P

F32 = jnp.float32
BF16 = jnp.bfloat16
HIGHEST = lax.Precision.HIGHEST
HBM = pl.BlockSpec(memory_space=pltpu.HBM)
VMEM = pl.BlockSpec(memory_space=pltpu.VMEM)


def outer_step(master, moment, summed, groups):
    difference = master - summed / groups
    velocity = 0.5 * moment + difference
    return (master - 0.7 * (difference + 0.5 * velocity), velocity)


def call(kernel, name, out_shape, in_specs, out_specs, scratch, *operands):
    size = sum(x.size * x.dtype.itemsize for x in jax.tree.leaves(out_shape))
    return pl.pallas_call(
        kernel,
        name=name,
        out_shape=out_shape,
        in_specs=in_specs,
        out_specs=out_specs,
        scratch_shapes=scratch,
        compiler_params=pltpu.CompilerParams(vmem_limit_bytes=24 * 2**20),
        cost_estimate=pl.CostEstimate(flops=0, bytes_accessed=3 * size, transcendentals=0),
    )(*operands)


def swap(x, axis, bit):
    return lax.ppermute(x, axis, [(i, i ^ bit) for i in range(lax.axis_size(axis))])


def bits_down(size):
    bit = size // 2
    while bit:
        yield bit
        bit //= 2


def bits_up(size):
    return reversed(list(bits_down(size)))


def fetch(down, up, owner, shard, dest, sems, first):
    rows, width = down.shape[2:]
    tall, cols = up.shape[2:]
    copies = [
        pltpu.make_async_copy(down.at[owner, shard], dest.at[pl.ds(0, rows)], sems.at[first])
    ]
    for chunk in range(cols // width):
        copies.append(
            pltpu.make_async_copy(
                up.at[owner, shard, :, pl.ds(chunk * width, width)],
                dest.at[pl.ds(rows + chunk * tall, tall)],
                sems.at[first + 1 + chunk],
            )
        )
    for copy in copies:
        copy.start()
    return copies


def project_kernel(trained, basis, norm, *refs):
    *outs, projected = refs
    rank, rows = basis.shape[0], outs[0].shape[1]
    high = basis[...].astype(BF16)
    rest = basis[...] - high.astype(F32)
    middle = rest.astype(BF16)
    low = (rest - middle.astype(F32)).astype(BF16)
    split = jnp.concatenate([high, middle, low], axis=0)
    product = lax.dot_general(
        split, trained[...], (((1,), (1,)), ((), ())), preferred_element_type=F32
    )
    projected[...] = product[:rank] + (product[rank : 2 * rank] + product[2 * rank :])
    pos = lax.axis_index("replica")
    values = norm[...].astype(F32)
    per = norm.shape[1] // rows
    for mask, out in enumerate(outs):
        owner = jnp.bitwise_xor(pos, mask)
        out[:rank, :] = projected[:, pl.ds(pl.multiple_of(owner * rows, rows), rows)]
        for i in range(norm.shape[0] * per):
            part = values[i // per : i // per + 1, (i % per) * rows : (i % per + 1) * rows]
            out[rank + i : rank + i + 1, :] = part


def pack_kernel(masks, down, up, *refs):
    *outs, sems = refs
    pos, shard = lax.axis_index("replica"), lax.axis_index("shard")
    each = 1 + up.shape[3] // down.shape[3]
    copies = []
    for i, mask in enumerate(masks):
        owner = jnp.bitwise_xor(pos, mask)
        copies += fetch(down, up, owner, shard, outs[i], sems, i * each)
    for copy in copies:
        copy.wait()


def add_kernel(mask, down, up, came, out, block, sems):
    pos, shard = lax.axis_index("replica"), lax.axis_index("shard")
    for copy in fetch(down, up, jnp.bitwise_xor(pos, mask), shard, block, sems, 0):
        copy.wait()
    out[...] = (block[...].astype(F32) + came[...].astype(F32)).astype(BF16)


def update_kernel(groups, tensors, n_came, *refs):
    refs = list(refs)
    down, up, master_down, moment_down, master_up, moment_up = refs[:6]
    came, state_came = refs[6 : 6 + n_came], refs[6 + n_came : 5 + n_came + tensors]
    piece, stored_down, velocity_down = refs[5 + n_came + tensors : 8 + n_came + tensors]
    sums = refs[8 + n_came + tensors : 8 + n_came + 2 * tensors]
    block, summed, master, moment, sems = refs[8 + n_came + 2 * tensors :]
    pos, shard = lax.axis_index("replica"), lax.axis_index("shard")
    me = lax.axis_index("tensor")
    copies = fetch(down, up, pos, shard, block, sems, 0)
    rows_down, width = master_down.shape
    rows_up = master_up.shape[0]
    tall, cols = summed.shape

    def at(index):
        return pl.ds(pl.multiple_of(index * rows_up, rows_up), rows_up)

    own_cols = pl.ds(pl.multiple_of(me * cols, cols), cols)
    master[at(me), :] = master_up[:, own_cols]
    moment[at(me), :] = moment_up[:, own_cols]
    for shift in range(1, tensors):
        source = lax.rem(me + tensors - shift, tensors)
        master[at(source), :] = state_came[shift - 1][0]
        moment[at(source), :] = state_came[shift - 1][1]
    for copy in copies:
        copy.wait()

    def total(lo, hi):
        value = block[lo:hi, :].astype(F32)
        for ref in came:
            value = value + ref[lo:hi, :].astype(F32)
        return value

    stored, velocity = outer_step(
        master_down[...], moment_down[...], total(0, rows_down), groups
    )
    stored_down[...] = stored
    velocity_down[...] = velocity
    piece[:rows_down, :] = stored.astype(BF16)
    for chunk in range(cols // width):
        lo = rows_down + chunk * tall
        part = total(lo, lo + tall)
        span = slice(chunk * width, (chunk + 1) * width)
        summed[:, span] = part
        stored, _ = outer_step(master[:, span], moment[:, span], part, groups)
        piece[lo : lo + tall, :] = stored.astype(BF16)
    for shift in range(tensors):
        sums[shift][...] = summed[at(lax.rem(me + shift, tensors)), :]


def up_kernel(groups, tensors, master_up, moment_up, *refs):
    sums, (stored_up, velocity_up) = refs[:tensors], refs[tensors:]
    cols = sums[0].shape[1]
    me = lax.axis_index("tensor")
    for shift in range(tensors):
        source = lax.rem(me + tensors - shift, tensors)
        span = pl.ds(pl.multiple_of(source * cols, cols), cols)
        stored, velocity = outer_step(
            master_up[:, span], moment_up[:, span], sums[shift][...], groups
        )
        stored_up[:, span] = stored
        velocity_up[:, span] = velocity


def state_kernel(tensors, master_up, moment_up, *outs):
    me = lax.axis_index("tensor")
    cols = outs[0].shape[2]
    for shift in range(1, tensors):
        target = lax.rem(me + shift, tensors)
        span = pl.ds(pl.multiple_of(target * cols, cols), cols)
        outs[shift - 1][0] = master_up[:, span]
        outs[shift - 1][1] = moment_up[:, span]


def place_kernel(keys, *refs):
    count = len(keys)
    pieces, (down, up, sems) = refs[:count], refs[count:]
    pos, shard = lax.axis_index("replica"), lax.axis_index("shard")
    rows, width = down.shape[2:]
    tall, cols = up.shape[2:]
    copies = []

    def send(source, dest):
        copies.append(pltpu.make_async_copy(source, dest, sems.at[len(copies)]))
        copies[-1].start()

    for piece, (far, mask) in zip(pieces, keys):
        owner, place = jnp.bitwise_xor(pos, far), jnp.bitwise_xor(shard, mask)
        send(piece.at[pl.ds(0, rows)], down.at[owner, place])
        for chunk in range(cols // width):
            send(
                piece.at[pl.ds(rows + chunk * tall, tall)],
                up.at[owner, place, :, pl.ds(chunk * width, width)],
            )
    for copy in copies:
        copy.wait()


def place_embed_kernel(masks, *refs):
    count = len(masks)
    pieces, (out, sems) = refs[:count], refs[count:]
    pos = lax.axis_index("replica")
    copies = [
        pltpu.make_async_copy(piece, out.at[jnp.bitwise_xor(pos, mask)], sems.at[i])
        for i, (piece, mask) in enumerate(zip(pieces, masks))
    ]
    for copy in copies:
        copy.start()
    for copy in copies:
        copy.wait()


def spread(pieces, axis):
    for bit in bits_down(lax.axis_size(axis)):
        pieces.update({mask ^ bit: swap(x, axis, bit) for mask, x in list(pieces.items())})
    return pieces


def body(
    trained_up,
    trained_down,
    trained_embed,
    trained_norm,
    master_up,
    moment_up,
    master_down,
    moment_down,
    master_embed,
    moment_embed,
    master_norm,
    moment_norm,
    embed_basis,
):
    replicas = lax.axis_size("replica")
    shards = lax.axis_size("shard")
    tensors = lax.axis_size("tensor")
    width, rank = embed_basis.shape
    rows_up, half_cols = master_up.shape[0], trained_up.shape[2]
    rows_down, rows_embed = master_down.shape[1], master_embed.shape[1]
    tall = tensors * rows_up
    chunks = half_cols // width
    packed = jax.ShapeDtypeStruct((rows_down + chunks * tall, width), BF16)
    dma = pltpu.SemaphoreType.DMA

    norm_rows = trained_norm.shape[1] * width // rows_embed
    basis_t = embed_basis.T
    packet = jax.ShapeDtypeStruct((rank + norm_rows, rows_embed), F32)
    packets = call(
        project_kernel,
        "project_rows",
        [packet] * replicas,
        [VMEM] * 3,
        [VMEM] * replicas,
        [pltpu.VMEM((rank, replicas * rows_embed), F32)],
        trained_embed[0],
        basis_t,
        trained_norm[0],
    )
    packet_sum = packets[0]
    for mask in range(1, replicas):
        packet_sum = packet_sum + swap(packets[mask], "replica", mask)
    norm_summed = packet_sum[rank:].reshape(master_norm.shape)
    stored_norm, velocity_norm = outer_step(master_norm, moment_norm, norm_summed, replicas)
    embed_own = master_embed[0]
    coefficient = (
        lax.dot_general(basis_t, embed_own, (((1,), (1,)), ((), ())), precision=HIGHEST)
        - packet_sum[:rank] / replicas
    )
    velocity_rows = 0.5 * moment_embed[0].T + coefficient
    stored_rows = embed_own - 0.7 * lax.dot_general(
        coefficient + 0.5 * velocity_rows,
        basis_t,
        (((0,), (0,)), ((), ())),
        precision=HIGHEST,
    )
    embed_pieces = spread({0: stored_rows.astype(BF16)}, "replica")
    recast_embed = call(
        functools.partial(place_embed_kernel, list(embed_pieces)),
        "place_embed",
        jax.ShapeDtypeStruct((replicas, rows_embed, width), BF16),
        [VMEM] * replicas,
        HBM,
        [dma((replicas,))],
        *embed_pieces.values(),
    ).reshape(-1, width)

    state = jax.ShapeDtypeStruct((2, rows_up, half_cols), F32)
    states = call(
        functools.partial(state_kernel, tensors),
        "up_state",
        [state] * (tensors - 1),
        [VMEM] * 2,
        [VMEM] * (tensors - 1),
        [],
        master_up,
        moment_up,
    )
    states = [
        lax.ppermute(x, "tensor", [(i, (i + shift) % tensors) for i in range(tensors)])
        for shift, x in enumerate(states, 1)
    ]

    down = trained_down[0].reshape(replicas, shards, rows_down, width)
    up = trained_up[0].reshape(replicas, shards, tall, half_cols)
    partial_sums = {}
    for bit in bits_up(replicas):
        masks = [m for m in range(replicas) if m % bit == 0 and m & bit]
        masks.sort(key=lambda m: m == bit)
        if not partial_sums:
            sends = call(
                functools.partial(pack_kernel, masks),
                "pack_blocks",
                [packed] * len(masks),
                [HBM] * 2,
                [VMEM] * len(masks),
                [dma((len(masks) * (1 + chunks),))],
                down,
                up,
            )
        else:
            sends = []
            for mask in masks:
                came = partial_sums.pop(mask)
                for extra in came[1:]:
                    came[0] = (came[0].astype(F32) + extra.astype(F32)).astype(BF16)
                sends.append(
                    call(
                        functools.partial(add_kernel, mask),
                        "add_block",
                        packed,
                        [HBM] * 2 + [VMEM],
                        VMEM,
                        [pltpu.VMEM(packed.shape, BF16), dma((1 + chunks,))],
                        down,
                        up,
                        came[0],
                    )
                )
        for mask, x in zip(masks, sends):
            partial_sums.setdefault(mask ^ bit, []).append(swap(x, "replica", bit))
    came = partial_sums[0]
    half_sum = jax.ShapeDtypeStruct((rows_up, half_cols), F32)
    down_state = jax.ShapeDtypeStruct((rows_down, width), F32)
    piece, stored_down, velocity_down, *sums = call(
        functools.partial(update_kernel, replicas, tensors, len(came)),
        "update_rows",
        [packed, down_state, down_state] + [half_sum] * tensors,
        [HBM] * 2 + [VMEM] * (4 + len(came) + len(states)),
        [VMEM] * (3 + tensors),
        [pltpu.VMEM(packed.shape, BF16)]
        + [pltpu.VMEM((tall, half_cols), F32)] * 3
        + [dma((1 + chunks,))],
        down,
        up,
        master_down[0],
        moment_down[0],
        master_up,
        moment_up,
        *came,
        *states,
    )
    sums = [sums[0]] + [
        lax.ppermute(x, "tensor", [(i, (i + shift) % tensors) for i in range(tensors)])
        for shift, x in enumerate(sums[1:], 1)
    ]
    stored_up, velocity_up = call(
        functools.partial(up_kernel, replicas, tensors),
        "update_up",
        [jax.ShapeDtypeStruct(master_up.shape, F32)] * 2,
        [VMEM] * (2 + tensors),
        [VMEM] * 2,
        [],
        master_up,
        moment_up,
        *sums,
    )

    pieces = {}
    for far, x in spread({0: piece}, "replica").items():
        for mask, y in spread({0: x}, "shard").items():
            pieces[far, mask] = y
    recast_down, recast_up = call(
        functools.partial(place_kernel, list(pieces)),
        "place_rows",
        [
            jax.ShapeDtypeStruct(down.shape, BF16),
            jax.ShapeDtypeStruct(up.shape, BF16),
        ],
        [VMEM] * len(pieces),
        [HBM] * 2,
        [dma((len(pieces) * (1 + chunks),))],
        *pieces.values(),
    )

    return (
        recast_up.reshape(-1, half_cols),
        recast_down.reshape(-1, width),
        recast_embed,
        stored_norm.astype(BF16),
        stored_up,
        velocity_up,
        stored_down[None],
        velocity_down[None],
        stored_rows[None],
        velocity_rows.T[None],
        stored_norm,
        velocity_norm,
    )


def solution(mesh):
    in_specs = (
        P("replica", None, "tensor"),
        P("replica", "tensor", None),
        P("replica", ("shard", "tensor"), None),
        P("replica", None, None),
        P(("replica", "shard", "tensor"), None),
        P(("replica", "shard", "tensor"), None),
        P("tensor", ("replica", "shard"), None),
        P("tensor", ("replica", "shard"), None),
        P(("shard", "tensor"), "replica", None),
        P(("shard", "tensor"), "replica", None),
        P(),
        P(),
        P(),
    )
    out_specs = (
        P(None, "tensor"),
        P("tensor", None),
        P(("shard", "tensor"), None),
        P(),
        P(("replica", "shard", "tensor"), None),
        P(("replica", "shard", "tensor"), None),
        P("tensor", ("replica", "shard"), None),
        P("tensor", ("replica", "shard"), None),
        P(("shard", "tensor"), "replica", None),
        P(("shard", "tensor"), "replica", None),
        P(),
        P(),
    )
    return jax.shard_map(body, mesh=mesh, in_specs=in_specs, out_specs=out_specs, check_vma=False)
```

```python
import functools

import jax
import jax.numpy as jnp
from jax import lax
from jax.experimental import pallas as pl
from jax.experimental.pallas import tpu as pltpu
from jax.sharding import PartitionSpec as P

F32 = jnp.float32
BF16 = jnp.bfloat16
HIGHEST = lax.Precision.HIGHEST
HBM = pl.BlockSpec(memory_space=pltpu.HBM)
ANY = pl.BlockSpec(memory_space=pl.ANY)
VMEM = pl.BlockSpec(memory_space=pltpu.VMEM)


def outer_step(master, moment, summed, groups):
    difference = master - summed / groups
    velocity = 0.5 * moment + difference
    return (master - 0.7 * (difference + 0.5 * velocity), velocity)


def call(kernel, name, out_shape, in_specs, out_specs, scratch, *operands, limit=24, aliases={}):
    size = sum(x.size * x.dtype.itemsize for x in jax.tree.leaves(out_shape))
    return pl.pallas_call(
        kernel,
        name=name,
        out_shape=out_shape,
        in_specs=in_specs,
        out_specs=out_specs,
        scratch_shapes=scratch,
        input_output_aliases=aliases,
        compiler_params=pltpu.CompilerParams(vmem_limit_bytes=limit * 2**20),
        cost_estimate=pl.CostEstimate(flops=0, bytes_accessed=3 * size, transcendentals=0),
    )(*operands)


def swap(x, axis, bit):
    return lax.ppermute(x, axis, [(i, i ^ bit) for i in range(lax.axis_size(axis))])


def bits_down(size):
    bit = size // 2
    while bit:
        yield bit
        bit //= 2


def project_kernel(trained, basis, norm, own, *refs):
    *outs, projected = refs
    rank, rows = basis.shape[0], own.shape[1]
    high = basis[...].astype(BF16)
    rest = basis[...] - high.astype(F32)
    middle = rest.astype(BF16)
    low = (rest - middle.astype(F32)).astype(BF16)
    split = jnp.concatenate([high, middle, low], axis=0)
    product = lax.dot_general(
        split, trained[...], (((1,), (1,)), ((), ())), preferred_element_type=F32
    )
    projected[...] = product[:rank] + (product[rank : 2 * rank] + product[2 * rank :])
    pos = lax.axis_index("replica")
    values = norm[...].astype(F32)
    per = norm.shape[1] // rows
    extra = outs[0].shape[0] - rank
    parts = [
        values[i // per : i // per + 1, (i % per) * rows : (i % per + 1) * rows]
        for i in range(norm.shape[0] * per)
    ]
    parts = jnp.concatenate((parts * extra)[:extra], axis=0).astype(BF16)
    own[...] = projected[:, pl.ds(pl.multiple_of(pos * rows, rows), rows)]
    for mask, out in enumerate(outs, 1):
        owner = jnp.bitwise_xor(pos, mask)
        block = projected[:, pl.ds(pl.multiple_of(owner * rows, rows), rows)]
        out[:rank, :] = block.astype(BF16)
        out[rank:, :] = parts


def embed_kernel(groups, n_came, *refs):
    refs = list(refs)
    own, base, master, moment, basis, norm, master_norm, moment_norm = refs[:8]
    came = refs[8 : 8 + n_came]
    stored, recast, velocity, norm_cast, norm_stored, norm_velocity = refs[-6:]
    rank, rows = own.shape
    total = own[...]
    for ref in came:
        total = total + ref[:rank, :].astype(F32)
    coefficient = base[...] - total / groups
    moved = 0.5 * moment[...] + coefficient
    velocity[...] = moved
    change = lax.dot_general(
        coefficient + 0.5 * moved,
        basis[...],
        (((0,), (0,)), ((), ())),
        precision=HIGHEST,
        preferred_element_type=F32,
    )
    new = master[...] - 0.7 * change
    stored[...] = new
    recast[...] = new.astype(BF16)
    per = norm.shape[1] // rows
    values = norm[...].astype(F32)
    tails = [ref[rank:, :].astype(F32) for ref in came]
    for i in range(norm.shape[0] * per):
        row, span = i // per, slice((i % per) * rows, (i % per + 1) * rows)
        summed = values[row : row + 1, span]
        for tail in tails:
            summed = summed + tail[i : i + 1, :]
        new_norm, moved_norm = outer_step(
            master_norm[row : row + 1, span], moment_norm[row : row + 1, span], summed, groups
        )
        norm_stored[row : row + 1, span] = new_norm
        norm_velocity[row : row + 1, span] = moved_norm
    norm_cast[...] = norm_stored[...].astype(BF16)


def pack_kernel(masks, down, up, *refs):
    *outs, sems = refs
    pos, shard = lax.axis_index("replica"), lax.axis_index("shard")
    rows, width = down.shape[2:]
    tall, cols = up.shape[2:]
    copies = []

    def bring(source, dest):
        copies.append(pltpu.make_async_copy(source, dest, sems.at[len(copies)]))
        copies[-1].start()

    for mask, out in zip(masks, outs):
        owner = jnp.bitwise_xor(pos, mask)
        bring(down.at[owner, shard], out.at[pl.ds(0, rows)])
        for chunk in range(cols // width):
            bring(
                up.at[owner, shard, :, pl.ds(chunk * width, width)],
                out.at[pl.ds(rows + chunk * tall, tall)],
            )
    for copy in copies:
        copy.wait()


def add_kernel(block, came, later, out, later_out):
    out[...] = (block[...].astype(F32) + came[...].astype(F32)).astype(BF16)
    later_out[...] = later[...]


def update_kernel(groups, tensors, n_came, *refs):
    refs = list(refs)
    master_down, moment_down, master_up, moment_up, embed = refs[:5]
    came, state_came = refs[5 : 5 + n_came], refs[5 + n_came : 4 + n_came + tensors]
    piece, embed_out, stored_down, velocity_down, *sums = refs[4 + n_came + tensors : -3]
    summed, master, moment = refs[-3:]
    me = lax.axis_index("tensor")
    rows_down, width = master_down.shape
    rows_up = master_up.shape[0]
    tall, cols = summed.shape

    def at(index):
        return pl.ds(pl.multiple_of(index * rows_up, rows_up), rows_up)

    own_cols = pl.ds(pl.multiple_of(me * cols, cols), cols)
    master[at(me), :] = master_up[:, own_cols]
    moment[at(me), :] = moment_up[:, own_cols]
    for shift in range(1, tensors):
        source = lax.rem(me + tensors - shift, tensors)
        master[at(source), :] = state_came[shift - 1][0]
        moment[at(source), :] = state_came[shift - 1][1]

    def total(lo, hi):
        value = came[0][lo:hi, :].astype(F32)
        for ref in came[1:]:
            value = value + ref[lo:hi, :].astype(F32)
        return value

    stored, velocity = outer_step(
        master_down[...], moment_down[...], total(0, rows_down), groups
    )
    stored_down[...] = stored
    velocity_down[...] = velocity
    piece[:rows_down, :] = stored.astype(BF16)
    for chunk in range(cols // width):
        lo = rows_down + chunk * tall
        part = total(lo, lo + tall)
        span = slice(chunk * width, (chunk + 1) * width)
        summed[:, span] = part
        stored, _ = outer_step(master[:, span], moment[:, span], part, groups)
        piece[lo : lo + tall, :] = stored.astype(BF16)
    for shift in range(tensors):
        sums[shift][...] = summed[at(lax.rem(me + shift, tensors)), :]
    embed_out[...] = embed[...]


def up_kernel(groups, tensors, master_up, moment_up, *refs):
    sums, (stored_up, velocity_up, token) = refs[:tensors], refs[tensors:]
    cols = sums[0].shape[1]
    me = lax.axis_index("tensor")
    for shift in range(tensors):
        source = lax.rem(me + tensors - shift, tensors)
        span = pl.ds(pl.multiple_of(source * cols, cols), cols)
        stored, velocity = outer_step(
            master_up[:, span], moment_up[:, span], sums[shift][...], groups
        )
        stored_up[:, span] = stored
        velocity_up[:, span] = velocity
    token[...] = jnp.zeros_like(token)


def state_kernel(tensors, master_up, moment_up, *outs):
    me = lax.axis_index("tensor")
    cols = outs[0].shape[2]
    for shift in range(1, tensors):
        target = lax.rem(me + shift, tensors)
        span = pl.ds(pl.multiple_of(target * cols, cols), cols)
        outs[shift - 1][0] = master_up[:, span]
        outs[shift - 1][1] = moment_up[:, span]


def gate_kernel(x, *refs):
    refs[-1][...] = x[...]


def gate(x, *after):
    return call(
        gate_kernel,
        "gate",
        jax.ShapeDtypeStruct(x.shape, x.dtype),
        [VMEM] + [ANY] * len(after),
        VMEM,
        [],
        x,
        *after,
    )


def place_kernel(far, masks, *refs):
    pieces, (down, up, token, sems) = refs[: len(masks)], refs[-4:]
    token[...] = jnp.zeros_like(token)
    pos, shard = lax.axis_index("replica"), lax.axis_index("shard")
    rows, width = down.shape[2:]
    tall, cols = up.shape[2:]
    copies = []

    def send(source, dest):
        copies.append(pltpu.make_async_copy(source, dest, sems.at[len(copies)]))
        copies[-1].start()

    owner = jnp.bitwise_xor(pos, far)
    for piece, mask in zip(pieces, masks):
        place = jnp.bitwise_xor(shard, mask)
        send(piece.at[pl.ds(0, rows)], down.at[owner, place])
        for chunk in range(cols // width):
            send(
                piece.at[pl.ds(rows + chunk * tall, tall)],
                up.at[owner, place, :, pl.ds(chunk * width, width)],
            )
    for copy in copies:
        copy.wait()


def place_embed_kernel(masks, *refs):
    pieces, (out, sems) = refs[: len(masks)], refs[-2:]
    pos = lax.axis_index("replica")
    copies = [
        pltpu.make_async_copy(piece, out.at[jnp.bitwise_xor(pos, mask)], sems.at[i])
        for i, (piece, mask) in enumerate(zip(pieces, masks))
    ]
    for copy in copies:
        copy.start()
    for copy in copies:
        copy.wait()


def spread(pieces, axis):
    for bit in bits_down(lax.axis_size(axis)):
        pieces.update({mask ^ bit: swap(x, axis, bit) for mask, x in list(pieces.items())})
    return pieces


def body(
    trained_up,
    trained_down,
    trained_embed,
    trained_norm,
    master_up,
    moment_up,
    master_down,
    moment_down,
    master_embed,
    moment_embed,
    master_norm,
    moment_norm,
    embed_basis,
):
    replicas = lax.axis_size("replica")
    shards = lax.axis_size("shard")
    tensors = lax.axis_size("tensor")
    width, rank = embed_basis.shape
    rows_up, half_cols = master_up.shape[0], trained_up.shape[2]
    rows_down, rows_embed = master_down.shape[1], master_embed.shape[1]
    tall = tensors * rows_up
    chunks = half_cols // width
    packed = jax.ShapeDtypeStruct((rows_down + chunks * tall, width), BF16)
    dma = pltpu.SemaphoreType.DMA

    basis_t = embed_basis.T
    rank_rows = jax.ShapeDtypeStruct((rank, rows_embed), F32)
    packet = jax.ShapeDtypeStruct((rank + 16, rows_embed), BF16)
    own_rows, *packets = call(
        project_kernel,
        "project_rows",
        [rank_rows] + [packet] * (replicas - 1),
        [VMEM] * 3,
        [VMEM] * replicas,
        [pltpu.VMEM((rank, replicas * rows_embed), F32)],
        trained_embed[0],
        basis_t,
        trained_norm[0],
    )
    packets_came = [swap(x, "replica", mask) for mask, x in enumerate(packets, 1)]

    down = trained_down[0].reshape(replicas, shards, rows_down, width)
    up = trained_up[0].reshape(replicas, shards, tall, half_cols)
    masks = [3, 2, 1, 0]
    block3, block2, block1, block0 = call(
        functools.partial(pack_kernel, masks),
        "pack_blocks",
        [packed] * replicas,
        [HBM] * 2,
        [VMEM] * replicas,
        [dma((replicas * (1 + chunks),))],
        down,
        up,
        limit=61,
    )
    came2 = swap(gate(block3, *packets_came), "replica", 1)

    state = jax.ShapeDtypeStruct((2, rows_up, half_cols), F32)
    states = call(
        functools.partial(state_kernel, tensors),
        "up_state",
        [state] * (tensors - 1),
        [VMEM] * 2,
        [VMEM] * (tensors - 1),
        [],
        master_up,
        moment_up,
    )
    states = [
        lax.ppermute(x, "tensor", [(i, (i + shift) % tensors) for i in range(tensors)])
        for shift, x in enumerate(states, 1)
    ]

    base = lax.dot_general(
        basis_t, master_embed[0], (((1,), (1,)), ((), ())), precision=HIGHEST
    )
    norm_state = jax.ShapeDtypeStruct(master_norm.shape, F32)
    embed_rows = jax.ShapeDtypeStruct((rows_embed, width), BF16)
    stored_rows, recast_rows, velocity_rows, norm_cast, stored_norm, velocity_norm = call(
        functools.partial(embed_kernel, replicas, replicas - 1),
        "embed_update",
        [
            jax.ShapeDtypeStruct((rows_embed, width), F32),
            embed_rows,
            rank_rows,
            jax.ShapeDtypeStruct(master_norm.shape, BF16),
            norm_state,
            norm_state,
        ],
        [VMEM] * (7 + replicas),
        [VMEM] * 6,
        [],
        own_rows,
        base,
        master_embed[0],
        moment_embed[0].T,
        basis_t,
        trained_norm[0],
        master_norm,
        moment_norm,
        *packets_came,
    )

    block2, block1 = call(
        add_kernel,
        "add_block",
        [packed] * 2,
        [VMEM] * 3,
        [VMEM] * 2,
        [],
        block2,
        came2,
        block1,
    )
    came0 = [block0, swap(block1, "replica", 1), swap(block2, "replica", 2)]
    half_sum = jax.ShapeDtypeStruct((rows_up, half_cols), F32)
    down_state = jax.ShapeDtypeStruct((rows_down, width), F32)
    piece, embed_late, stored_down, velocity_down, *sums = call(
        functools.partial(update_kernel, replicas, tensors, len(came0)),
        "update_rows",
        [packed, embed_rows, down_state, down_state] + [half_sum] * tensors,
        [VMEM] * (5 + len(came0) + len(states)),
        [VMEM] * (4 + tensors),
        [pltpu.VMEM((tall, half_cols), F32)] * 3,
        master_down[0],
        moment_down[0],
        master_up,
        moment_up,
        recast_rows,
        *came0,
        *states,
    )

    top = shards // 2
    pieces = {0: piece, 1: swap(piece, "replica", 1), 2: swap(piece, "replica", 2)}
    groups = {0: spread({0: piece}, "shard")}
    groups[1] = spread({0: gate(pieces[1], groups[0][top])}, "shard")
    groups[2] = spread({0: pieces[2]}, "shard")
    pieces[3] = swap(gate(pieces[2], groups[1][top]), "replica", 1)
    groups[3] = spread({0: pieces[3]}, "shard")
    last_far = groups[3][top]
    embed_near = swap(embed_late, "replica", 1)
    embed_far = swap(gate(embed_late, pieces[2]), "replica", 2)
    embed_last = swap(gate(embed_far, last_far), "replica", 1)

    sums = [sums[0]] + [
        lax.ppermute(
            gate(x, last_far), "tensor", [(i, (i + shift) % tensors) for i in range(tensors)]
        )
        for shift, x in enumerate(sums[1:], 1)
    ]
    token_shape = jax.ShapeDtypeStruct((8, 128), F32)
    stored_up, velocity_up, token = call(
        functools.partial(up_kernel, replicas, tensors),
        "update_up",
        [jax.ShapeDtypeStruct(master_up.shape, F32)] * 2 + [token_shape],
        [VMEM] * (2 + tensors),
        [VMEM] * 3,
        [],
        master_up,
        moment_up,
        *sums,
    )

    shapes = [jax.ShapeDtypeStruct(down.shape, BF16), jax.ShapeDtypeStruct(up.shape, BF16)]
    placed = ()
    for far, group in groups.items():
        extra = (token,) if far == replicas - 1 else ()
        count = len(group) + len(extra)
        *placed, placed_token = call(
            functools.partial(place_kernel, far, list(group)),
            "place_rows",
            shapes + [token_shape],
            [VMEM] * count + [HBM] * len(placed),
            [HBM] * 2 + [VMEM],
            [dma((len(group) * (1 + chunks),))],
            *group.values(),
            *extra,
            *placed,
            aliases={count: 0, count + 1: 1} if placed else {},
        )
    recast_down, recast_up = placed

    embed_shape = jax.ShapeDtypeStruct((replicas, rows_embed, width), BF16)
    recast_embed = call(
        functools.partial(place_embed_kernel, [0, 1]),
        "place_embed",
        embed_shape,
        [VMEM] * 2,
        HBM,
        [dma((2,))],
        embed_late,
        embed_near,
    )
    recast_embed = call(
        functools.partial(place_embed_kernel, [2, 3]),
        "place_embed",
        embed_shape,
        [VMEM] * 3 + [HBM],
        HBM,
        [dma((2,))],
        embed_far,
        embed_last,
        placed_token,
        recast_embed,
        aliases={3: 0},
    )

    return (
        recast_up.reshape(-1, half_cols),
        recast_down.reshape(-1, width),
        recast_embed.reshape(-1, width),
        norm_cast,
        stored_up,
        velocity_up,
        stored_down[None],
        velocity_down[None],
        stored_rows[None],
        velocity_rows.T[None],
        stored_norm,
        velocity_norm,
    )


def solution(mesh):
    in_specs = (
        P("replica", None, "tensor"),
        P("replica", "tensor", None),
        P("replica", ("shard", "tensor"), None),
        P("replica", None, None),
        P(("replica", "shard", "tensor"), None),
        P(("replica", "shard", "tensor"), None),
        P("tensor", ("replica", "shard"), None),
        P("tensor", ("replica", "shard"), None),
        P(("shard", "tensor"), "replica", None),
        P(("shard", "tensor"), "replica", None),
        P(),
        P(),
        P(),
    )
    out_specs = (
        P(None, "tensor"),
        P("tensor", None),
        P(("shard", "tensor"), None),
        P(),
        P(("replica", "shard", "tensor"), None),
        P(("replica", "shard", "tensor"), None),
        P("tensor", ("replica", "shard"), None),
        P("tensor", ("replica", "shard"), None),
        P(("shard", "tensor"), "replica", None),
        P(("shard", "tensor"), "replica", None),
        P(),
        P(),
    )
    return jax.shard_map(body, mesh=mesh, in_specs=in_specs, out_specs=out_specs, check_vma=False)
```

```python
import functools

import jax
import jax.numpy as jnp
from jax import lax
from jax.experimental import pallas as pl
from jax.experimental.pallas import tpu as pltpu
from jax.sharding import PartitionSpec as P

F32 = jnp.float32
BF16 = jnp.bfloat16
HIGHEST = lax.Precision.HIGHEST
HBM = pl.BlockSpec(memory_space=pltpu.HBM)
ANY = pl.BlockSpec(memory_space=pl.ANY)
VMEM = pl.BlockSpec(memory_space=pltpu.VMEM)


def outer_step(master, moment, summed, groups):
    difference = master - summed / groups
    velocity = 0.5 * moment + difference
    return (master - 0.7 * (difference + 0.5 * velocity), velocity)


def call(kernel, name, out_shape, in_specs, out_specs, scratch, *operands, limit=24, aliases={}):
    size = sum(x.size * x.dtype.itemsize for x in jax.tree.leaves(out_shape))
    return pl.pallas_call(
        kernel,
        name=name,
        out_shape=out_shape,
        in_specs=in_specs,
        out_specs=out_specs,
        scratch_shapes=scratch,
        input_output_aliases=aliases,
        compiler_params=pltpu.CompilerParams(vmem_limit_bytes=limit * 2**20),
        cost_estimate=pl.CostEstimate(flops=0, bytes_accessed=3 * size, transcendentals=0),
    )(*operands)


OUTER = (0, 3)
INWARD = ((0, 1), (3, 2))
ACROSS = ((1, 2), (2, 1))
OUTWARD = ((1, 0), (2, 3))


def owners():
    pos = lax.axis_index("replica")
    low = pos < 2
    return pos, jnp.bitwise_xor(pos, 1), jnp.where(low, 2, 1), jnp.where(low, 3, 0)


def along(x, pairs):
    return lax.ppermute(x, "replica", pairs)


def swap(x, axis, bit):
    return lax.ppermute(x, axis, [(i, i ^ bit) for i in range(lax.axis_size(axis))])


def bits_down(size):
    bit = size // 2
    while bit:
        yield bit
        bit //= 2


def project_kernel(trained, basis, norm, own, *refs):
    *outs, token, projected = refs
    token[...] = jnp.zeros_like(token)
    rank, rows = basis.shape[0], own.shape[1]
    high = basis[...].astype(BF16)
    rest = basis[...] - high.astype(F32)
    middle = rest.astype(BF16)
    low = (rest - middle.astype(F32)).astype(BF16)
    split = jnp.concatenate([high, middle, low], axis=0)
    product = lax.dot_general(
        split, trained[...], (((1,), (1,)), ((), ())), preferred_element_type=F32
    )
    projected[...] = product[:rank] + (product[rank : 2 * rank] + product[2 * rank :])
    pos = lax.axis_index("replica")
    values = norm[...].astype(F32)
    per = norm.shape[1] // rows
    extra = outs[0].shape[0] - rank
    parts = [
        values[i // per : i // per + 1, (i % per) * rows : (i % per + 1) * rows]
        for i in range(norm.shape[0] * per)
    ]
    parts = jnp.concatenate((parts * extra)[:extra], axis=0).astype(BF16)
    own[...] = projected[:, pl.ds(pl.multiple_of(pos * rows, rows), rows)]
    for mask, out in enumerate(outs, 1):
        owner = jnp.bitwise_xor(pos, mask)
        block = projected[:, pl.ds(pl.multiple_of(owner * rows, rows), rows)]
        out[:rank, :] = block.astype(BF16)
        out[rank:, :] = parts


def embed_kernel(groups, n_came, *refs):
    refs = list(refs)
    own, base, master, moment, basis, norm, master_norm, moment_norm = refs[:8]
    came = refs[8 : 8 + n_came]
    stored, recast, velocity, norm_cast, norm_stored, norm_velocity = refs[-6:]
    rank, rows = own.shape
    total = own[...]
    for ref in came:
        total = total + ref[:rank, :].astype(F32)
    coefficient = base[...] - total / groups
    moved = 0.5 * moment[...] + coefficient
    velocity[...] = moved
    change = lax.dot_general(
        coefficient + 0.5 * moved,
        basis[...],
        (((0,), (0,)), ((), ())),
        precision=HIGHEST,
        preferred_element_type=F32,
    )
    new = master[...] - 0.7 * change
    stored[...] = new
    recast[...] = new.astype(BF16)
    per = norm.shape[1] // rows
    values = norm[...].astype(F32)
    tails = [ref[rank:, :].astype(F32) for ref in came]
    for i in range(norm.shape[0] * per):
        row, span = i // per, slice((i % per) * rows, (i % per + 1) * rows)
        summed = values[row : row + 1, span]
        for tail in tails:
            summed = summed + tail[i : i + 1, :]
        new_norm, moved_norm = outer_step(
            master_norm[row : row + 1, span], moment_norm[row : row + 1, span], summed, groups
        )
        norm_stored[row : row + 1, span] = new_norm
        norm_velocity[row : row + 1, span] = moved_norm
    norm_cast[...] = norm_stored[...].astype(BF16)


def pack_kernel(down, up, _, *refs):
    *outs, sems = refs
    shard = lax.axis_index("shard")
    rows, width = down.shape[2:]
    tall, cols = up.shape[2:]
    copies = []

    def bring(source, dest):
        copies.append(pltpu.make_async_copy(source, dest, sems.at[len(copies)]))
        copies[-1].start()

    for owner, out in reversed(list(zip(owners(), outs))):
        bring(down.at[owner, shard], out.at[pl.ds(0, rows)])
        for chunk in range(cols // width):
            bring(
                up.at[owner, shard, :, pl.ds(chunk * width, width)],
                out.at[pl.ds(rows + chunk * tall, tall)],
            )
    for copy in copies:
        copy.wait()


def add_kernel(block, came, *refs):
    refs[-1][...] = (block[...].astype(F32) + came[...].astype(F32)).astype(BF16)


def add(block, came, *after):
    return call(
        add_kernel,
        "add_block",
        jax.ShapeDtypeStruct(block.shape, BF16),
        [VMEM] * 2 + [ANY] * len(after),
        VMEM,
        [],
        block,
        came,
        *after,
    )


def pick_kernel(middle, end, out):
    pos = lax.axis_index("replica")
    outer = jnp.logical_or(pos == OUTER[0], pos == OUTER[1])

    @pl.when(outer)
    def _():
        out[...] = end[...]

    @pl.when(jnp.logical_not(outer))
    def _():
        out[...] = middle[...]


def pick(middle, end):
    shape = jax.ShapeDtypeStruct(end.shape, end.dtype)
    return call(pick_kernel, "pick", shape, [VMEM] * 2, VMEM, [], middle, end)


def update_kernel(groups, tensors, n_came, *refs):
    refs = list(refs)
    master_down, moment_down, master_up, moment_up = refs[:4]
    came, state_came = refs[4 : 4 + n_came], refs[4 + n_came : 3 + n_came + tensors]
    piece, stored_down, velocity_down, *sums = refs[3 + n_came + tensors : -3]
    summed, master, moment = refs[-3:]
    me = lax.axis_index("tensor")
    rows_down, width = master_down.shape
    rows_up = master_up.shape[0]
    tall, cols = summed.shape

    def at(index):
        return pl.ds(pl.multiple_of(index * rows_up, rows_up), rows_up)

    own_cols = pl.ds(pl.multiple_of(me * cols, cols), cols)
    master[at(me), :] = master_up[:, own_cols]
    moment[at(me), :] = moment_up[:, own_cols]
    for shift in range(1, tensors):
        source = lax.rem(me + tensors - shift, tensors)
        master[at(source), :] = state_came[shift - 1][0]
        moment[at(source), :] = state_came[shift - 1][1]

    def total(lo, hi):
        value = came[0][lo:hi, :].astype(F32)
        for ref in came[1:]:
            value = value + ref[lo:hi, :].astype(F32)
        return value

    stored, velocity = outer_step(
        master_down[...], moment_down[...], total(0, rows_down), groups
    )
    stored_down[...] = stored
    velocity_down[...] = velocity
    piece[:rows_down, :] = stored.astype(BF16)
    for chunk in range(cols // width):
        lo = rows_down + chunk * tall
        part = total(lo, lo + tall)
        span = slice(chunk * width, (chunk + 1) * width)
        summed[:, span] = part
        stored, _ = outer_step(master[:, span], moment[:, span], part, groups)
        piece[lo : lo + tall, :] = stored.astype(BF16)
    for shift in range(tensors):
        sums[shift][...] = summed[at(lax.rem(me + shift, tensors)), :]


def up_kernel(groups, tensors, master_up, moment_up, *refs):
    sums, (stored_up, velocity_up, token) = refs[:tensors], refs[tensors:]
    cols = sums[0].shape[1]
    me = lax.axis_index("tensor")
    for shift in range(tensors):
        source = lax.rem(me + tensors - shift, tensors)
        span = pl.ds(pl.multiple_of(source * cols, cols), cols)
        stored, velocity = outer_step(
            master_up[:, span], moment_up[:, span], sums[shift][...], groups
        )
        stored_up[:, span] = stored
        velocity_up[:, span] = velocity
    token[...] = jnp.zeros_like(token)


def state_kernel(tensors, master_up, moment_up, *outs):
    me = lax.axis_index("tensor")
    cols = outs[0].shape[2]
    for shift in range(1, tensors):
        target = lax.rem(me + shift, tensors)
        span = pl.ds(pl.multiple_of(target * cols, cols), cols)
        outs[shift - 1][0] = master_up[:, span]
        outs[shift - 1][1] = moment_up[:, span]


def gate_kernel(x, *refs):
    refs[-1][...] = x[...]


def gate(x, *after):
    return call(
        gate_kernel,
        "gate",
        jax.ShapeDtypeStruct(x.shape, x.dtype),
        [VMEM] + [ANY] * len(after),
        VMEM,
        [],
        x,
        *after,
    )


def place_kernel(slot, masks, *refs):
    pieces, (down, up, token, sems) = refs[: len(masks)], refs[-4:]
    token[...] = jnp.zeros_like(token)
    shard = lax.axis_index("shard")
    rows, width = down.shape[2:]
    tall, cols = up.shape[2:]
    copies = []

    def send(source, dest):
        copies.append(pltpu.make_async_copy(source, dest, sems.at[len(copies)]))
        copies[-1].start()

    owner = owners()[slot]
    for piece, mask in zip(pieces, masks):
        place = jnp.bitwise_xor(shard, mask)
        send(piece.at[pl.ds(0, rows)], down.at[owner, place])
        for chunk in range(cols // width):
            send(
                piece.at[pl.ds(rows + chunk * tall, tall)],
                up.at[owner, place, :, pl.ds(chunk * width, width)],
            )
    for copy in copies:
        copy.wait()


def place_embed_kernel(slots, *refs):
    pieces, (out, sems) = refs[: len(slots)], refs[-2:]
    copies = [
        pltpu.make_async_copy(piece, out.at[owners()[slot]], sems.at[i])
        for i, (piece, slot) in enumerate(zip(pieces, slots))
    ]
    for copy in copies:
        copy.start()
    for copy in copies:
        copy.wait()


def spread(piece):
    top = lax.axis_size("shard") // 2
    return spread_low({0: piece, top: swap(piece, "shard", top)})


def spread_low(pieces):
    for bit in bits_down(lax.axis_size("shard") // 2):
        pieces.update({mask ^ bit: swap(x, "shard", bit) for mask, x in list(pieces.items())})
    return pieces


def body(
    trained_up,
    trained_down,
    trained_embed,
    trained_norm,
    master_up,
    moment_up,
    master_down,
    moment_down,
    master_embed,
    moment_embed,
    master_norm,
    moment_norm,
    embed_basis,
):
    replicas = lax.axis_size("replica")
    shards = lax.axis_size("shard")
    tensors = lax.axis_size("tensor")
    width, rank = embed_basis.shape
    rows_up, half_cols = master_up.shape[0], trained_up.shape[2]
    rows_down, rows_embed = master_down.shape[1], master_embed.shape[1]
    tall = tensors * rows_up
    chunks = half_cols // width
    packed = jax.ShapeDtypeStruct((rows_down + chunks * tall, width), BF16)
    dma = pltpu.SemaphoreType.DMA

    basis_t = embed_basis.T
    rank_rows = jax.ShapeDtypeStruct((rank, rows_embed), F32)
    packet = jax.ShapeDtypeStruct((rank + 16, rows_embed), BF16)
    token_shape = jax.ShapeDtypeStruct((8, 128), F32)
    own_rows, *packets, projected = call(
        project_kernel,
        "project_rows",
        [rank_rows] + [packet] * (replicas - 1) + [token_shape],
        [VMEM] * 3,
        [VMEM] * (replicas + 1),
        [pltpu.VMEM((rank, replicas * rows_embed), F32)],
        pltpu.with_memory_space_constraint(trained_embed[0], pltpu.HBM),
        pltpu.with_memory_space_constraint(basis_t, pltpu.HBM),
        pltpu.with_memory_space_constraint(trained_norm[0], pltpu.HBM),
    )
    packets_came = [swap(x, "replica", mask) for mask, x in enumerate(packets, 1)]

    down = trained_down[0].reshape(replicas, shards, rows_down, width)
    up = trained_up[0].reshape(replicas, shards, tall, half_cols)
    own, near, middle, end = call(
        pack_kernel,
        "pack_blocks",
        [packed] * replicas,
        [HBM] * 2 + [VMEM],
        [VMEM] * replicas,
        [dma((replicas * (1 + chunks),))],
        pltpu.with_memory_space_constraint(down, pltpu.HBM),
        pltpu.with_memory_space_constraint(up, pltpu.HBM),
        projected,
    )
    end = gate(end, packets_came[0])
    from_end = [along(x, INWARD) for x in (end, middle, near)]

    state = jax.ShapeDtypeStruct((2, rows_up, half_cols), F32)
    states = call(
        functools.partial(state_kernel, tensors),
        "up_state",
        [state] * (tensors - 1),
        [VMEM] * 2,
        [VMEM] * (tensors - 1),
        [],
        master_up,
        moment_up,
    )
    states = [
        lax.ppermute(x, "tensor", [(i, (i + shift) % tensors) for i in range(tensors)])
        for shift, x in enumerate(states, 1)
    ]

    base = lax.dot_general(
        basis_t, master_embed[0], (((1,), (1,)), ((), ())), precision=HIGHEST
    )
    norm_state = jax.ShapeDtypeStruct(master_norm.shape, F32)
    embed_rows = jax.ShapeDtypeStruct((rows_embed, width), BF16)
    stored_rows, recast_rows, velocity_rows, norm_cast, stored_norm, velocity_norm = call(
        functools.partial(embed_kernel, replicas, replicas - 1),
        "embed_update",
        [
            jax.ShapeDtypeStruct((rows_embed, width), F32),
            embed_rows,
            rank_rows,
            jax.ShapeDtypeStruct(master_norm.shape, BF16),
            norm_state,
            norm_state,
        ],
        [VMEM] * (7 + replicas) + [ANY],
        [VMEM] * 6,
        [],
        own_rows,
        base,
        master_embed[0],
        moment_embed[0].T,
        basis_t,
        trained_norm[0],
        master_norm,
        moment_norm,
        *packets_came,
        end,
    )

    embed_out = along(recast_rows, OUTWARD)
    embed_middle = along(recast_rows, ACROSS)
    end_partial = along(add(end, from_end[0], embed_out, embed_middle), ACROSS)
    middle_partial = along(add(middle, from_end[1]), ACROSS)
    embed_middle_out = along(embed_middle, OUTWARD)
    to_end = along(add(near, end_partial, embed_middle_out), OUTWARD)
    came0 = [own, from_end[2], middle_partial, to_end]
    half_sum = jax.ShapeDtypeStruct((rows_up, half_cols), F32)
    down_state = jax.ShapeDtypeStruct((rows_down, width), F32)
    piece, stored_down, velocity_down, *sums = call(
        functools.partial(update_kernel, replicas, tensors, len(came0)),
        "update_rows",
        [packed, down_state, down_state] + [half_sum] * tensors,
        [VMEM] * (4 + len(came0) + len(states)),
        [VMEM] * (3 + tensors),
        [pltpu.VMEM((tall, half_cols), F32)] * 3,
        master_down[0],
        moment_down[0],
        master_up,
        moment_up,
        *came0,
        *states,
    )

    top = shards // 2
    near_piece = swap(piece, "replica", 1)
    middle_piece = along(piece, ACROSS)
    end_piece = along(near_piece, ACROSS)
    second = pick(middle_piece, along(middle_piece, OUTWARD))
    third = pick(end_piece, along(end_piece, OUTWARD))
    groups = [spread(x) for x in (piece, near_piece, second)]

    embed_in = along(gate(recast_rows, near_piece), INWARD)
    embed_end = along(embed_in, ACROSS)
    embed_last = along(embed_end, OUTWARD)

    sums = [sums[0]] + [
        lax.ppermute(
            gate(x, second), "tensor", [(i, (i + shift) % tensors) for i in range(tensors)]
        )
        for shift, x in enumerate(sums[1:], 1)
    ]
    stored_up, velocity_up, token = call(
        functools.partial(up_kernel, replicas, tensors),
        "update_up",
        [jax.ShapeDtypeStruct(master_up.shape, F32)] * 2 + [token_shape],
        [VMEM] * (2 + tensors),
        [VMEM] * 3,
        [],
        master_up,
        moment_up,
        *sums,
    )

    embed_shape = jax.ShapeDtypeStruct((replicas, rows_embed, width), BF16)
    recast_embed = call(
        functools.partial(place_embed_kernel, [0, 1, 2]),
        "place_embed",
        embed_shape,
        [VMEM] * 4,
        HBM,
        [dma((3,))],
        recast_rows,
        pick(embed_in, embed_out),
        pick(embed_middle, embed_middle_out),
        token,
    )

    shapes = [jax.ShapeDtypeStruct(down.shape, BF16), jax.ShapeDtypeStruct(up.shape, BF16)]

    def place(slot, group, placed, *after):
        count = len(group) + len(after)
        return call(
            functools.partial(place_kernel, slot, list(group)),
            "place_rows",
            shapes + [token_shape],
            [VMEM] * count + [HBM] * len(placed),
            [HBM] * 2 + [VMEM],
            [dma((len(group) * (1 + chunks),))],
            *group.values(),
            *after,
            *placed,
            aliases={count: 0, count + 1: 1} if placed else {},
        )

    placed = []
    for slot, group in enumerate(groups):
        *placed, token = place(slot, group, placed, token)
    far = gate(swap(third, "shard", top), token)
    *placed, token = place(3, spread_low({0: third}), placed)
    recast_down, recast_up, token = place(3, spread_low({top: far}), placed)
    recast_embed = call(
        functools.partial(place_embed_kernel, [3]),
        "place_embed",
        embed_shape,
        [VMEM] * 2 + [HBM],
        HBM,
        [dma((1,))],
        pick(embed_end, embed_last),
        token,
        recast_embed,
        aliases={2: 0},
    )

    return (
        recast_up.reshape(-1, half_cols),
        recast_down.reshape(-1, width),
        recast_embed.reshape(-1, width),
        norm_cast,
        stored_up,
        velocity_up,
        stored_down[None],
        velocity_down[None],
        stored_rows[None],
        velocity_rows.T[None],
        stored_norm,
        velocity_norm,
    )


def solution(mesh):
    in_specs = (
        P("replica", None, "tensor"),
        P("replica", "tensor", None),
        P("replica", ("shard", "tensor"), None),
        P("replica", None, None),
        P(("replica", "shard", "tensor"), None),
        P(("replica", "shard", "tensor"), None),
        P("tensor", ("replica", "shard"), None),
        P("tensor", ("replica", "shard"), None),
        P(("shard", "tensor"), "replica", None),
        P(("shard", "tensor"), "replica", None),
        P(),
        P(),
        P(),
    )
    out_specs = (
        P(None, "tensor"),
        P("tensor", None),
        P(("shard", "tensor"), None),
        P(),
        P(("replica", "shard", "tensor"), None),
        P(("replica", "shard", "tensor"), None),
        P("tensor", ("replica", "shard"), None),
        P("tensor", ("replica", "shard"), None),
        P(("shard", "tensor"), "replica", None),
        P(("shard", "tensor"), "replica", None),
        P(),
        P(),
    )
    return jax.shard_map(body, mesh=mesh, in_specs=in_specs, out_specs=out_specs, check_vma=False)
```

```python
import functools

import jax
import jax.numpy as jnp
from jax import lax
from jax.experimental import pallas as pl
from jax.experimental.pallas import tpu as pltpu
from jax.sharding import PartitionSpec as P

F32 = jnp.float32
BF16 = jnp.bfloat16
HIGHEST = lax.Precision.HIGHEST
HBM = pl.BlockSpec(memory_space=pltpu.HBM)
ANY = pl.BlockSpec(memory_space=pl.ANY)
VMEM = pl.BlockSpec(memory_space=pltpu.VMEM)


def outer_step(master, moment, summed, groups):
    difference = master - summed / groups
    velocity = 0.5 * moment + difference
    return (master - 0.7 * (difference + 0.5 * velocity), velocity)


def call(kernel, name, out_shape, in_specs, out_specs, scratch, *operands, limit=24, aliases={}):
    size = sum(x.size * x.dtype.itemsize for x in jax.tree.leaves(out_shape))
    return pl.pallas_call(
        kernel,
        name=name,
        out_shape=out_shape,
        in_specs=in_specs,
        out_specs=out_specs,
        scratch_shapes=scratch,
        input_output_aliases=aliases,
        compiler_params=pltpu.CompilerParams(vmem_limit_bytes=limit * 2**20),
        cost_estimate=pl.CostEstimate(flops=0, bytes_accessed=3 * size, transcendentals=0),
    )(*operands)


OUTER = (0, 3)
INWARD = ((0, 1), (3, 2))
ACROSS = ((1, 2), (2, 1))
OUTWARD = ((1, 0), (2, 3))


def owners():
    pos = lax.axis_index("replica")
    low = pos < 2
    return pos, jnp.bitwise_xor(pos, 1), jnp.where(low, 2, 1), jnp.where(low, 3, 0)


def along(x, pairs):
    return lax.ppermute(x, "replica", pairs)


def swap(x, axis, bit):
    return lax.ppermute(x, axis, [(i, i ^ bit) for i in range(lax.axis_size(axis))])


def bits_down(size):
    bit = size // 2
    while bit:
        yield bit
        bit //= 2


def project_kernel(trained, basis, norm, own, *refs):
    *outs, projected = refs
    rank, rows = basis.shape[0], own.shape[1]
    high = basis[...].astype(BF16)
    rest = basis[...] - high.astype(F32)
    middle = rest.astype(BF16)
    low = (rest - middle.astype(F32)).astype(BF16)
    split = jnp.concatenate([high, middle, low], axis=0)
    product = lax.dot_general(
        split, trained[...], (((1,), (1,)), ((), ())), preferred_element_type=F32
    )
    projected[...] = product[:rank] + (product[rank : 2 * rank] + product[2 * rank :])
    pos = lax.axis_index("replica")
    values = norm[...].astype(F32)
    per = norm.shape[1] // rows
    extra = outs[0].shape[0] - rank
    parts = [
        values[i // per : i // per + 1, (i % per) * rows : (i % per + 1) * rows]
        for i in range(norm.shape[0] * per)
    ]
    parts = jnp.concatenate((parts * extra)[:extra], axis=0).astype(BF16)
    own[...] = projected[:, pl.ds(pl.multiple_of(pos * rows, rows), rows)]
    for mask, out in enumerate(outs, 1):
        owner = jnp.bitwise_xor(pos, mask)
        block = projected[:, pl.ds(pl.multiple_of(owner * rows, rows), rows)]
        out[:rank, :] = block.astype(BF16)
        out[rank:, :] = parts


def embed_kernel(groups, n_came, *refs):
    refs = list(refs)
    own, master, moment, basis, norm, master_norm, moment_norm = refs[:7]
    came = refs[7 : 7 + n_came]
    stored, recast, velocity, norm_cast, norm_stored, norm_velocity = refs[-6:]
    rank, rows = own.shape
    total = own[...]
    for ref in came:
        total = total + ref[:rank, :].astype(F32)
    base = lax.dot_general(
        basis[...],
        master[...],
        (((1,), (1,)), ((), ())),
        precision=HIGHEST,
        preferred_element_type=F32,
    )
    coefficient = base - total / groups
    moved = 0.5 * moment[...] + coefficient
    velocity[...] = moved
    change = lax.dot_general(
        coefficient + 0.5 * moved,
        basis[...],
        (((0,), (0,)), ((), ())),
        precision=HIGHEST,
        preferred_element_type=F32,
    )
    new = master[...] - 0.7 * change
    stored[...] = new
    recast[...] = new.astype(BF16)
    per = norm.shape[1] // rows
    values = norm[...].astype(F32)
    tails = [ref[rank:, :].astype(F32) for ref in came]
    for i in range(norm.shape[0] * per):
        row, span = i // per, slice((i % per) * rows, (i % per + 1) * rows)
        summed = values[row : row + 1, span]
        for tail in tails:
            summed = summed + tail[i : i + 1, :]
        new_norm, moved_norm = outer_step(
            master_norm[row : row + 1, span], moment_norm[row : row + 1, span], summed, groups
        )
        norm_stored[row : row + 1, span] = new_norm
        norm_velocity[row : row + 1, span] = moved_norm
    norm_cast[...] = norm_stored[...].astype(BF16)


def pack_kernel(down, up, *refs):
    *outs, sems = refs
    shard = lax.axis_index("shard")
    rows, width = down.shape[2:]
    tall, cols = up.shape[2:]
    copies = []

    def bring(source, dest):
        copies.append(pltpu.make_async_copy(source, dest, sems.at[len(copies)]))
        copies[-1].start()

    for owner, out in reversed(list(zip(owners(), outs))):
        bring(down.at[owner, shard], out.at[pl.ds(0, rows)])
        for chunk in range(cols // width):
            bring(
                up.at[owner, shard, :, pl.ds(chunk * width, width)],
                out.at[pl.ds(rows + chunk * tall, tall)],
            )
    for copy in copies:
        copy.wait()


def add_kernel(block, came, *refs):
    refs[-1][...] = (block[...].astype(F32) + came[...].astype(F32)).astype(BF16)


def add(block, came, *after):
    return call(
        add_kernel,
        "add_block",
        jax.ShapeDtypeStruct(block.shape, BF16),
        [VMEM] * 2 + [ANY] * len(after),
        VMEM,
        [],
        block,
        came,
        *after,
    )


def pick_kernel(middle, end, *refs):
    out = refs[-1]
    pos = lax.axis_index("replica")
    outer = jnp.logical_or(pos == OUTER[0], pos == OUTER[1])

    @pl.when(outer)
    def _():
        out[...] = end[...]

    @pl.when(jnp.logical_not(outer))
    def _():
        out[...] = middle[...]


def pick(middle, end, *after):
    specs = [VMEM] * 2 + [ANY] * len(after)
    shape = jax.ShapeDtypeStruct(end.shape, end.dtype)
    return call(pick_kernel, "pick", shape, specs, VMEM, [], middle, end, *after)


def update_kernel(groups, tensors, n_came, *refs):
    refs = list(refs)
    master_down, moment_down, master_up, moment_up = refs[:4]
    came, state_came = refs[4 : 4 + n_came], refs[4 + n_came : 3 + n_came + tensors]
    piece, stored_down, velocity_down, *sums = refs[3 + n_came + tensors : -3]
    summed, master, moment = refs[-3:]
    me = lax.axis_index("tensor")
    rows_down, width = master_down.shape
    rows_up = master_up.shape[0]
    tall, cols = summed.shape

    def at(index):
        return pl.ds(pl.multiple_of(index * rows_up, rows_up), rows_up)

    own_cols = pl.ds(pl.multiple_of(me * cols, cols), cols)
    master[at(me), :] = master_up[:, own_cols]
    moment[at(me), :] = moment_up[:, own_cols]
    for shift in range(1, tensors):
        source = lax.rem(me + tensors - shift, tensors)
        master[at(source), :] = state_came[shift - 1][0]
        moment[at(source), :] = state_came[shift - 1][1]

    def total(lo, hi):
        value = came[0][lo:hi, :].astype(F32)
        for ref in came[1:]:
            value = value + ref[lo:hi, :].astype(F32)
        return value

    stored, velocity = outer_step(
        master_down[...], moment_down[...], total(0, rows_down), groups
    )
    stored_down[...] = stored
    velocity_down[...] = velocity
    piece[:rows_down, :] = stored.astype(BF16)
    for chunk in range(cols // width):
        lo = rows_down + chunk * tall
        part = total(lo, lo + tall)
        span = slice(chunk * width, (chunk + 1) * width)
        summed[:, span] = part
        stored, _ = outer_step(master[:, span], moment[:, span], part, groups)
        piece[lo : lo + tall, :] = stored.astype(BF16)
    for shift in range(tensors):
        sums[shift][...] = summed[at(lax.rem(me + shift, tensors)), :]


def up_kernel(groups, tensors, master_up, moment_up, *refs):
    sums, (stored_up, velocity_up, token) = refs[:tensors], refs[tensors:]
    cols = sums[0].shape[1]
    me = lax.axis_index("tensor")
    for shift in range(tensors):
        source = lax.rem(me + tensors - shift, tensors)
        span = pl.ds(pl.multiple_of(source * cols, cols), cols)
        stored, velocity = outer_step(
            master_up[:, span], moment_up[:, span], sums[shift][...], groups
        )
        stored_up[:, span] = stored
        velocity_up[:, span] = velocity
    token[...] = jnp.zeros_like(token)


def state_kernel(tensors, master_up, moment_up, *outs):
    me = lax.axis_index("tensor")
    cols = outs[0].shape[2]
    for shift in range(1, tensors):
        target = lax.rem(me + shift, tensors)
        span = pl.ds(pl.multiple_of(target * cols, cols), cols)
        outs[shift - 1][0] = master_up[:, span]
        outs[shift - 1][1] = moment_up[:, span]


def gate_kernel(x, *refs):
    refs[-1][...] = x[...]


def gate(x, *after):
    return call(
        gate_kernel,
        "gate",
        jax.ShapeDtypeStruct(x.shape, x.dtype),
        [VMEM] + [ANY] * len(after),
        VMEM,
        [],
        x,
        *after,
    )


def stack_kernel(count, *refs):
    for i in range(count):
        refs[-1][i] = refs[i][...]


def bundle(pieces, *after):
    return call(
        functools.partial(stack_kernel, len(pieces)),
        "bundle",
        jax.ShapeDtypeStruct((len(pieces),) + pieces[0].shape, BF16),
        [VMEM] * len(pieces) + [ANY] * len(after),
        VMEM,
        [],
        *pieces,
        *after,
    )


def place_kernel(keys, *refs):
    bundles, (down, up, token, sems) = refs[: len(keys)], refs[-4:]
    token[...] = jnp.zeros_like(token)
    shard = lax.axis_index("shard")
    rows, width = down.shape[2:]
    tall, cols = up.shape[2:]
    copies = []

    def send(source, dest):
        copies.append(pltpu.make_async_copy(source, dest, sems.at[len(copies)]))
        copies[-1].start()

    for pieces, (low, slots) in zip(bundles, keys):
        for i, (slot, mask) in enumerate(slots):
            owner, place = owners()[slot], jnp.bitwise_xor(shard, mask ^ low)
            send(pieces.at[i, pl.ds(0, rows)], down.at[owner, place])
            for chunk in range(cols // width):
                send(
                    pieces.at[i, pl.ds(rows + chunk * tall, tall)],
                    up.at[owner, place, :, pl.ds(chunk * width, width)],
                )
    for copy in copies:
        copy.wait()


def place_embed_kernel(slots, *refs):
    pieces, (out, sems) = refs[: len(slots)], refs[-2:]
    copies = [
        pltpu.make_async_copy(piece, out.at[owners()[slot]], sems.at[i])
        for i, (piece, slot) in enumerate(zip(pieces, slots))
    ]
    for copy in copies:
        copy.start()
    for copy in copies:
        copy.wait()


def spread_low(x):
    found = {0: x}
    for bit in bits_down(lax.axis_size("shard") // 2):
        found.update({mask ^ bit: swap(y, "shard", bit) for mask, y in list(found.items())})
    return found


def body(
    trained_up,
    trained_down,
    trained_embed,
    trained_norm,
    master_up,
    moment_up,
    master_down,
    moment_down,
    master_embed,
    moment_embed,
    master_norm,
    moment_norm,
    embed_basis,
):
    replicas = lax.axis_size("replica")
    shards = lax.axis_size("shard")
    tensors = lax.axis_size("tensor")
    width, rank = embed_basis.shape
    rows_up, half_cols = master_up.shape[0], trained_up.shape[2]
    rows_down, rows_embed = master_down.shape[1], master_embed.shape[1]
    tall = tensors * rows_up
    chunks = half_cols // width
    packed = jax.ShapeDtypeStruct((rows_down + chunks * tall, width), BF16)
    dma = pltpu.SemaphoreType.DMA

    basis_t = embed_basis.T
    rank_rows = jax.ShapeDtypeStruct((rank, rows_embed), F32)
    packet = jax.ShapeDtypeStruct((rank + 16, rows_embed), BF16)
    token_shape = jax.ShapeDtypeStruct((8, 128), F32)
    own_rows, *packets = call(
        project_kernel,
        "project_rows",
        [rank_rows] + [packet] * (replicas - 1),
        [VMEM] * 3,
        [VMEM] * replicas,
        [pltpu.VMEM((rank, replicas * rows_embed), F32)],
        pltpu.with_memory_space_constraint(trained_embed[0], pltpu.HBM),
        pltpu.with_memory_space_constraint(basis_t, pltpu.HBM),
        pltpu.with_memory_space_constraint(trained_norm[0], pltpu.HBM),
    )
    down = trained_down[0].reshape(replicas, shards, rows_down, width)
    up = trained_up[0].reshape(replicas, shards, tall, half_cols)
    own, near, middle, end = call(
        pack_kernel,
        "pack_blocks",
        [packed] * replicas,
        [HBM] * 2,
        [VMEM] * replicas,
        [dma((replicas * (1 + chunks),))],
        pltpu.with_memory_space_constraint(down, pltpu.HBM),
        pltpu.with_memory_space_constraint(up, pltpu.HBM),
    )
    from_end = [along(x, INWARD) for x in (end, middle, near)]
    end_sum = add(end, from_end[0])
    packets[1] = gate(packets[1], end_sum)
    packets_came = [swap(x, "replica", mask) for mask, x in enumerate(packets, 1)]

    state = jax.ShapeDtypeStruct((2, rows_up, half_cols), F32)
    states = call(
        functools.partial(state_kernel, tensors),
        "up_state",
        [state] * (tensors - 1),
        [VMEM] * 2,
        [VMEM] * (tensors - 1),
        [],
        master_up,
        moment_up,
    )
    states = [
        lax.ppermute(x, "tensor", [(i, (i + shift) % tensors) for i in range(tensors)])
        for shift, x in enumerate(states, 1)
    ]

    norm_state = jax.ShapeDtypeStruct(master_norm.shape, F32)
    embed_rows = jax.ShapeDtypeStruct((rows_embed, width), BF16)
    stored_rows, recast_rows, velocity_rows, norm_cast, stored_norm, velocity_norm = call(
        functools.partial(embed_kernel, replicas, replicas - 1),
        "embed_update",
        [
            jax.ShapeDtypeStruct((rows_embed, width), F32),
            embed_rows,
            rank_rows,
            jax.ShapeDtypeStruct(master_norm.shape, BF16),
            norm_state,
            norm_state,
        ],
        [VMEM] * (6 + replicas),
        [VMEM] * 6,
        [],
        own_rows,
        master_embed[0],
        moment_embed[0].T,
        basis_t,
        trained_norm[0],
        master_norm,
        moment_norm,
        *packets_came,
    )

    embed_out = along(recast_rows, OUTWARD)
    end_partial = along(end_sum, ACROSS)
    middle_partial = along(add(middle, from_end[1]), ACROSS)
    to_end = along(add(near, end_partial, embed_out), OUTWARD)
    came0 = [own, from_end[2], middle_partial, to_end]
    half_sum = jax.ShapeDtypeStruct((rows_up, half_cols), F32)
    down_state = jax.ShapeDtypeStruct((rows_down, width), F32)
    piece, stored_down, velocity_down, *sums = call(
        functools.partial(update_kernel, replicas, tensors, len(came0)),
        "update_rows",
        [packed, down_state, down_state] + [half_sum] * tensors,
        [VMEM] * (4 + len(came0) + len(states)),
        [VMEM] * (3 + tensors),
        [pltpu.VMEM((tall, half_cols), F32)] * 3,
        master_down[0],
        moment_down[0],
        master_up,
        moment_up,
        *came0,
        *states,
    )

    top = shards // 2
    far_piece = swap(piece, "shard", top)
    middle_piece = along(piece, ACROSS)
    near_piece = gate(swap(piece, "replica", 1), far_piece, middle_piece)
    far_near = swap(near_piece, "shard", top)
    end_piece = along(near_piece, ACROSS)
    embed_late = gate(recast_rows, near_piece)
    embed_in = along(embed_late, INWARD)
    embed_middle = along(embed_late, ACROSS)
    sums = [sums[0]] + [
        lax.ppermute(
            gate(x, near_piece), "tensor", [(i, (i + shift) % tensors) for i in range(tensors)]
        )
        for shift, x in enumerate(sums[1:], 1)
    ]
    second = pick(middle_piece, along(middle_piece, OUTWARD), embed_in, far_near)
    far_second = swap(second, "shard", top)
    third = pick(end_piece, along(end_piece, OUTWARD), embed_middle, far_second, *sums[1:])
    far_third = swap(third, "shard", top)
    bundles = [
        (
            [(0, 0), (0, top), (1, 0), (1, top)],
            spread_low(bundle([piece, far_piece, near_piece, far_near], third)),
        ),
        (
            [(2, 0), (2, top), (3, 0)],
            spread_low(bundle([second, far_second, third])),
        ),
    ]

    embed_middle_out = along(embed_middle, OUTWARD)
    embed_end = along(gate(embed_in, third), ACROSS)
    embed_last = along(embed_end, OUTWARD)

    stored_up, velocity_up, token = call(
        functools.partial(up_kernel, replicas, tensors),
        "update_up",
        [jax.ShapeDtypeStruct(master_up.shape, F32)] * 2 + [token_shape],
        [VMEM] * (2 + tensors),
        [VMEM] * 3,
        [],
        master_up,
        moment_up,
        *sums,
    )

    embed_shape = jax.ShapeDtypeStruct((replicas, rows_embed, width), BF16)
    recast_embed = call(
        functools.partial(place_embed_kernel, [0, 1, 2]),
        "place_embed",
        embed_shape,
        [VMEM] * 4,
        HBM,
        [dma((3,))],
        recast_rows,
        pick(embed_in, embed_out),
        pick(embed_middle, embed_middle_out),
        token,
    )

    shapes = [jax.ShapeDtypeStruct(down.shape, BF16), jax.ShapeDtypeStruct(up.shape, BF16)]

    def place(slots, arrays, placed, *after):
        keys = [(low, slots) for low in arrays]
        count = len(keys) + len(after)
        return call(
            functools.partial(place_kernel, keys),
            "place_rows",
            shapes + [token_shape],
            [VMEM] * count + [HBM] * len(placed),
            [HBM] * 2 + [VMEM],
            [dma((len(keys) * len(slots) * (1 + chunks),))],
            *arrays.values(),
            *after,
            *placed,
            aliases={count: 0, count + 1: 1} if placed else {},
        )

    placed = []
    for slots, arrays in bundles:
        *placed, token = place(slots, arrays, placed, token)
    last = spread_low(bundle([far_third], token))
    recast_down, recast_up, token = place([(3, top)], last, placed)
    recast_embed = call(
        functools.partial(place_embed_kernel, [3]),
        "place_embed",
        embed_shape,
        [VMEM] * 2 + [HBM],
        HBM,
        [dma((1,))],
        pick(embed_end, embed_last),
        token,
        recast_embed,
        aliases={2: 0},
    )

    return (
        recast_up.reshape(-1, half_cols),
        recast_down.reshape(-1, width),
        recast_embed.reshape(-1, width),
        norm_cast,
        stored_up,
        velocity_up,
        stored_down[None],
        velocity_down[None],
        stored_rows[None],
        velocity_rows.T[None],
        stored_norm,
        velocity_norm,
    )


def solution(mesh):
    in_specs = (
        P("replica", None, "tensor"),
        P("replica", "tensor", None),
        P("replica", ("shard", "tensor"), None),
        P("replica", None, None),
        P(("replica", "shard", "tensor"), None),
        P(("replica", "shard", "tensor"), None),
        P("tensor", ("replica", "shard"), None),
        P("tensor", ("replica", "shard"), None),
        P(("shard", "tensor"), "replica", None),
        P(("shard", "tensor"), "replica", None),
        P(),
        P(),
        P(),
    )
    out_specs = (
        P(None, "tensor"),
        P("tensor", None),
        P(("shard", "tensor"), None),
        P(),
        P(("replica", "shard", "tensor"), None),
        P(("replica", "shard", "tensor"), None),
        P("tensor", ("replica", "shard"), None),
        P("tensor", ("replica", "shard"), None),
        P(("shard", "tensor"), "replica", None),
        P(("shard", "tensor"), "replica", None),
        P(),
        P(),
    )
    return jax.shard_map(body, mesh=mesh, in_specs=in_specs, out_specs=out_specs, check_vma=False)
```

```python
import functools

import jax
import jax.numpy as jnp
from jax import lax
from jax.experimental import pallas as pl
from jax.experimental.pallas import tpu as pltpu
from jax.sharding import PartitionSpec as P

F32 = jnp.float32
BF16 = jnp.bfloat16
HIGHEST = lax.Precision.HIGHEST
HBM = pl.BlockSpec(memory_space=pltpu.HBM)
ANY = pl.BlockSpec(memory_space=pl.ANY)
VMEM = pl.BlockSpec(memory_space=pltpu.VMEM)


def outer_step(master, moment, summed, groups):
    difference = master - summed / groups
    velocity = 0.5 * moment + difference
    return (master - 0.7 * (difference + 0.5 * velocity), velocity)


def call(kernel, name, out_shape, in_specs, out_specs, scratch, *operands, limit=24, aliases={}):
    size = sum(x.size * x.dtype.itemsize for x in jax.tree.leaves(out_shape))
    return pl.pallas_call(
        kernel,
        name=name,
        out_shape=out_shape,
        in_specs=in_specs,
        out_specs=out_specs,
        scratch_shapes=scratch,
        input_output_aliases=aliases,
        compiler_params=pltpu.CompilerParams(vmem_limit_bytes=limit * 2**20),
        cost_estimate=pl.CostEstimate(flops=0, bytes_accessed=3 * size, transcendentals=0),
    )(*operands)


OUTER = (0, 3)
INWARD = ((0, 1), (3, 2))
ACROSS = ((1, 2), (2, 1))
OUTWARD = ((1, 0), (2, 3))


def owners():
    pos = lax.axis_index("replica")
    low = pos < 2
    return pos, jnp.bitwise_xor(pos, 1), jnp.where(low, 2, 1), jnp.where(low, 3, 0)


def along(x, pairs):
    return lax.ppermute(x, "replica", pairs)


def swap(x, axis, bit):
    return lax.ppermute(x, axis, [(i, i ^ bit) for i in range(lax.axis_size(axis))])


def bits_down(size):
    bit = size // 2
    while bit:
        yield bit
        bit //= 2


def project_kernel(trained, basis, norm, own, *refs):
    *outs, projected = refs
    rank, rows = basis.shape[0], own.shape[1]
    high = basis[...].astype(BF16)
    rest = basis[...] - high.astype(F32)
    middle = rest.astype(BF16)
    low = (rest - middle.astype(F32)).astype(BF16)
    split = jnp.concatenate([high, middle, low], axis=0)
    product = lax.dot_general(
        split, trained[...], (((1,), (1,)), ((), ())), preferred_element_type=F32
    )
    projected[...] = product[:rank] + (product[rank : 2 * rank] + product[2 * rank :])
    pos = lax.axis_index("replica")
    values = norm[...].astype(F32)
    per = norm.shape[1] // rows
    extra = outs[0].shape[0] - rank
    parts = [
        values[i // per : i // per + 1, (i % per) * rows : (i % per + 1) * rows]
        for i in range(norm.shape[0] * per)
    ]
    parts = jnp.concatenate((parts * extra)[:extra], axis=0).astype(BF16)
    own[...] = projected[:, pl.ds(pl.multiple_of(pos * rows, rows), rows)]
    for mask, out in enumerate(outs, 1):
        owner = jnp.bitwise_xor(pos, mask)
        block = projected[:, pl.ds(pl.multiple_of(owner * rows, rows), rows)]
        out[:rank, :] = block.astype(BF16)
        out[rank:, :] = parts


def embed_kernel(groups, n_came, *refs):
    refs = list(refs)
    own, base, master, moment, basis, norm, master_norm, moment_norm = refs[:8]
    came = refs[8 : 8 + n_came]
    stored, recast, velocity, norm_cast, norm_stored, norm_velocity = refs[-6:]
    rank, rows = own.shape
    total = own[...]
    for ref in came:
        total = total + ref[:rank, :].astype(F32)
    coefficient = base[...] - total / groups
    moved = 0.5 * moment[...] + coefficient
    velocity[...] = moved
    change = lax.dot_general(
        coefficient + 0.5 * moved,
        basis[...],
        (((0,), (0,)), ((), ())),
        precision=HIGHEST,
        preferred_element_type=F32,
    )
    new = master[...] - 0.7 * change
    stored[...] = new
    recast[...] = new.astype(BF16)
    per = norm.shape[1] // rows
    values = norm[...].astype(F32)
    tails = [ref[rank:, :].astype(F32) for ref in came]
    for i in range(norm.shape[0] * per):
        row, span = i // per, slice((i % per) * rows, (i % per + 1) * rows)
        summed = values[row : row + 1, span]
        for tail in tails:
            summed = summed + tail[i : i + 1, :]
        new_norm, moved_norm = outer_step(
            master_norm[row : row + 1, span], moment_norm[row : row + 1, span], summed, groups
        )
        norm_stored[row : row + 1, span] = new_norm
        norm_velocity[row : row + 1, span] = moved_norm
    norm_cast[...] = norm_stored[...].astype(BF16)


def pack_kernel(down, up, *refs):
    *outs, sems = refs
    shard = lax.axis_index("shard")
    rows, width = down.shape[2:]
    tall, cols = up.shape[2:]
    copies = []

    def bring(source, dest):
        copies.append(pltpu.make_async_copy(source, dest, sems.at[len(copies)]))
        copies[-1].start()

    for owner, out in reversed(list(zip(owners(), outs))):
        bring(down.at[owner, shard], out.at[pl.ds(0, rows)])
        for chunk in range(cols // width):
            bring(
                up.at[owner, shard, :, pl.ds(chunk * width, width)],
                out.at[pl.ds(rows + chunk * tall, tall)],
            )
    for copy in copies:
        copy.wait()


def add_kernel(block, came, *refs):
    refs[-1][...] = (block[...].astype(F32) + came[...].astype(F32)).astype(BF16)


def add(block, came, *after):
    return call(
        add_kernel,
        "add_block",
        jax.ShapeDtypeStruct(block.shape, BF16),
        [VMEM] * 2 + [ANY] * len(after),
        VMEM,
        [],
        block,
        came,
        *after,
    )


def pick_kernel(middle, end, *refs):
    out = refs[-1]
    pos = lax.axis_index("replica")
    outer = jnp.logical_or(pos == OUTER[0], pos == OUTER[1])

    @pl.when(outer)
    def _():
        out[...] = end[...]

    @pl.when(jnp.logical_not(outer))
    def _():
        out[...] = middle[...]


def pick(middle, end, *after):
    specs = [VMEM] * 2 + [ANY] * len(after)
    shape = jax.ShapeDtypeStruct(end.shape, end.dtype)
    return call(pick_kernel, "pick", shape, specs, VMEM, [], middle, end, *after)


def update_kernel(groups, tensors, n_came, *refs):
    refs = list(refs)
    master_down, moment_down, master_up, moment_up = refs[:4]
    came, state_came = refs[4 : 4 + n_came], refs[4 + n_came : 3 + n_came + tensors]
    piece, stored_down, velocity_down, *sums = refs[3 + n_came + tensors : -3]
    summed, master, moment = refs[-3:]
    me = lax.axis_index("tensor")
    rows_down, width = master_down.shape
    rows_up = master_up.shape[0]
    tall, cols = summed.shape

    def at(index):
        return pl.ds(pl.multiple_of(index * rows_up, rows_up), rows_up)

    own_cols = pl.ds(pl.multiple_of(me * cols, cols), cols)
    master[at(me), :] = master_up[:, own_cols]
    moment[at(me), :] = moment_up[:, own_cols]
    for shift in range(1, tensors):
        source = lax.rem(me + tensors - shift, tensors)
        master[at(source), :] = state_came[shift - 1][0]
        moment[at(source), :] = state_came[shift - 1][1]

    def total(lo, hi):
        value = came[0][lo:hi, :].astype(F32)
        for ref in came[1:]:
            value = value + ref[lo:hi, :].astype(F32)
        return value

    stored, velocity = outer_step(
        master_down[...], moment_down[...], total(0, rows_down), groups
    )
    stored_down[...] = stored
    velocity_down[...] = velocity
    piece[:rows_down, :] = stored.astype(BF16)
    for chunk in range(cols // width):
        lo = rows_down + chunk * tall
        part = total(lo, lo + tall)
        span = slice(chunk * width, (chunk + 1) * width)
        summed[:, span] = part
        stored, _ = outer_step(master[:, span], moment[:, span], part, groups)
        piece[lo : lo + tall, :] = stored.astype(BF16)
    for shift in range(tensors):
        sums[shift][...] = summed[at(lax.rem(me + shift, tensors)), :]


def up_kernel(groups, tensors, master_up, moment_up, *refs):
    sums, (stored_up, velocity_up, token) = refs[:tensors], refs[tensors:]
    cols = sums[0].shape[1]
    me = lax.axis_index("tensor")
    for shift in range(tensors):
        source = lax.rem(me + tensors - shift, tensors)
        span = pl.ds(pl.multiple_of(source * cols, cols), cols)
        stored, velocity = outer_step(
            master_up[:, span], moment_up[:, span], sums[shift][...], groups
        )
        stored_up[:, span] = stored
        velocity_up[:, span] = velocity
    token[...] = jnp.zeros_like(token)


def state_kernel(tensors, master_up, moment_up, *outs):
    me = lax.axis_index("tensor")
    cols = outs[0].shape[2]
    for shift in range(1, tensors):
        target = lax.rem(me + shift, tensors)
        span = pl.ds(pl.multiple_of(target * cols, cols), cols)
        outs[shift - 1][0] = master_up[:, span]
        outs[shift - 1][1] = moment_up[:, span]


def gate_kernel(x, *refs):
    refs[-1][...] = x[...]


def gate(x, *after):
    return call(
        gate_kernel,
        "gate",
        jax.ShapeDtypeStruct(x.shape, x.dtype),
        [VMEM] + [ANY] * len(after),
        VMEM,
        [],
        x,
        *after,
    )


def stack_kernel(count, *refs):
    for i in range(count):
        refs[-1][i] = refs[i][...]


def bundle(pieces, *after):
    return call(
        functools.partial(stack_kernel, len(pieces)),
        "bundle",
        jax.ShapeDtypeStruct((len(pieces),) + pieces[0].shape, BF16),
        [VMEM] * len(pieces) + [ANY] * len(after),
        VMEM,
        [],
        *pieces,
        *after,
    )


def place_kernel(keys, *refs):
    bundles, (down, up, token, sems) = refs[: len(keys)], refs[-4:]
    token[...] = jnp.zeros_like(token)
    shard = lax.axis_index("shard")
    rows, width = down.shape[2:]
    tall, cols = up.shape[2:]
    copies = []

    def send(source, dest):
        copies.append(pltpu.make_async_copy(source, dest, sems.at[len(copies)]))
        copies[-1].start()

    for pieces, (low, slots) in zip(bundles, keys):
        for i, (slot, mask) in enumerate(slots):
            owner, place = owners()[slot], jnp.bitwise_xor(shard, mask ^ low)
            send(pieces.at[i, pl.ds(0, rows)], down.at[owner, place])
            for chunk in range(cols // width):
                send(
                    pieces.at[i, pl.ds(rows + chunk * tall, tall)],
                    up.at[owner, place, :, pl.ds(chunk * width, width)],
                )
    for copy in copies:
        copy.wait()


def place_embed_kernel(slots, *refs):
    pieces, (out, sems) = refs[: len(slots)], refs[-2:]
    copies = [
        pltpu.make_async_copy(piece, out.at[owners()[slot]], sems.at[i])
        for i, (piece, slot) in enumerate(zip(pieces, slots))
    ]
    for copy in copies:
        copy.start()
    for copy in copies:
        copy.wait()


def spread_low(x):
    found = {0: x}
    for bit in bits_down(lax.axis_size("shard") // 2):
        found.update({mask ^ bit: swap(y, "shard", bit) for mask, y in list(found.items())})
    return found


def body(
    trained_up,
    trained_down,
    trained_embed,
    trained_norm,
    master_up,
    moment_up,
    master_down,
    moment_down,
    master_embed,
    moment_embed,
    master_norm,
    moment_norm,
    embed_basis,
):
    replicas = lax.axis_size("replica")
    shards = lax.axis_size("shard")
    tensors = lax.axis_size("tensor")
    width, rank = embed_basis.shape
    rows_up, half_cols = master_up.shape[0], trained_up.shape[2]
    rows_down, rows_embed = master_down.shape[1], master_embed.shape[1]
    tall = tensors * rows_up
    chunks = half_cols // width
    packed = jax.ShapeDtypeStruct((rows_down + chunks * tall, width), BF16)
    dma = pltpu.SemaphoreType.DMA

    basis_t = embed_basis.T
    rank_rows = jax.ShapeDtypeStruct((rank, rows_embed), F32)
    packet = jax.ShapeDtypeStruct((rank + 16, rows_embed), BF16)
    token_shape = jax.ShapeDtypeStruct((8, 128), F32)
    own_rows, *packets = call(
        project_kernel,
        "project_rows",
        [rank_rows] + [packet] * (replicas - 1),
        [VMEM] * 3,
        [VMEM] * replicas,
        [pltpu.VMEM((rank, replicas * rows_embed), F32)],
        pltpu.with_memory_space_constraint(trained_embed[0], pltpu.HBM),
        pltpu.with_memory_space_constraint(basis_t, pltpu.HBM),
        pltpu.with_memory_space_constraint(trained_norm[0], pltpu.HBM),
    )
    down = trained_down[0].reshape(replicas, shards, rows_down, width)
    up = trained_up[0].reshape(replicas, shards, tall, half_cols)
    own, near, middle, end = call(
        pack_kernel,
        "pack_blocks",
        [packed] * replicas,
        [HBM] * 2,
        [VMEM] * replicas,
        [dma((replicas * (1 + chunks),))],
        pltpu.with_memory_space_constraint(down, pltpu.HBM),
        pltpu.with_memory_space_constraint(up, pltpu.HBM),
    )
    from_end = [along(x, INWARD) for x in (end, middle, near)]
    end_sum = add(end, from_end[0])
    packets_came = [swap(x, "replica", mask) for mask, x in enumerate(packets, 1)]

    state = jax.ShapeDtypeStruct((2, rows_up, half_cols), F32)
    states = call(
        functools.partial(state_kernel, tensors),
        "up_state",
        [state] * (tensors - 1),
        [VMEM] * 2,
        [VMEM] * (tensors - 1),
        [],
        master_up,
        moment_up,
    )
    states = [
        lax.ppermute(x, "tensor", [(i, (i + shift) % tensors) for i in range(tensors)])
        for shift, x in enumerate(states, 1)
    ]

    base = lax.dot_general(
        basis_t, master_embed[0], (((1,), (1,)), ((), ())), precision=HIGHEST
    )
    norm_state = jax.ShapeDtypeStruct(master_norm.shape, F32)
    embed_rows = jax.ShapeDtypeStruct((rows_embed, width), BF16)
    stored_rows, recast_rows, velocity_rows, norm_cast, stored_norm, velocity_norm = call(
        functools.partial(embed_kernel, replicas, replicas - 1),
        "embed_update",
        [
            jax.ShapeDtypeStruct((rows_embed, width), F32),
            embed_rows,
            rank_rows,
            jax.ShapeDtypeStruct(master_norm.shape, BF16),
            norm_state,
            norm_state,
        ],
        [VMEM] * (7 + replicas),
        [VMEM] * 6,
        [],
        own_rows,
        base,
        master_embed[0],
        moment_embed[0].T,
        basis_t,
        trained_norm[0],
        master_norm,
        moment_norm,
        *packets_came,
    )

    embed_out = along(recast_rows, OUTWARD)
    end_partial = along(end_sum, ACROSS)
    middle_partial = along(add(middle, from_end[1]), ACROSS)
    to_end = along(add(near, end_partial, embed_out), OUTWARD)
    came0 = [own, from_end[2], middle_partial, to_end]
    half_sum = jax.ShapeDtypeStruct((rows_up, half_cols), F32)
    down_state = jax.ShapeDtypeStruct((rows_down, width), F32)
    piece, stored_down, velocity_down, *sums = call(
        functools.partial(update_kernel, replicas, tensors, len(came0)),
        "update_rows",
        [packed, down_state, down_state] + [half_sum] * tensors,
        [VMEM] * (4 + len(came0) + len(states)),
        [VMEM] * (3 + tensors),
        [pltpu.VMEM((tall, half_cols), F32)] * 3,
        master_down[0],
        moment_down[0],
        master_up,
        moment_up,
        *came0,
        *states,
    )

    top = shards // 2
    far_piece = swap(piece, "shard", top)
    middle_piece = along(piece, ACROSS)
    near_piece = gate(swap(piece, "replica", 1), far_piece, middle_piece)
    far_near = swap(near_piece, "shard", top)
    end_piece = along(near_piece, ACROSS)
    embed_late = gate(recast_rows, near_piece)
    embed_in = along(embed_late, INWARD)
    embed_middle = along(embed_late, ACROSS)
    sums = [sums[0]] + [
        lax.ppermute(
            gate(x, near_piece), "tensor", [(i, (i + shift) % tensors) for i in range(tensors)]
        )
        for shift, x in enumerate(sums[1:], 1)
    ]
    second = pick(middle_piece, along(middle_piece, OUTWARD), far_near)
    far_second = swap(second, "shard", top)
    third = pick(end_piece, along(end_piece, OUTWARD), embed_in, embed_middle, far_second, *sums[1:])
    far_third = swap(third, "shard", top)
    bundles = [
        (
            [(0, 0), (0, top), (1, 0), (1, top)],
            spread_low(bundle([piece, far_piece, near_piece, far_near], third)),
        ),
        (
            [(2, 0), (2, top), (3, 0)],
            spread_low(bundle([second, far_second, third])),
        ),
    ]

    embed_middle_out = along(embed_middle, OUTWARD)
    embed_end = along(gate(embed_in, third), ACROSS)
    embed_last = along(embed_end, OUTWARD)

    stored_up, velocity_up, token = call(
        functools.partial(up_kernel, replicas, tensors),
        "update_up",
        [jax.ShapeDtypeStruct(master_up.shape, F32)] * 2 + [token_shape],
        [VMEM] * (2 + tensors),
        [VMEM] * 3,
        [],
        master_up,
        moment_up,
        *sums,
    )

    embed_shape = jax.ShapeDtypeStruct((replicas, rows_embed, width), BF16)
    recast_embed = call(
        functools.partial(place_embed_kernel, [0, 1, 2]),
        "place_embed",
        embed_shape,
        [VMEM] * 4,
        HBM,
        [dma((3,))],
        recast_rows,
        pick(embed_in, embed_out),
        pick(embed_middle, embed_middle_out),
        token,
    )

    shapes = [jax.ShapeDtypeStruct(down.shape, BF16), jax.ShapeDtypeStruct(up.shape, BF16)]

    def place(slots, arrays, placed, *after):
        keys = [(low, slots) for low in arrays]
        count = len(keys) + len(after)
        return call(
            functools.partial(place_kernel, keys),
            "place_rows",
            shapes + [token_shape],
            [VMEM] * count + [HBM] * len(placed),
            [HBM] * 2 + [VMEM],
            [dma((len(keys) * len(slots) * (1 + chunks),))],
            *arrays.values(),
            *after,
            *placed,
            aliases={count: 0, count + 1: 1} if placed else {},
        )

    placed = []
    for slots, arrays in bundles:
        *placed, token = place(slots, arrays, placed, token)
    last = spread_low(bundle([far_third], token))
    recast_down, recast_up, token = place([(3, top)], last, placed)
    recast_embed = call(
        functools.partial(place_embed_kernel, [3]),
        "place_embed",
        embed_shape,
        [VMEM] * 2 + [HBM],
        HBM,
        [dma((1,))],
        pick(embed_end, embed_last),
        token,
        recast_embed,
        aliases={2: 0},
    )

    return (
        recast_up.reshape(-1, half_cols),
        recast_down.reshape(-1, width),
        recast_embed.reshape(-1, width),
        norm_cast,
        stored_up,
        velocity_up,
        stored_down[None],
        velocity_down[None],
        stored_rows[None],
        velocity_rows.T[None],
        stored_norm,
        velocity_norm,
    )


def solution(mesh):
    in_specs = (
        P("replica", None, "tensor"),
        P("replica", "tensor", None),
        P("replica", ("shard", "tensor"), None),
        P("replica", None, None),
        P(("replica", "shard", "tensor"), None),
        P(("replica", "shard", "tensor"), None),
        P("tensor", ("replica", "shard"), None),
        P("tensor", ("replica", "shard"), None),
        P(("shard", "tensor"), "replica", None),
        P(("shard", "tensor"), "replica", None),
        P(),
        P(),
        P(),
    )
    out_specs = (
        P(None, "tensor"),
        P("tensor", None),
        P(("shard", "tensor"), None),
        P(),
        P(("replica", "shard", "tensor"), None),
        P(("replica", "shard", "tensor"), None),
        P("tensor", ("replica", "shard"), None),
        P("tensor", ("replica", "shard"), None),
        P(("shard", "tensor"), "replica", None),
        P(("shard", "tensor"), "replica", None),
        P(),
        P(),
    )
    return jax.shard_map(body, mesh=mesh, in_specs=in_specs, out_specs=out_specs, check_vma=False)
```

```python
import functools

import jax
import jax.numpy as jnp
from jax import lax
from jax.experimental import pallas as pl
from jax.experimental.pallas import tpu as pltpu
from jax.sharding import PartitionSpec as P

F32 = jnp.float32
BF16 = jnp.bfloat16
HIGHEST = lax.Precision.HIGHEST
HBM = pl.BlockSpec(memory_space=pltpu.HBM)
ANY = pl.BlockSpec(memory_space=pl.ANY)
VMEM = pl.BlockSpec(memory_space=pltpu.VMEM)


def outer_step(master, moment, summed, groups):
    difference = master - summed / groups
    velocity = 0.5 * moment + difference
    return (master - 0.7 * (difference + 0.5 * velocity), velocity)


def call(kernel, name, out_shape, in_specs, out_specs, scratch, *operands, limit=24, aliases={}):
    size = sum(x.size * x.dtype.itemsize for x in jax.tree.leaves(out_shape))
    return pl.pallas_call(
        kernel,
        name=name,
        out_shape=out_shape,
        in_specs=in_specs,
        out_specs=out_specs,
        scratch_shapes=scratch,
        input_output_aliases=aliases,
        compiler_params=pltpu.CompilerParams(vmem_limit_bytes=limit * 2**20),
        cost_estimate=pl.CostEstimate(flops=0, bytes_accessed=3 * size, transcendentals=0),
    )(*operands)


OUTER = (0, 3)
INWARD = ((0, 1), (3, 2))
ACROSS = ((1, 2), (2, 1))
OUTWARD = ((1, 0), (2, 3))


def owners():
    pos = lax.axis_index("replica")
    low = pos < 2
    return pos, jnp.bitwise_xor(pos, 1), jnp.where(low, 2, 1), jnp.where(low, 3, 0)


def along(x, pairs):
    return lax.ppermute(x, "replica", pairs)


def swap(x, axis, bit):
    return lax.ppermute(x, axis, [(i, i ^ bit) for i in range(lax.axis_size(axis))])


def bits_down(size):
    bit = size // 2
    while bit:
        yield bit
        bit //= 2


def project_kernel(trained, basis, norm, own, *refs):
    *outs, projected = refs
    rank, rows = basis.shape[0], own.shape[1]
    high = basis[...].astype(BF16)
    rest = basis[...] - high.astype(F32)
    middle = rest.astype(BF16)
    low = (rest - middle.astype(F32)).astype(BF16)
    split = jnp.concatenate([high, middle, low], axis=0)
    product = lax.dot_general(
        split, trained[...], (((1,), (1,)), ((), ())), preferred_element_type=F32
    )
    projected[...] = product[:rank] + (product[rank : 2 * rank] + product[2 * rank :])
    pos = lax.axis_index("replica")
    values = norm[...].astype(F32)
    per = norm.shape[1] // rows
    extra = outs[0].shape[0] - rank
    parts = [
        values[i // per : i // per + 1, (i % per) * rows : (i % per + 1) * rows]
        for i in range(norm.shape[0] * per)
    ]
    parts = jnp.concatenate((parts * extra)[:extra], axis=0).astype(BF16)
    own[...] = projected[:, pl.ds(pl.multiple_of(pos * rows, rows), rows)]
    for mask, out in enumerate(outs, 1):
        owner = jnp.bitwise_xor(pos, mask)
        block = projected[:, pl.ds(pl.multiple_of(owner * rows, rows), rows)]
        out[:rank, :] = block.astype(BF16)
        out[rank:, :] = parts


def embed_kernel(groups, n_came, *refs):
    refs = list(refs)
    own, base, master, moment, basis, norm, master_norm, moment_norm = refs[:8]
    came = refs[8 : 8 + n_came]
    stored, recast, velocity, norm_cast, norm_stored, norm_velocity = refs[-6:]
    rank, rows = own.shape
    total = own[...]
    for ref in came:
        total = total + ref[:rank, :].astype(F32)
    coefficient = base[...] - total / groups
    moved = 0.5 * moment[...] + coefficient
    velocity[...] = moved
    change = lax.dot_general(
        coefficient + 0.5 * moved,
        basis[...],
        (((0,), (0,)), ((), ())),
        precision=HIGHEST,
        preferred_element_type=F32,
    )
    new = master[...] - 0.7 * change
    stored[...] = new
    recast[...] = new.astype(BF16)
    per = norm.shape[1] // rows
    values = norm[...].astype(F32)
    tails = [ref[rank:, :].astype(F32) for ref in came]
    for i in range(norm.shape[0] * per):
        row, span = i // per, slice((i % per) * rows, (i % per + 1) * rows)
        summed = values[row : row + 1, span]
        for tail in tails:
            summed = summed + tail[i : i + 1, :]
        new_norm, moved_norm = outer_step(
            master_norm[row : row + 1, span], moment_norm[row : row + 1, span], summed, groups
        )
        norm_stored[row : row + 1, span] = new_norm
        norm_velocity[row : row + 1, span] = moved_norm
    norm_cast[...] = norm_stored[...].astype(BF16)


def pack_kernel(down, up, *refs):
    *outs, sems = refs
    shard = lax.axis_index("shard")
    rows, width = down.shape[2:]
    tall, cols = up.shape[2:]
    copies = []

    def bring(source, dest):
        copies.append(pltpu.make_async_copy(source, dest, sems.at[len(copies)]))
        copies[-1].start()

    for owner, out in reversed(list(zip(owners(), outs))):
        bring(down.at[owner, shard], out.at[pl.ds(0, rows)])
        for chunk in range(cols // width):
            bring(
                up.at[owner, shard, :, pl.ds(chunk * width, width)],
                out.at[pl.ds(rows + chunk * tall, tall)],
            )
    for copy in copies:
        copy.wait()


def add_kernel(block, came, *refs):
    refs[-1][...] = (block[...].astype(F32) + came[...].astype(F32)).astype(BF16)


def add(block, came, *after):
    return call(
        add_kernel,
        "add_block",
        jax.ShapeDtypeStruct(block.shape, BF16),
        [VMEM] * 2 + [ANY] * len(after),
        VMEM,
        [],
        block,
        came,
        *after,
    )


def pick_kernel(middle, end, *refs):
    out = refs[-1]
    pos = lax.axis_index("replica")
    outer = jnp.logical_or(pos == OUTER[0], pos == OUTER[1])

    @pl.when(outer)
    def _():
        out[...] = end[...]

    @pl.when(jnp.logical_not(outer))
    def _():
        out[...] = middle[...]


def pick(middle, end, *after):
    specs = [VMEM] * 2 + [ANY] * len(after)
    shape = jax.ShapeDtypeStruct(end.shape, end.dtype)
    return call(pick_kernel, "pick", shape, specs, VMEM, [], middle, end, *after)


def update_kernel(groups, tensors, n_came, *refs):
    refs = list(refs)
    master_down, moment_down, master_up, moment_up = refs[:4]
    came, state_came = refs[4 : 4 + n_came], refs[4 + n_came : 3 + n_came + tensors]
    piece, stored_down, velocity_down, *sums = refs[3 + n_came + tensors : -3]
    summed, master, moment = refs[-3:]
    me = lax.axis_index("tensor")
    rows_down, width = master_down.shape
    rows_up = master_up.shape[0]
    tall, cols = summed.shape

    def at(index):
        return pl.ds(pl.multiple_of(index * rows_up, rows_up), rows_up)

    own_cols = pl.ds(pl.multiple_of(me * cols, cols), cols)
    master[at(me), :] = master_up[:, own_cols]
    moment[at(me), :] = moment_up[:, own_cols]
    for shift in range(1, tensors):
        source = lax.rem(me + tensors - shift, tensors)
        master[at(source), :] = state_came[shift - 1][0]
        moment[at(source), :] = state_came[shift - 1][1]

    def total(lo, hi):
        value = came[0][lo:hi, :].astype(F32)
        for ref in came[1:]:
            value = value + ref[lo:hi, :].astype(F32)
        return value

    stored, velocity = outer_step(
        master_down[...], moment_down[...], total(0, rows_down), groups
    )
    stored_down[...] = stored
    velocity_down[...] = velocity
    piece[:rows_down, :] = stored.astype(BF16)
    for chunk in range(cols // width):
        lo = rows_down + chunk * tall
        part = total(lo, lo + tall)
        span = slice(chunk * width, (chunk + 1) * width)
        summed[:, span] = part
        stored, _ = outer_step(master[:, span], moment[:, span], part, groups)
        piece[lo : lo + tall, :] = stored.astype(BF16)
    for shift in range(tensors):
        sums[shift][...] = summed[at(lax.rem(me + shift, tensors)), :]


def up_kernel(groups, tensors, master_up, moment_up, *refs):
    sums, (stored_up, velocity_up, token) = refs[:tensors], refs[tensors:]
    cols = sums[0].shape[1]
    me = lax.axis_index("tensor")
    for shift in range(tensors):
        source = lax.rem(me + tensors - shift, tensors)
        span = pl.ds(pl.multiple_of(source * cols, cols), cols)
        stored, velocity = outer_step(
            master_up[:, span], moment_up[:, span], sums[shift][...], groups
        )
        stored_up[:, span] = stored
        velocity_up[:, span] = velocity
    token[...] = jnp.zeros_like(token)


def state_kernel(tensors, master_up, moment_up, *outs):
    me = lax.axis_index("tensor")
    cols = outs[0].shape[2]
    for shift in range(1, tensors):
        target = lax.rem(me + shift, tensors)
        span = pl.ds(pl.multiple_of(target * cols, cols), cols)
        outs[shift - 1][0] = master_up[:, span]
        outs[shift - 1][1] = moment_up[:, span]


def gate_kernel(x, *refs):
    refs[-1][...] = x[...]


def gate(x, *after):
    return call(
        gate_kernel,
        "gate",
        jax.ShapeDtypeStruct(x.shape, x.dtype),
        [VMEM] + [ANY] * len(after),
        VMEM,
        [],
        x,
        *after,
    )


def stack_kernel(count, *refs):
    for i in range(count):
        refs[-1][i] = refs[i][...]


def bundle(pieces, *after):
    return call(
        functools.partial(stack_kernel, len(pieces)),
        "bundle",
        jax.ShapeDtypeStruct((len(pieces),) + pieces[0].shape, BF16),
        [VMEM] * len(pieces) + [ANY] * len(after),
        VMEM,
        [],
        *pieces,
        *after,
    )


def place_kernel(keys, *refs):
    bundles, (down, up, token, sems) = refs[: len(keys)], refs[-4:]
    token[...] = jnp.zeros_like(token)
    shard = lax.axis_index("shard")
    rows, width = down.shape[2:]
    tall, cols = up.shape[2:]
    copies = []

    def send(source, dest):
        copies.append(pltpu.make_async_copy(source, dest, sems.at[len(copies)]))
        copies[-1].start()

    for pieces, (low, slots) in zip(bundles, keys):
        for i, (slot, mask) in enumerate(slots):
            owner, place = owners()[slot], jnp.bitwise_xor(shard, mask ^ low)
            send(pieces.at[i, pl.ds(0, rows)], down.at[owner, place])
            for chunk in range(cols // width):
                send(
                    pieces.at[i, pl.ds(rows + chunk * tall, tall)],
                    up.at[owner, place, :, pl.ds(chunk * width, width)],
                )
    for copy in copies:
        copy.wait()


def place_embed_kernel(slots, *refs):
    pieces, (out, sems) = refs[: len(slots)], refs[-2:]
    copies = [
        pltpu.make_async_copy(piece, out.at[owners()[slot]], sems.at[i])
        for i, (piece, slot) in enumerate(zip(pieces, slots))
    ]
    for copy in copies:
        copy.start()
    for copy in copies:
        copy.wait()


def spread_low(x):
    found = {0: x}
    for bit in bits_down(lax.axis_size("shard") // 2):
        found.update({mask ^ bit: swap(y, "shard", bit) for mask, y in list(found.items())})
    return found


def body(
    trained_up,
    trained_down,
    trained_embed,
    trained_norm,
    master_up,
    moment_up,
    master_down,
    moment_down,
    master_embed,
    moment_embed,
    master_norm,
    moment_norm,
    embed_basis,
):
    replicas = lax.axis_size("replica")
    shards = lax.axis_size("shard")
    tensors = lax.axis_size("tensor")
    width, rank = embed_basis.shape
    rows_up, half_cols = master_up.shape[0], trained_up.shape[2]
    rows_down, rows_embed = master_down.shape[1], master_embed.shape[1]
    tall = tensors * rows_up
    chunks = half_cols // width
    packed = jax.ShapeDtypeStruct((rows_down + chunks * tall, width), BF16)
    dma = pltpu.SemaphoreType.DMA

    basis_t = embed_basis.T
    rank_rows = jax.ShapeDtypeStruct((rank, rows_embed), F32)
    packet = jax.ShapeDtypeStruct((rank + 16, rows_embed), BF16)
    token_shape = jax.ShapeDtypeStruct((8, 128), F32)
    own_rows, *packets = call(
        project_kernel,
        "project_rows",
        [rank_rows] + [packet] * (replicas - 1),
        [VMEM] * 3,
        [VMEM] * replicas,
        [pltpu.VMEM((rank, replicas * rows_embed), F32)],
        pltpu.with_memory_space_constraint(trained_embed[0], pltpu.HBM),
        pltpu.with_memory_space_constraint(basis_t, pltpu.HBM),
        pltpu.with_memory_space_constraint(trained_norm[0], pltpu.HBM),
    )
    down = trained_down[0].reshape(replicas, shards, rows_down, width)
    up = trained_up[0].reshape(replicas, shards, tall, half_cols)
    own, near, middle, end = call(
        pack_kernel,
        "pack_blocks",
        [packed] * replicas,
        [HBM] * 2,
        [VMEM] * replicas,
        [dma((replicas * (1 + chunks),))],
        pltpu.with_memory_space_constraint(down, pltpu.HBM),
        pltpu.with_memory_space_constraint(up, pltpu.HBM),
    )
    packets_came = [swap(packets[0], "replica", 1), swap(packets[1], "replica", 2)]
    end = gate(end, packets_came[0])
    packets_came.append(swap(gate(packets[2], end), "replica", 3))
    from_end = [along(x, INWARD) for x in (end, middle, near)]

    state = jax.ShapeDtypeStruct((2, rows_up, half_cols), F32)
    states = call(
        functools.partial(state_kernel, tensors),
        "up_state",
        [state] * (tensors - 1),
        [VMEM] * 2,
        [VMEM] * (tensors - 1),
        [],
        master_up,
        moment_up,
    )
    states = [
        lax.ppermute(x, "tensor", [(i, (i + shift) % tensors) for i in range(tensors)])
        for shift, x in enumerate(states, 1)
    ]

    base = lax.dot_general(
        basis_t, master_embed[0], (((1,), (1,)), ((), ())), precision=HIGHEST
    )
    norm_state = jax.ShapeDtypeStruct(master_norm.shape, F32)
    embed_rows = jax.ShapeDtypeStruct((rows_embed, width), BF16)
    stored_rows, recast_rows, velocity_rows, norm_cast, stored_norm, velocity_norm = call(
        functools.partial(embed_kernel, replicas, replicas - 1),
        "embed_update",
        [
            jax.ShapeDtypeStruct((rows_embed, width), F32),
            embed_rows,
            rank_rows,
            jax.ShapeDtypeStruct(master_norm.shape, BF16),
            norm_state,
            norm_state,
        ],
        [VMEM] * (7 + replicas),
        [VMEM] * 6,
        [],
        own_rows,
        base,
        master_embed[0],
        moment_embed[0].T,
        basis_t,
        trained_norm[0],
        master_norm,
        moment_norm,
        *packets_came,
    )

    embed_out = along(recast_rows, OUTWARD)
    embed_middle = along(recast_rows, ACROSS)
    end_partial = along(add(end, from_end[0], embed_middle), ACROSS)
    middle_partial = along(add(middle, from_end[1]), ACROSS)
    embed_middle_out = along(embed_middle, OUTWARD)
    to_end = along(add(near, end_partial, embed_out, embed_middle_out), OUTWARD)
    came0 = [own, from_end[2], middle_partial, to_end]
    half_sum = jax.ShapeDtypeStruct((rows_up, half_cols), F32)
    down_state = jax.ShapeDtypeStruct((rows_down, width), F32)
    piece, stored_down, velocity_down, *sums = call(
        functools.partial(update_kernel, replicas, tensors, len(came0)),
        "update_rows",
        [packed, down_state, down_state] + [half_sum] * tensors,
        [VMEM] * (4 + len(came0) + len(states)),
        [VMEM] * (3 + tensors),
        [pltpu.VMEM((tall, half_cols), F32)] * 3,
        master_down[0],
        moment_down[0],
        master_up,
        moment_up,
        *came0,
        *states,
    )

    top = shards // 2
    far_piece = swap(piece, "shard", top)
    middle_piece = along(piece, ACROSS)
    near_piece = gate(swap(piece, "replica", 1), far_piece, middle_piece)
    far_near = swap(near_piece, "shard", top)
    end_piece = along(near_piece, ACROSS)
    embed_in = along(gate(recast_rows, piece), INWARD)
    sums = [sums[0]] + [
        lax.ppermute(
            gate(x, near_piece), "tensor", [(i, (i + shift) % tensors) for i in range(tensors)]
        )
        for shift, x in enumerate(sums[1:], 1)
    ]
    second = pick(middle_piece, along(middle_piece, OUTWARD), far_near, embed_in)
    far_second = swap(second, "shard", top)
    embed_end = along(embed_in, ACROSS)
    third = pick(end_piece, along(end_piece, OUTWARD), embed_end, far_second, *sums[1:])
    far_third = swap(third, "shard", top)
    bundles = [
        (
            [(0, 0), (0, top), (1, 0), (1, top)],
            spread_low(bundle([piece, far_piece, near_piece, far_near], third)),
        ),
        (
            [(2, 0), (2, top), (3, 0)],
            spread_low(bundle([second, far_second, third])),
        ),
    ]

    embed_last = along(embed_end, OUTWARD)

    stored_up, velocity_up, token = call(
        functools.partial(up_kernel, replicas, tensors),
        "update_up",
        [jax.ShapeDtypeStruct(master_up.shape, F32)] * 2 + [token_shape],
        [VMEM] * (2 + tensors),
        [VMEM] * 3,
        [],
        master_up,
        moment_up,
        *sums,
    )

    embed_shape = jax.ShapeDtypeStruct((replicas, rows_embed, width), BF16)
    recast_embed = call(
        functools.partial(place_embed_kernel, [0, 1, 2]),
        "place_embed",
        embed_shape,
        [VMEM] * 4,
        HBM,
        [dma((3,))],
        recast_rows,
        pick(embed_in, embed_out),
        pick(embed_middle, embed_middle_out),
        token,
    )

    shapes = [jax.ShapeDtypeStruct(down.shape, BF16), jax.ShapeDtypeStruct(up.shape, BF16)]

    def place(slots, arrays, placed, *after):
        keys = [(low, slots) for low in arrays]
        count = len(keys) + len(after)
        return call(
            functools.partial(place_kernel, keys),
            "place_rows",
            shapes + [token_shape],
            [VMEM] * count + [HBM] * len(placed),
            [HBM] * 2 + [VMEM],
            [dma((len(keys) * len(slots) * (1 + chunks),))],
            *arrays.values(),
            *after,
            *placed,
            aliases={count: 0, count + 1: 1} if placed else {},
        )

    placed = []
    for slots, arrays in bundles:
        *placed, token = place(slots, arrays, placed, token)
    last = spread_low(bundle([far_third], token))
    recast_down, recast_up, token = place([(3, top)], last, placed)
    recast_embed = call(
        functools.partial(place_embed_kernel, [3]),
        "place_embed",
        embed_shape,
        [VMEM] * 2 + [HBM],
        HBM,
        [dma((1,))],
        pick(embed_end, embed_last),
        token,
        recast_embed,
        aliases={2: 0},
    )

    return (
        recast_up.reshape(-1, half_cols),
        recast_down.reshape(-1, width),
        recast_embed.reshape(-1, width),
        norm_cast,
        stored_up,
        velocity_up,
        stored_down[None],
        velocity_down[None],
        stored_rows[None],
        velocity_rows.T[None],
        stored_norm,
        velocity_norm,
    )


def solution(mesh):
    in_specs = (
        P("replica", None, "tensor"),
        P("replica", "tensor", None),
        P("replica", ("shard", "tensor"), None),
        P("replica", None, None),
        P(("replica", "shard", "tensor"), None),
        P(("replica", "shard", "tensor"), None),
        P("tensor", ("replica", "shard"), None),
        P("tensor", ("replica", "shard"), None),
        P(("shard", "tensor"), "replica", None),
        P(("shard", "tensor"), "replica", None),
        P(),
        P(),
        P(),
    )
    out_specs = (
        P(None, "tensor"),
        P("tensor", None),
        P(("shard", "tensor"), None),
        P(),
        P(("replica", "shard", "tensor"), None),
        P(("replica", "shard", "tensor"), None),
        P("tensor", ("replica", "shard"), None),
        P("tensor", ("replica", "shard"), None),
        P(("shard", "tensor"), "replica", None),
        P(("shard", "tensor"), "replica", None),
        P(),
        P(),
    )
    return jax.shard_map(body, mesh=mesh, in_specs=in_specs, out_specs=out_specs, check_vma=False)
```

```python
import functools

import jax
import jax.numpy as jnp
from jax import lax
from jax.experimental import pallas as pl
from jax.experimental.pallas import tpu as pltpu
from jax.sharding import PartitionSpec as P

F32 = jnp.float32
BF16 = jnp.bfloat16
HIGHEST = lax.Precision.HIGHEST
HBM = pl.BlockSpec(memory_space=pltpu.HBM)
ANY = pl.BlockSpec(memory_space=pl.ANY)
VMEM = pl.BlockSpec(memory_space=pltpu.VMEM)


def outer_step(master, moment, summed, groups):
    difference = master - summed / groups
    velocity = 0.5 * moment + difference
    return (master - 0.7 * (difference + 0.5 * velocity), velocity)


def call(kernel, name, out_shape, in_specs, out_specs, scratch, *operands, limit=24, aliases={}):
    size = sum(x.size * x.dtype.itemsize for x in jax.tree.leaves(out_shape))
    return pl.pallas_call(
        kernel,
        name=name,
        out_shape=out_shape,
        in_specs=in_specs,
        out_specs=out_specs,
        scratch_shapes=scratch,
        input_output_aliases=aliases,
        compiler_params=pltpu.CompilerParams(vmem_limit_bytes=limit * 2**20),
        cost_estimate=pl.CostEstimate(flops=0, bytes_accessed=3 * size, transcendentals=0),
    )(*operands)


OUTER = (0, 3)
INWARD = ((0, 1), (3, 2))
ACROSS = ((1, 2), (2, 1))
OUTWARD = ((1, 0), (2, 3))


def owners():
    pos = lax.axis_index("replica")
    low = pos < 2
    return pos, jnp.bitwise_xor(pos, 1), jnp.where(low, 2, 1), jnp.where(low, 3, 0)


def along(x, pairs):
    return lax.ppermute(x, "replica", pairs)


def swap(x, axis, bit):
    return lax.ppermute(x, axis, [(i, i ^ bit) for i in range(lax.axis_size(axis))])


def bits_down(size):
    bit = size // 2
    while bit:
        yield bit
        bit //= 2


def prepare_kernel(n_slots, trained, basis, norm, down, up, *refs):
    blocks, (own, *outs, projected, sems) = refs[:n_slots], refs[n_slots:]
    shard = lax.axis_index("shard")
    height, width = down.shape[2:]
    tall, cols = up.shape[2:]
    copies = []

    def bring(source, dest):
        copies.append(pltpu.make_async_copy(source, dest, sems.at[len(copies)]))
        copies[-1].start()

    for owner, block in reversed(list(zip(owners(), blocks))):
        bring(down.at[owner, shard], block.at[pl.ds(0, height)])
        for chunk in range(cols // width):
            bring(
                up.at[owner, shard, :, pl.ds(chunk * width, width)],
                block.at[pl.ds(height + chunk * tall, tall)],
            )

    rank, rows = basis.shape[0], own.shape[1]
    high = basis[...].astype(BF16)
    rest = basis[...] - high.astype(F32)
    middle = rest.astype(BF16)
    low = (rest - middle.astype(F32)).astype(BF16)
    split = jnp.concatenate([high, middle, low], axis=0)
    product = lax.dot_general(
        split, trained[...], (((1,), (1,)), ((), ())), preferred_element_type=F32
    )
    projected[...] = product[:rank] + (product[rank : 2 * rank] + product[2 * rank :])
    pos = lax.axis_index("replica")
    values = norm[...].astype(F32)
    per = norm.shape[1] // rows
    extra = outs[0].shape[0] - rank
    parts = [
        values[i // per : i // per + 1, (i % per) * rows : (i % per + 1) * rows]
        for i in range(norm.shape[0] * per)
    ]
    parts = jnp.concatenate((parts * extra)[:extra], axis=0).astype(BF16)
    own[...] = projected[:, pl.ds(pl.multiple_of(pos * rows, rows), rows)]
    for mask, out in enumerate(outs, 1):
        owner = jnp.bitwise_xor(pos, mask)
        block = projected[:, pl.ds(pl.multiple_of(owner * rows, rows), rows)]
        out[:rank, :] = block.astype(BF16)
        out[rank:, :] = parts
    for copy in copies:
        copy.wait()


def embed_kernel(groups, n_came, *refs):
    refs = list(refs)
    own, base, master, moment, basis, norm, master_norm, moment_norm = refs[:8]
    came = refs[8 : 8 + n_came]
    stored, recast, velocity, norm_cast, norm_stored, norm_velocity = refs[-6:]
    rank, rows = own.shape
    total = own[...]
    for ref in came:
        total = total + ref[:rank, :].astype(F32)
    coefficient = base[...] - total / groups
    moved = 0.5 * moment[...] + coefficient
    velocity[...] = moved
    change = lax.dot_general(
        coefficient + 0.5 * moved,
        basis[...],
        (((0,), (0,)), ((), ())),
        precision=HIGHEST,
        preferred_element_type=F32,
    )
    new = master[...] - 0.7 * change
    stored[...] = new
    recast[...] = new.astype(BF16)
    per = norm.shape[1] // rows
    values = norm[...].astype(F32)
    tails = [ref[rank:, :].astype(F32) for ref in came]
    for i in range(norm.shape[0] * per):
        row, span = i // per, slice((i % per) * rows, (i % per + 1) * rows)
        summed = values[row : row + 1, span]
        for tail in tails:
            summed = summed + tail[i : i + 1, :]
        new_norm, moved_norm = outer_step(
            master_norm[row : row + 1, span], moment_norm[row : row + 1, span], summed, groups
        )
        norm_stored[row : row + 1, span] = new_norm
        norm_velocity[row : row + 1, span] = moved_norm
    norm_cast[...] = norm_stored[...].astype(BF16)


def add_kernel(block, came, *refs):
    refs[-1][...] = (block[...].astype(F32) + came[...].astype(F32)).astype(BF16)


def add(block, came, *after):
    return call(
        add_kernel,
        "add_block",
        jax.ShapeDtypeStruct(block.shape, BF16),
        [VMEM] * 2 + [ANY] * len(after),
        VMEM,
        [],
        block,
        came,
        *after,
    )


def pick_kernel(middle, end, *refs):
    out = refs[-1]
    pos = lax.axis_index("replica")
    outer = jnp.logical_or(pos == OUTER[0], pos == OUTER[1])

    @pl.when(outer)
    def _():
        out[...] = end[...]

    @pl.when(jnp.logical_not(outer))
    def _():
        out[...] = middle[...]


def pick(middle, end, *after):
    specs = [VMEM] * 2 + [ANY] * len(after)
    shape = jax.ShapeDtypeStruct(end.shape, end.dtype)
    return call(pick_kernel, "pick", shape, specs, VMEM, [], middle, end, *after)


def update_kernel(groups, tensors, n_came, *refs):
    refs = list(refs)
    master_down, moment_down, master_up, moment_up = refs[:4]
    came, state_came = refs[4 : 4 + n_came], refs[4 + n_came : 3 + n_came + tensors]
    piece, stored_down, velocity_down, *sums = refs[3 + n_came + tensors : -3]
    summed, master, moment = refs[-3:]
    me = lax.axis_index("tensor")
    rows_down, width = master_down.shape
    rows_up = master_up.shape[0]
    tall, cols = summed.shape

    def at(index):
        return pl.ds(pl.multiple_of(index * rows_up, rows_up), rows_up)

    own_cols = pl.ds(pl.multiple_of(me * cols, cols), cols)
    master[at(me), :] = master_up[:, own_cols]
    moment[at(me), :] = moment_up[:, own_cols]
    for shift in range(1, tensors):
        source = lax.rem(me + tensors - shift, tensors)
        master[at(source), :] = state_came[shift - 1][0]
        moment[at(source), :] = state_came[shift - 1][1]

    def total(lo, hi):
        value = came[0][lo:hi, :].astype(F32)
        for ref in came[1:]:
            value = value + ref[lo:hi, :].astype(F32)
        return value

    stored, velocity = outer_step(
        master_down[...], moment_down[...], total(0, rows_down), groups
    )
    stored_down[...] = stored
    velocity_down[...] = velocity
    piece[:rows_down, :] = stored.astype(BF16)
    for chunk in range(cols // width):
        lo = rows_down + chunk * tall
        part = total(lo, lo + tall)
        span = slice(chunk * width, (chunk + 1) * width)
        summed[:, span] = part
        stored, _ = outer_step(master[:, span], moment[:, span], part, groups)
        piece[lo : lo + tall, :] = stored.astype(BF16)
    for shift in range(tensors):
        sums[shift][...] = summed[at(lax.rem(me + shift, tensors)), :]


def up_kernel(groups, tensors, master_up, moment_up, *refs):
    sums, (stored_up, velocity_up, token) = refs[:tensors], refs[-3:]
    cols = sums[0].shape[1]
    me = lax.axis_index("tensor")
    for shift in range(tensors):
        source = lax.rem(me + tensors - shift, tensors)
        span = pl.ds(pl.multiple_of(source * cols, cols), cols)
        stored, velocity = outer_step(
            master_up[:, span], moment_up[:, span], sums[shift][...], groups
        )
        stored_up[:, span] = stored
        velocity_up[:, span] = velocity
    token[...] = jnp.zeros_like(token)


def state_kernel(tensors, master_up, moment_up, *outs):
    me = lax.axis_index("tensor")
    cols = outs[0].shape[2]
    for shift in range(1, tensors):
        target = lax.rem(me + shift, tensors)
        span = pl.ds(pl.multiple_of(target * cols, cols), cols)
        outs[shift - 1][0] = master_up[:, span]
        outs[shift - 1][1] = moment_up[:, span]


def gate_kernel(x, *refs):
    refs[-1][...] = x[...]


def gate(x, *after):
    return call(
        gate_kernel,
        "gate",
        jax.ShapeDtypeStruct(x.shape, x.dtype),
        [VMEM] + [ANY] * len(after),
        VMEM,
        [],
        x,
        *after,
    )


def stack_kernel(count, *refs):
    for i in range(count):
        refs[-1][i] = refs[i][...]


def bundle(pieces, *after):
    return call(
        functools.partial(stack_kernel, len(pieces)),
        "bundle",
        jax.ShapeDtypeStruct((len(pieces),) + pieces[0].shape, BF16),
        [VMEM] * len(pieces) + [ANY] * len(after),
        VMEM,
        [],
        *pieces,
        *after,
    )


def place_kernel(keys, *refs):
    bundles, (down, up, token, sems) = refs[: len(keys)], refs[-4:]
    token[...] = jnp.zeros_like(token)
    shard = lax.axis_index("shard")
    rows, width = down.shape[2:]
    tall, cols = up.shape[2:]
    copies = []

    def send(source, dest):
        copies.append(pltpu.make_async_copy(source, dest, sems.at[len(copies)]))
        copies[-1].start()

    for pieces, (low, slots) in zip(bundles, keys):
        for i, (slot, mask) in enumerate(slots):
            owner, place = owners()[slot], jnp.bitwise_xor(shard, mask ^ low)
            send(pieces.at[i, pl.ds(0, rows)], down.at[owner, place])
            for chunk in range(cols // width):
                send(
                    pieces.at[i, pl.ds(rows + chunk * tall, tall)],
                    up.at[owner, place, :, pl.ds(chunk * width, width)],
                )
    for copy in copies:
        copy.wait()


def place_embed_kernel(slots, *refs):
    pieces, (out, token, sems) = refs[: len(slots)], refs[-3:]
    token[...] = jnp.zeros_like(token)
    copies = [
        pltpu.make_async_copy(piece, out.at[owners()[slot]], sems.at[i])
        for i, (piece, slot) in enumerate(zip(pieces, slots))
    ]
    for copy in copies:
        copy.start()
    for copy in copies:
        copy.wait()


def spread_low(x):
    found = {0: x}
    for bit in bits_down(lax.axis_size("shard") // 2):
        found.update({mask ^ bit: swap(y, "shard", bit) for mask, y in list(found.items())})
    return found


def body(
    trained_up,
    trained_down,
    trained_embed,
    trained_norm,
    master_up,
    moment_up,
    master_down,
    moment_down,
    master_embed,
    moment_embed,
    master_norm,
    moment_norm,
    embed_basis,
):
    replicas = lax.axis_size("replica")
    shards = lax.axis_size("shard")
    tensors = lax.axis_size("tensor")
    width, rank = embed_basis.shape
    rows_up, half_cols = master_up.shape[0], trained_up.shape[2]
    rows_down, rows_embed = master_down.shape[1], master_embed.shape[1]
    tall = tensors * rows_up
    chunks = half_cols // width
    packed = jax.ShapeDtypeStruct((rows_down + chunks * tall, width), BF16)
    dma = pltpu.SemaphoreType.DMA

    basis_t = embed_basis.T
    rank_rows = jax.ShapeDtypeStruct((rank, rows_embed), F32)
    packet = jax.ShapeDtypeStruct((rank + 16, rows_embed), BF16)
    token_shape = jax.ShapeDtypeStruct((8, 128), F32)
    down = trained_down[0].reshape(replicas, shards, rows_down, width)
    up = trained_up[0].reshape(replicas, shards, tall, half_cols)
    own, near, middle, end, own_rows, *packets = call(
        functools.partial(prepare_kernel, replicas),
        "prepare",
        [packed] * replicas + [rank_rows] + [packet] * (replicas - 1),
        [VMEM] * 3 + [HBM] * 2,
        [VMEM] * (2 * replicas),
        [
            pltpu.VMEM((rank, replicas * rows_embed), F32),
            dma((replicas * (1 + chunks),)),
        ],
        *[
            pltpu.with_memory_space_constraint(x, pltpu.HBM)
            for x in (trained_embed[0], basis_t, trained_norm[0], down, up)
        ],
    )

    packets_came = [swap(packets[0], "replica", 1), swap(packets[1], "replica", 2)]
    end = gate(end, packets_came[0])
    packets_came.append(swap(gate(packets[2], end), "replica", 3))
    from_end = along(end, INWARD)
    from_middle = along(middle, INWARD)

    state = jax.ShapeDtypeStruct((2, rows_up, half_cols), F32)
    states = call(
        functools.partial(state_kernel, tensors),
        "up_state",
        [state] * (tensors - 1),
        [VMEM] * 2,
        [VMEM] * (tensors - 1),
        [],
        master_up,
        moment_up,
    )
    states = [
        lax.ppermute(x, "tensor", [(i, (i + shift) % tensors) for i in range(tensors)])
        for shift, x in enumerate(states, 1)
    ]

    base = lax.dot_general(
        basis_t, master_embed[0], (((1,), (1,)), ((), ())), precision=HIGHEST
    )
    norm_state = jax.ShapeDtypeStruct(master_norm.shape, F32)
    embed_rows = jax.ShapeDtypeStruct((rows_embed, width), BF16)
    stored_rows, recast_rows, velocity_rows, norm_cast, stored_norm, velocity_norm = call(
        functools.partial(embed_kernel, replicas, replicas - 1),
        "embed_update",
        [
            jax.ShapeDtypeStruct((rows_embed, width), F32),
            embed_rows,
            rank_rows,
            jax.ShapeDtypeStruct(master_norm.shape, BF16),
            norm_state,
            norm_state,
        ],
        [VMEM] * (7 + replicas),
        [VMEM] * 6,
        [],
        own_rows,
        base,
        master_embed[0],
        moment_embed[0].T,
        basis_t,
        trained_norm[0],
        master_norm,
        moment_norm,
        *packets_came,
    )

    embed_out = along(recast_rows, OUTWARD)
    embed_middle = along(recast_rows, ACROSS)
    end_partial = along(add(end, from_end, embed_middle, embed_out), ACROSS)
    middle_sum = add(middle, from_middle)
    middle_partial = along(middle_sum, ACROSS)
    embed_middle_out = along(embed_middle, OUTWARD)
    to_end = along(add(near, end_partial, embed_middle_out), OUTWARD)
    from_near = along(gate(near, middle_sum), INWARD)
    came0 = [own, middle_partial, from_near, to_end]
    half_sum = jax.ShapeDtypeStruct((rows_up, half_cols), F32)
    down_state = jax.ShapeDtypeStruct((rows_down, width), F32)
    piece, stored_down, velocity_down, *sums = call(
        functools.partial(update_kernel, replicas, tensors, len(came0)),
        "update_rows",
        [packed, down_state, down_state] + [half_sum] * tensors,
        [VMEM] * (4 + len(came0) + len(states)),
        [VMEM] * (3 + tensors),
        [pltpu.VMEM((tall, half_cols), F32)] * 3,
        master_down[0],
        moment_down[0],
        master_up,
        moment_up,
        *came0,
        *states,
    )

    top = shards // 2
    came_near = swap(piece, "replica", 1)
    middle_piece = along(piece, ACROSS)
    far_piece = swap(piece, "shard", top)
    embed_in = along(gate(recast_rows, piece), INWARD)
    end_piece = along(came_near, ACROSS)
    second_out = along(gate(middle_piece, came_near), OUTWARD)
    near_piece = gate(came_near, far_piece)
    far_near = swap(near_piece, "shard", top)
    sums = [sums[0]] + [
        lax.ppermute(
            gate(x, near_piece), "tensor", [(i, (i + shift) % tensors) for i in range(tensors)]
        )
        for shift, x in enumerate(sums[1:], 1)
    ]
    second = pick(middle_piece, second_out, far_near, embed_in)
    far_second = swap(second, "shard", top)
    embed_end = along(embed_in, ACROSS)
    third = pick(end_piece, along(end_piece, OUTWARD), embed_end, far_second, *sums[1:])
    far_third = swap(third, "shard", top)
    embed_last = along(embed_end, OUTWARD)
    bundles = [
        (
            [(0, 0), (0, top), (1, 0), (1, top)],
            spread_low(bundle([piece, far_piece, near_piece, far_near], third)),
        ),
        (
            [(2, 0), (2, top), (3, 0)],
            spread_low(bundle([second, far_second, third])),
        ),
    ]

    stored_up, velocity_up, token = call(
        functools.partial(up_kernel, replicas, tensors),
        "update_up",
        [jax.ShapeDtypeStruct(master_up.shape, F32)] * 2 + [token_shape],
        [VMEM] * (2 + tensors) + [ANY],
        [VMEM] * 3,
        [],
        master_up,
        moment_up,
        *sums,
        list(bundles[0][1].values())[-1],
    )

    embed_shape = jax.ShapeDtypeStruct((replicas, rows_embed, width), BF16)
    recast_embed, token = call(
        functools.partial(place_embed_kernel, [0, 1, 2]),
        "place_embed",
        [embed_shape, token_shape],
        [VMEM] * 4,
        [HBM, VMEM],
        [dma((3,))],
        recast_rows,
        pick(embed_in, embed_out),
        pick(embed_middle, embed_middle_out),
        token,
    )

    shapes = [jax.ShapeDtypeStruct(down.shape, BF16), jax.ShapeDtypeStruct(up.shape, BF16)]

    def place(slots, arrays, placed, *after):
        keys = [(low, slots) for low in arrays]
        count = len(keys) + len(after)
        return call(
            functools.partial(place_kernel, keys),
            "place_rows",
            shapes + [token_shape],
            [VMEM] * count + [HBM] * len(placed),
            [HBM] * 2 + [VMEM],
            [dma((len(keys) * len(slots) * (1 + chunks),))],
            *arrays.values(),
            *after,
            *placed,
            aliases={count: 0, count + 1: 1} if placed else {},
        )

    placed = []
    for slots, arrays in bundles:
        *placed, token = place(slots, arrays, placed, token)
    last = spread_low(bundle([far_third], token))
    recast_embed, token = call(
        functools.partial(place_embed_kernel, [3]),
        "place_embed",
        [embed_shape, token_shape],
        [VMEM] * 2 + [HBM],
        [HBM, VMEM],
        [dma((1,))],
        pick(embed_end, embed_last),
        last[0],
        recast_embed,
        aliases={2: 0},
    )
    recast_down, recast_up, _ = place([(3, top)], last, placed, token)

    return (
        recast_up.reshape(-1, half_cols),
        recast_down.reshape(-1, width),
        recast_embed.reshape(-1, width),
        norm_cast,
        stored_up,
        velocity_up,
        stored_down[None],
        velocity_down[None],
        stored_rows[None],
        velocity_rows.T[None],
        stored_norm,
        velocity_norm,
    )


def solution(mesh):
    in_specs = (
        P("replica", None, "tensor"),
        P("replica", "tensor", None),
        P("replica", ("shard", "tensor"), None),
        P("replica", None, None),
        P(("replica", "shard", "tensor"), None),
        P(("replica", "shard", "tensor"), None),
        P("tensor", ("replica", "shard"), None),
        P("tensor", ("replica", "shard"), None),
        P(("shard", "tensor"), "replica", None),
        P(("shard", "tensor"), "replica", None),
        P(),
        P(),
        P(),
    )
    out_specs = (
        P(None, "tensor"),
        P("tensor", None),
        P(("shard", "tensor"), None),
        P(),
        P(("replica", "shard", "tensor"), None),
        P(("replica", "shard", "tensor"), None),
        P("tensor", ("replica", "shard"), None),
        P("tensor", ("replica", "shard"), None),
        P(("shard", "tensor"), "replica", None),
        P(("shard", "tensor"), "replica", None),
        P(),
        P(),
    )
    return jax.shard_map(body, mesh=mesh, in_specs=in_specs, out_specs=out_specs, check_vma=False)
```

```python
import functools

import jax
import jax.numpy as jnp
from jax import lax
from jax.experimental import pallas as pl
from jax.experimental.pallas import tpu as pltpu
from jax.sharding import PartitionSpec as P

F32 = jnp.float32
BF16 = jnp.bfloat16
HIGHEST = lax.Precision.HIGHEST
HBM = pl.BlockSpec(memory_space=pltpu.HBM)
ANY = pl.BlockSpec(memory_space=pl.ANY)
VMEM = pl.BlockSpec(memory_space=pltpu.VMEM)


def outer_step(master, moment, summed, groups):
    difference = master - summed / groups
    velocity = 0.5 * moment + difference
    return (master - 0.7 * (difference + 0.5 * velocity), velocity)


def call(kernel, name, out_shape, in_specs, out_specs, scratch, *operands, limit=24, aliases={}):
    size = sum(x.size * x.dtype.itemsize for x in jax.tree.leaves(out_shape))
    return pl.pallas_call(
        kernel,
        name=name,
        out_shape=out_shape,
        in_specs=in_specs,
        out_specs=out_specs,
        scratch_shapes=scratch,
        input_output_aliases=aliases,
        compiler_params=pltpu.CompilerParams(vmem_limit_bytes=limit * 2**20),
        cost_estimate=pl.CostEstimate(flops=0, bytes_accessed=3 * size, transcendentals=0),
    )(*operands)


OUTER = (0, 3)
INWARD = ((0, 1), (3, 2))
ACROSS = ((1, 2), (2, 1))
OUTWARD = ((1, 0), (2, 3))
ENDS = ((0, 3), (3, 0))


def owners():
    pos = lax.axis_index("replica")
    low = pos < 2
    middle, end = jnp.where(low, 2, 1), jnp.where(low, 3, 0)
    return pos, jnp.bitwise_xor(pos, 1), middle, end, 3 - pos, jnp.bitwise_xor(3 - pos, 1)


def along(x, pairs):
    return lax.ppermute(x, "replica", pairs)


def swap(x, axis, bit):
    return lax.ppermute(x, axis, [(i, i ^ bit) for i in range(lax.axis_size(axis))])


def bits_down(size):
    bit = size // 2
    while bit:
        yield bit
        bit //= 2


def prepare_kernel(n_slots, trained, basis, norm, down, up, *refs):
    blocks, (own, *outs, projected, sems) = refs[:n_slots], refs[n_slots:]
    shard = lax.axis_index("shard")
    height, width = down.shape[2:]
    tall, cols = up.shape[2:]
    copies = []

    def bring(source, dest):
        copies.append(pltpu.make_async_copy(source, dest, sems.at[len(copies)]))
        copies[-1].start()

    for owner, block in reversed(list(zip(owners(), blocks))):
        bring(down.at[owner, shard], block.at[pl.ds(0, height)])
        for chunk in range(cols // width):
            bring(
                up.at[owner, shard, :, pl.ds(chunk * width, width)],
                block.at[pl.ds(height + chunk * tall, tall)],
            )

    rank, rows = basis.shape[0], own.shape[1]
    high = basis[...].astype(BF16)
    rest = basis[...] - high.astype(F32)
    middle = rest.astype(BF16)
    low = (rest - middle.astype(F32)).astype(BF16)
    split = jnp.concatenate([high, middle, low], axis=0)
    product = lax.dot_general(
        split, trained[...], (((1,), (1,)), ((), ())), preferred_element_type=F32
    )
    projected[...] = product[:rank] + (product[rank : 2 * rank] + product[2 * rank :])
    pos = lax.axis_index("replica")
    values = norm[...].astype(F32)
    per = norm.shape[1] // rows
    extra = outs[0].shape[0] - rank
    parts = [
        values[i // per : i // per + 1, (i % per) * rows : (i % per + 1) * rows]
        for i in range(norm.shape[0] * per)
    ]
    parts = jnp.concatenate((parts * extra)[:extra], axis=0).astype(BF16)
    own[...] = projected[:, pl.ds(pl.multiple_of(pos * rows, rows), rows)]
    for mask, out in enumerate(outs, 1):
        owner = jnp.bitwise_xor(pos, mask)
        block = projected[:, pl.ds(pl.multiple_of(owner * rows, rows), rows)]
        out[:rank, :] = block.astype(BF16)
        out[rank:, :] = parts
    for copy in copies:
        copy.wait()


def embed_kernel(groups, n_came, *refs):
    refs = list(refs)
    own, base, master, moment, basis, norm, master_norm, moment_norm = refs[:8]
    came = refs[8 : 8 + n_came]
    stored, recast, velocity, norm_cast, norm_stored, norm_velocity = refs[-6:]
    rank, rows = own.shape
    total = own[...]
    for ref in came:
        total = total + ref[:rank, :].astype(F32)
    coefficient = base[...] - total / groups
    moved = 0.5 * moment[...] + coefficient
    velocity[...] = moved
    change = lax.dot_general(
        coefficient + 0.5 * moved,
        basis[...],
        (((0,), (0,)), ((), ())),
        precision=HIGHEST,
        preferred_element_type=F32,
    )
    new = master[...] - 0.7 * change
    stored[...] = new
    recast[...] = new.astype(BF16)
    per = norm.shape[1] // rows
    values = norm[...].astype(F32)
    tails = [ref[rank:, :].astype(F32) for ref in came]
    for i in range(norm.shape[0] * per):
        row, span = i // per, slice((i % per) * rows, (i % per + 1) * rows)
        summed = values[row : row + 1, span]
        for tail in tails:
            summed = summed + tail[i : i + 1, :]
        new_norm, moved_norm = outer_step(
            master_norm[row : row + 1, span], moment_norm[row : row + 1, span], summed, groups
        )
        norm_stored[row : row + 1, span] = new_norm
        norm_velocity[row : row + 1, span] = moved_norm
    norm_cast[...] = norm_stored[...].astype(BF16)


def add_kernel(block, came, *refs):
    refs[-1][...] = (block[...].astype(F32) + came[...].astype(F32)).astype(BF16)


def add(block, came, *after):
    return call(
        add_kernel,
        "add_block",
        jax.ShapeDtypeStruct(block.shape, BF16),
        [VMEM] * 2 + [ANY] * len(after),
        VMEM,
        [],
        block,
        came,
        *after,
    )


def pick_kernel(middle, end, *refs):
    out = refs[-1]
    pos = lax.axis_index("replica")
    outer = jnp.logical_or(pos == OUTER[0], pos == OUTER[1])

    @pl.when(outer)
    def _():
        out[...] = end[...]

    @pl.when(jnp.logical_not(outer))
    def _():
        out[...] = middle[...]


def pick(middle, end, *after):
    specs = [VMEM] * 2 + [ANY] * len(after)
    shape = jax.ShapeDtypeStruct(end.shape, end.dtype)
    return call(pick_kernel, "pick", shape, specs, VMEM, [], middle, end, *after)


def update_kernel(groups, tensors, n_came, *refs):
    refs = list(refs)
    master_down, moment_down, master_up, moment_up = refs[:4]
    came, state_came = refs[4 : 4 + n_came], refs[4 + n_came : 3 + n_came + tensors]
    piece, stored_down, velocity_down, *sums = refs[3 + n_came + tensors : -3]
    summed, master, moment = refs[-3:]
    me = lax.axis_index("tensor")
    rows_down, width = master_down.shape
    rows_up = master_up.shape[0]
    tall, cols = summed.shape

    def at(index):
        return pl.ds(pl.multiple_of(index * rows_up, rows_up), rows_up)

    own_cols = pl.ds(pl.multiple_of(me * cols, cols), cols)
    master[at(me), :] = master_up[:, own_cols]
    moment[at(me), :] = moment_up[:, own_cols]
    for shift in range(1, tensors):
        source = lax.rem(me + tensors - shift, tensors)
        master[at(source), :] = state_came[shift - 1][0]
        moment[at(source), :] = state_came[shift - 1][1]

    def total(lo, hi):
        value = came[0][lo:hi, :].astype(F32)
        for ref in came[1:]:
            value = value + ref[lo:hi, :].astype(F32)
        return value

    stored, velocity = outer_step(
        master_down[...], moment_down[...], total(0, rows_down), groups
    )
    stored_down[...] = stored
    velocity_down[...] = velocity
    piece[:rows_down, :] = stored.astype(BF16)
    for chunk in range(cols // width):
        lo = rows_down + chunk * tall
        part = total(lo, lo + tall)
        span = slice(chunk * width, (chunk + 1) * width)
        summed[:, span] = part
        stored, _ = outer_step(master[:, span], moment[:, span], part, groups)
        piece[lo : lo + tall, :] = stored.astype(BF16)
    for shift in range(tensors):
        sums[shift][...] = summed[at(lax.rem(me + shift, tensors)), :]


def up_kernel(groups, tensors, master_up, moment_up, *refs):
    sums, (stored_up, velocity_up, token) = refs[:tensors], refs[-3:]
    cols = sums[0].shape[1]
    me = lax.axis_index("tensor")
    for shift in range(tensors):
        source = lax.rem(me + tensors - shift, tensors)
        span = pl.ds(pl.multiple_of(source * cols, cols), cols)
        stored, velocity = outer_step(
            master_up[:, span], moment_up[:, span], sums[shift][...], groups
        )
        stored_up[:, span] = stored
        velocity_up[:, span] = velocity
    token[...] = jnp.zeros_like(token)


def state_kernel(tensors, master_up, moment_up, *outs):
    me = lax.axis_index("tensor")
    cols = outs[0].shape[2]
    for shift in range(1, tensors):
        target = lax.rem(me + shift, tensors)
        span = pl.ds(pl.multiple_of(target * cols, cols), cols)
        outs[shift - 1][0] = master_up[:, span]
        outs[shift - 1][1] = moment_up[:, span]


def gate_kernel(x, *refs):
    refs[-1][...] = x[...]


def gate(x, *after):
    return call(
        gate_kernel,
        "gate",
        jax.ShapeDtypeStruct(x.shape, x.dtype),
        [VMEM] + [ANY] * len(after),
        VMEM,
        [],
        x,
        *after,
    )


def stack_kernel(count, *refs):
    for i in range(count):
        refs[-1][i] = refs[i][...]


def bundle(pieces, *after):
    return call(
        functools.partial(stack_kernel, len(pieces)),
        "bundle",
        jax.ShapeDtypeStruct((len(pieces),) + pieces[0].shape, BF16),
        [VMEM] * len(pieces) + [ANY] * len(after),
        VMEM,
        [],
        *pieces,
        *after,
    )


def place_kernel(keys, *refs):
    bundles, (down, up, token, sems) = refs[: len(keys)], refs[-4:]
    token[...] = jnp.zeros_like(token)
    shard = lax.axis_index("shard")
    rows, width = down.shape[2:]
    tall, cols = up.shape[2:]
    copies = []

    def send(source, dest):
        copies.append(pltpu.make_async_copy(source, dest, sems.at[len(copies)]))
        copies[-1].start()

    for pieces, (low, slots) in zip(bundles, keys):
        for i, (slot, mask) in enumerate(slots):
            owner, place = owners()[slot], jnp.bitwise_xor(shard, mask ^ low)
            send(pieces.at[i, pl.ds(0, rows)], down.at[owner, place])
            for chunk in range(cols // width):
                send(
                    pieces.at[i, pl.ds(rows + chunk * tall, tall)],
                    up.at[owner, place, :, pl.ds(chunk * width, width)],
                )
    for copy in copies:
        copy.wait()


def place_embed_kernel(slots, *refs):
    pieces, (out, token, sems) = refs[: len(slots)], refs[-3:]
    token[...] = jnp.zeros_like(token)
    copies = [
        pltpu.make_async_copy(piece, out.at[owners()[slot]], sems.at[i])
        for i, (piece, slot) in enumerate(zip(pieces, slots))
    ]
    for copy in copies:
        copy.start()
    for copy in copies:
        copy.wait()


def spread_low(x):
    found = {0: x}
    for bit in bits_down(lax.axis_size("shard") // 2):
        found.update({mask ^ bit: swap(y, "shard", bit) for mask, y in list(found.items())})
    return found


def body(
    trained_up,
    trained_down,
    trained_embed,
    trained_norm,
    master_up,
    moment_up,
    master_down,
    moment_down,
    master_embed,
    moment_embed,
    master_norm,
    moment_norm,
    embed_basis,
):
    replicas = lax.axis_size("replica")
    shards = lax.axis_size("shard")
    tensors = lax.axis_size("tensor")
    width, rank = embed_basis.shape
    rows_up, half_cols = master_up.shape[0], trained_up.shape[2]
    rows_down, rows_embed = master_down.shape[1], master_embed.shape[1]
    tall = tensors * rows_up
    chunks = half_cols // width
    packed = jax.ShapeDtypeStruct((rows_down + chunks * tall, width), BF16)
    dma = pltpu.SemaphoreType.DMA

    basis_t = embed_basis.T
    rank_rows = jax.ShapeDtypeStruct((rank, rows_embed), F32)
    packet = jax.ShapeDtypeStruct((rank + 16, rows_embed), BF16)
    token_shape = jax.ShapeDtypeStruct((8, 128), F32)
    down = trained_down[0].reshape(replicas, shards, rows_down, width)
    up = trained_up[0].reshape(replicas, shards, tall, half_cols)
    own, near, middle, end, own_rows, *packets = call(
        functools.partial(prepare_kernel, replicas),
        "prepare",
        [packed] * replicas + [rank_rows] + [packet] * (replicas - 1),
        [VMEM] * 3 + [HBM] * 2,
        [VMEM] * (2 * replicas),
        [
            pltpu.VMEM((rank, replicas * rows_embed), F32),
            dma((replicas * (1 + chunks),)),
        ],
        *[
            pltpu.with_memory_space_constraint(x, pltpu.HBM)
            for x in (trained_embed[0], basis_t, trained_norm[0], down, up)
        ],
    )

    packets_came = [swap(packets[0], "replica", 1), swap(packets[1], "replica", 2)]
    end = gate(end, packets_came[0])
    packets_came.append(swap(gate(packets[2], end), "replica", 3))
    end_across = along(end, ACROSS)
    middle_in = along(middle, INWARD)
    end_direct = along(end, ENDS)
    near_in = along(near, INWARD)

    state = jax.ShapeDtypeStruct((2, rows_up, half_cols), F32)
    states = call(
        functools.partial(state_kernel, tensors),
        "up_state",
        [state] * (tensors - 1),
        [VMEM] * 2,
        [VMEM] * (tensors - 1),
        [],
        master_up,
        moment_up,
    )
    states = [
        lax.ppermute(x, "tensor", [(i, (i + shift) % tensors) for i in range(tensors)])
        for shift, x in enumerate(states, 1)
    ]

    base = lax.dot_general(
        basis_t, master_embed[0], (((1,), (1,)), ((), ())), precision=HIGHEST
    )
    norm_state = jax.ShapeDtypeStruct(master_norm.shape, F32)
    embed_rows = jax.ShapeDtypeStruct((rows_embed, width), BF16)
    stored_rows, recast_rows, velocity_rows, norm_cast, stored_norm, velocity_norm = call(
        functools.partial(embed_kernel, replicas, replicas - 1),
        "embed_update",
        [
            jax.ShapeDtypeStruct((rows_embed, width), F32),
            embed_rows,
            rank_rows,
            jax.ShapeDtypeStruct(master_norm.shape, BF16),
            norm_state,
            norm_state,
        ],
        [VMEM] * (7 + replicas),
        [VMEM] * 6,
        [],
        own_rows,
        base,
        master_embed[0],
        moment_embed[0].T,
        basis_t,
        trained_norm[0],
        master_norm,
        moment_norm,
        *packets_came,
    )

    embed_out = along(recast_rows, OUTWARD)
    middle_across = along(add(middle, middle_in), ACROSS)
    near_sum = add(near, end_across, embed_out, end_direct)
    near_out = along(near_sum, OUTWARD)
    embed_middle = along(gate(recast_rows, near_sum), ACROSS)
    came0 = [own, near_in, end_direct, middle_across, near_out]
    half_sum = jax.ShapeDtypeStruct((rows_up, half_cols), F32)
    down_state = jax.ShapeDtypeStruct((rows_down, width), F32)
    piece, stored_down, velocity_down, *sums = call(
        functools.partial(update_kernel, replicas, tensors, len(came0)),
        "update_rows",
        [packed, down_state, down_state] + [half_sum] * tensors,
        [VMEM] * (4 + len(came0) + len(states)),
        [VMEM] * (3 + tensors),
        [pltpu.VMEM((tall, half_cols), F32)] * 3,
        master_down[0],
        moment_down[0],
        master_up,
        moment_up,
        *came0,
        *states,
    )

    top = shards // 2
    near_piece = swap(piece, "replica", 1)
    middle_piece = along(piece, ACROSS)
    end_piece = along(piece, ENDS)
    far_piece = swap(piece, "shard", top)
    embed_in = along(gate(recast_rows, piece), INWARD)
    middle_out = along(middle_piece, OUTWARD)
    near_across = along(near_piece, ACROSS)
    far_near = swap(gate(near_piece, far_piece), "shard", top)
    second = pick(middle_piece, end_piece, far_near, embed_middle)
    far_second = swap(second, "shard", top)
    embed_end = along(embed_in, ACROSS)
    embed_middle_out = along(embed_middle, OUTWARD)
    sums = [sums[0]] + [
        lax.ppermute(
            gate(x, near_piece), "tensor", [(i, (i + shift) % tensors) for i in range(tensors)]
        )
        for shift, x in enumerate(sums[1:], 1)
    ]
    third = pick(near_across, middle_out, far_second, embed_in, *sums[1:])
    far_third = swap(third, "shard", top)
    embed_last = along(embed_end, OUTWARD)
    bundles = [
        (
            [(0, 0), (0, top), (1, 0), (1, top)],
            spread_low(bundle([piece, far_piece, near_piece, far_near], third)),
        ),
        (
            [(4, 0), (4, top), (5, 0)],
            spread_low(bundle([second, far_second, third])),
        ),
    ]

    stored_up, velocity_up, token = call(
        functools.partial(up_kernel, replicas, tensors),
        "update_up",
        [jax.ShapeDtypeStruct(master_up.shape, F32)] * 2 + [token_shape],
        [VMEM] * (2 + tensors) + [ANY],
        [VMEM] * 3,
        [],
        master_up,
        moment_up,
        *sums,
        list(bundles[0][1].values())[-1],
    )

    embed_shape = jax.ShapeDtypeStruct((replicas, rows_embed, width), BF16)
    recast_embed, token = call(
        functools.partial(place_embed_kernel, [0, 1, 2]),
        "place_embed",
        [embed_shape, token_shape],
        [VMEM] * 4,
        [HBM, VMEM],
        [dma((3,))],
        recast_rows,
        pick(embed_in, embed_out),
        pick(embed_middle, embed_middle_out),
        token,
    )

    shapes = [jax.ShapeDtypeStruct(down.shape, BF16), jax.ShapeDtypeStruct(up.shape, BF16)]

    def place(slots, arrays, placed, *after):
        keys = [(low, slots) for low in arrays]
        count = len(keys) + len(after)
        return call(
            functools.partial(place_kernel, keys),
            "place_rows",
            shapes + [token_shape],
            [VMEM] * count + [HBM] * len(placed),
            [HBM] * 2 + [VMEM],
            [dma((len(keys) * len(slots) * (1 + chunks),))],
            *arrays.values(),
            *after,
            *placed,
            aliases={count: 0, count + 1: 1} if placed else {},
        )

    placed = []
    for slots, arrays in bundles:
        *placed, token = place(slots, arrays, placed, token)
    last = spread_low(bundle([far_third], token))
    recast_embed, token = call(
        functools.partial(place_embed_kernel, [3]),
        "place_embed",
        [embed_shape, token_shape],
        [VMEM] * 2 + [HBM],
        [HBM, VMEM],
        [dma((1,))],
        pick(embed_end, embed_last),
        last[0],
        recast_embed,
        aliases={2: 0},
    )
    recast_down, recast_up, _ = place([(5, top)], last, placed, token)

    return (
        recast_up.reshape(-1, half_cols),
        recast_down.reshape(-1, width),
        recast_embed.reshape(-1, width),
        norm_cast,
        stored_up,
        velocity_up,
        stored_down[None],
        velocity_down[None],
        stored_rows[None],
        velocity_rows.T[None],
        stored_norm,
        velocity_norm,
    )


def solution(mesh):
    in_specs = (
        P("replica", None, "tensor"),
        P("replica", "tensor", None),
        P("replica", ("shard", "tensor"), None),
        P("replica", None, None),
        P(("replica", "shard", "tensor"), None),
        P(("replica", "shard", "tensor"), None),
        P("tensor", ("replica", "shard"), None),
        P("tensor", ("replica", "shard"), None),
        P(("shard", "tensor"), "replica", None),
        P(("shard", "tensor"), "replica", None),
        P(),
        P(),
        P(),
    )
    out_specs = (
        P(None, "tensor"),
        P("tensor", None),
        P(("shard", "tensor"), None),
        P(),
        P(("replica", "shard", "tensor"), None),
        P(("replica", "shard", "tensor"), None),
        P("tensor", ("replica", "shard"), None),
        P("tensor", ("replica", "shard"), None),
        P(("shard", "tensor"), "replica", None),
        P(("shard", "tensor"), "replica", None),
        P(),
        P(),
    )
    return jax.shard_map(body, mesh=mesh, in_specs=in_specs, out_specs=out_specs, check_vma=False)
```

```python
import functools

import jax
import jax.numpy as jnp
from jax import lax
from jax.experimental import pallas as pl
from jax.experimental.pallas import tpu as pltpu
from jax.sharding import PartitionSpec as P

F32 = jnp.float32
BF16 = jnp.bfloat16
HIGHEST = lax.Precision.HIGHEST
HBM = pl.BlockSpec(memory_space=pltpu.HBM)
ANY = pl.BlockSpec(memory_space=pl.ANY)
VMEM = pl.BlockSpec(memory_space=pltpu.VMEM)


def outer_step(master, moment, summed, groups):
    difference = master - summed / groups
    velocity = 0.5 * moment + difference
    return (master - 0.7 * (difference + 0.5 * velocity), velocity)


def call(kernel, name, out_shape, in_specs, out_specs, scratch, *operands, limit=24, aliases={}):
    size = sum(x.size * x.dtype.itemsize for x in jax.tree.leaves(out_shape))
    return pl.pallas_call(
        kernel,
        name=name,
        out_shape=out_shape,
        in_specs=in_specs,
        out_specs=out_specs,
        scratch_shapes=scratch,
        input_output_aliases=aliases,
        compiler_params=pltpu.CompilerParams(vmem_limit_bytes=limit * 2**20),
        cost_estimate=pl.CostEstimate(flops=0, bytes_accessed=3 * size, transcendentals=0),
    )(*operands)


OUTER = (0, 3)
INWARD = ((0, 1), (3, 2))
ACROSS = ((1, 2), (2, 1))
OUTWARD = ((1, 0), (2, 3))


def owners():
    pos = lax.axis_index("replica")
    low = pos < 2
    return pos, jnp.bitwise_xor(pos, 1), jnp.where(low, 2, 1), jnp.where(low, 3, 0)


def along(x, pairs):
    return lax.ppermute(x, "replica", pairs)


def swap(x, axis, bit):
    return lax.ppermute(x, axis, [(i, i ^ bit) for i in range(lax.axis_size(axis))])


def bits_down(size):
    bit = size // 2
    while bit:
        yield bit
        bit //= 2


def project_kernel(trained, basis, norm, own, *refs):
    *outs, projected = refs
    rank, rows = basis.shape[0], own.shape[1]
    high = basis[...].astype(BF16)
    rest = basis[...] - high.astype(F32)
    middle = rest.astype(BF16)
    low = (rest - middle.astype(F32)).astype(BF16)
    split = jnp.concatenate([high, middle, low], axis=0)
    product = lax.dot_general(
        split, trained[...], (((1,), (1,)), ((), ())), preferred_element_type=F32
    )
    projected[...] = product[:rank] + (product[rank : 2 * rank] + product[2 * rank :])
    pos = lax.axis_index("replica")
    values = norm[...].astype(F32)
    per = norm.shape[1] // rows
    extra = outs[0].shape[0] - rank
    parts = [
        values[i // per : i // per + 1, (i % per) * rows : (i % per + 1) * rows]
        for i in range(norm.shape[0] * per)
    ]
    parts = jnp.concatenate((parts * extra)[:extra], axis=0).astype(BF16)
    own[...] = projected[:, pl.ds(pl.multiple_of(pos * rows, rows), rows)]
    for mask, out in enumerate(outs, 1):
        owner = jnp.bitwise_xor(pos, mask)
        block = projected[:, pl.ds(pl.multiple_of(owner * rows, rows), rows)]
        out[:rank, :] = block.astype(BF16)
        out[rank:, :] = parts


def embed_kernel(groups, n_came, *refs):
    refs = list(refs)
    own, base, master, moment, basis, norm, master_norm, moment_norm = refs[:8]
    came = refs[8 : 8 + n_came]
    stored, recast, velocity, norm_cast, norm_stored, norm_velocity = refs[-6:]
    rank, rows = own.shape
    total = own[...]
    for ref in came:
        total = total + ref[:rank, :].astype(F32)
    coefficient = base[...] - total / groups
    moved = 0.5 * moment[...] + coefficient
    velocity[...] = moved
    change = lax.dot_general(
        coefficient + 0.5 * moved,
        basis[...],
        (((0,), (0,)), ((), ())),
        precision=HIGHEST,
        preferred_element_type=F32,
    )
    new = master[...] - 0.7 * change
    stored[...] = new
    recast[...] = new.astype(BF16)
    per = norm.shape[1] // rows
    values = norm[...].astype(F32)
    tails = [ref[rank:, :].astype(F32) for ref in came]
    for i in range(norm.shape[0] * per):
        row, span = i // per, slice((i % per) * rows, (i % per + 1) * rows)
        summed = values[row : row + 1, span]
        for tail in tails:
            summed = summed + tail[i : i + 1, :]
        new_norm, moved_norm = outer_step(
            master_norm[row : row + 1, span], moment_norm[row : row + 1, span], summed, groups
        )
        norm_stored[row : row + 1, span] = new_norm
        norm_velocity[row : row + 1, span] = moved_norm
    norm_cast[...] = norm_stored[...].astype(BF16)


def pack_kernel(down, up, *refs):
    *outs, sems = refs
    shard = lax.axis_index("shard")
    rows, width = down.shape[2:]
    tall, cols = up.shape[2:]
    copies = []

    def bring(source, dest):
        copies.append(pltpu.make_async_copy(source, dest, sems.at[len(copies)]))
        copies[-1].start()

    for owner, out in reversed(list(zip(owners(), outs))):
        bring(down.at[owner, shard], out.at[pl.ds(0, rows)])
        for chunk in range(cols // width):
            bring(
                up.at[owner, shard, :, pl.ds(chunk * width, width)],
                out.at[pl.ds(rows + chunk * tall, tall)],
            )
    for copy in copies:
        copy.wait()


def add_kernel(block, came, *refs):
    refs[-1][...] = (block[...].astype(F32) + came[...].astype(F32)).astype(BF16)


def add(block, came, *after):
    return call(
        add_kernel,
        "add_block",
        jax.ShapeDtypeStruct(block.shape, BF16),
        [VMEM] * 2 + [ANY] * len(after),
        VMEM,
        [],
        block,
        came,
        *after,
    )


def pick_kernel(middle, end, *refs):
    out = refs[-1]
    pos = lax.axis_index("replica")
    outer = jnp.logical_or(pos == OUTER[0], pos == OUTER[1])

    @pl.when(outer)
    def _():
        out[...] = end[...]

    @pl.when(jnp.logical_not(outer))
    def _():
        out[...] = middle[...]


def pick(middle, end, *after):
    specs = [VMEM] * 2 + [ANY] * len(after)
    shape = jax.ShapeDtypeStruct(end.shape, end.dtype)
    return call(pick_kernel, "pick", shape, specs, VMEM, [], middle, end, *after)


def update_kernel(groups, tensors, n_came, *refs):
    refs = list(refs)
    master_down, moment_down, master_up, moment_up = refs[:4]
    came, state_came = refs[4 : 4 + n_came], refs[4 + n_came : 3 + n_came + tensors]
    piece, stored_down, velocity_down, *sums = refs[3 + n_came + tensors : -3]
    summed, master, moment = refs[-3:]
    me = lax.axis_index("tensor")
    rows_down, width = master_down.shape
    rows_up = master_up.shape[0]
    tall, cols = summed.shape

    def at(index):
        return pl.ds(pl.multiple_of(index * rows_up, rows_up), rows_up)

    own_cols = pl.ds(pl.multiple_of(me * cols, cols), cols)
    master[at(me), :] = master_up[:, own_cols]
    moment[at(me), :] = moment_up[:, own_cols]
    for shift in range(1, tensors):
        source = lax.rem(me + tensors - shift, tensors)
        master[at(source), :] = state_came[shift - 1][0]
        moment[at(source), :] = state_came[shift - 1][1]

    def total(lo, hi):
        value = came[0][lo:hi, :].astype(F32)
        for ref in came[1:]:
            value = value + ref[lo:hi, :].astype(F32)
        return value

    stored, velocity = outer_step(
        master_down[...], moment_down[...], total(0, rows_down), groups
    )
    stored_down[...] = stored
    velocity_down[...] = velocity
    piece[:rows_down, :] = stored.astype(BF16)
    for chunk in range(cols // width):
        lo = rows_down + chunk * tall
        part = total(lo, lo + tall)
        span = slice(chunk * width, (chunk + 1) * width)
        summed[:, span] = part
        stored, _ = outer_step(master[:, span], moment[:, span], part, groups)
        piece[lo : lo + tall, :] = stored.astype(BF16)
    for shift in range(tensors):
        sums[shift][...] = summed[at(lax.rem(me + shift, tensors)), :]


def up_kernel(groups, tensors, master_up, moment_up, *refs):
    sums, (stored_up, velocity_up, token) = refs[:tensors], refs[-3:]
    cols = sums[0].shape[1]
    me = lax.axis_index("tensor")
    for shift in range(tensors):
        source = lax.rem(me + tensors - shift, tensors)
        span = pl.ds(pl.multiple_of(source * cols, cols), cols)
        stored, velocity = outer_step(
            master_up[:, span], moment_up[:, span], sums[shift][...], groups
        )
        stored_up[:, span] = stored
        velocity_up[:, span] = velocity
    token[...] = jnp.zeros_like(token)


def state_kernel(tensors, master_up, moment_up, *outs):
    me = lax.axis_index("tensor")
    cols = outs[0].shape[2]
    for shift in range(1, tensors):
        target = lax.rem(me + shift, tensors)
        span = pl.ds(pl.multiple_of(target * cols, cols), cols)
        outs[shift - 1][0] = master_up[:, span]
        outs[shift - 1][1] = moment_up[:, span]


def gate_kernel(x, *refs):
    refs[-1][...] = x[...]


def gate(x, *after):
    return call(
        gate_kernel,
        "gate",
        jax.ShapeDtypeStruct(x.shape, x.dtype),
        [VMEM] + [ANY] * len(after),
        VMEM,
        [],
        x,
        *after,
    )


def join_kernel(top, bottom, out):
    rows = top.shape[0]
    out[:rows, :] = top[...]
    out[rows:, :] = bottom[...]


def join(top, bottom):
    shape = jax.ShapeDtypeStruct((top.shape[0] + bottom.shape[0], top.shape[1]), BF16)
    return call(join_kernel, "join", shape, [VMEM] * 2, VMEM, [], top, bottom)


def tail_kernel(x, *refs):
    out = refs[-1]
    out[...] = x[x.shape[0] - out.shape[0] :, :]


def tail(x, rows, *after):
    shape = jax.ShapeDtypeStruct((rows, x.shape[1]), x.dtype)
    specs = [VMEM] + [ANY] * len(after)
    return call(tail_kernel, "tail", shape, specs, VMEM, [], x, *after)


def stack_kernel(count, *refs):
    for i in range(count):
        refs[-1][i] = refs[i][...]


def bundle(pieces, *after):
    return call(
        functools.partial(stack_kernel, len(pieces)),
        "bundle",
        jax.ShapeDtypeStruct((len(pieces),) + pieces[0].shape, BF16),
        [VMEM] * len(pieces) + [ANY] * len(after),
        VMEM,
        [],
        *pieces,
        *after,
    )


def place_kernel(keys, *refs):
    bundles, (down, up, token, sems) = refs[: len(keys)], refs[-4:]
    token[...] = jnp.zeros_like(token)
    shard = lax.axis_index("shard")
    rows, width = down.shape[2:]
    tall, cols = up.shape[2:]
    copies = []

    def send(source, dest):
        copies.append(pltpu.make_async_copy(source, dest, sems.at[len(copies)]))
        copies[-1].start()

    for pieces, (low, slots) in zip(bundles, keys):
        for i, (slot, mask) in enumerate(slots):
            owner, place = owners()[slot], jnp.bitwise_xor(shard, mask ^ low)
            send(pieces.at[i, pl.ds(0, rows)], down.at[owner, place])
            for chunk in range(cols // width):
                send(
                    pieces.at[i, pl.ds(rows + chunk * tall, tall)],
                    up.at[owner, place, :, pl.ds(chunk * width, width)],
                )
    for copy in copies:
        copy.wait()


def place_embed_kernel(slots, *refs):
    pieces, (out, token, sems) = refs[: len(slots)], refs[-3:]
    token[...] = jnp.zeros_like(token)
    copies = [
        pltpu.make_async_copy(piece, out.at[owners()[slot]], sems.at[i])
        for i, (piece, slot) in enumerate(zip(pieces, slots))
    ]
    for copy in copies:
        copy.start()
    for copy in copies:
        copy.wait()


def spread_low(x):
    found = {0: x}
    for bit in bits_down(lax.axis_size("shard") // 2):
        found.update({mask ^ bit: swap(y, "shard", bit) for mask, y in list(found.items())})
    return found


def body(
    trained_up,
    trained_down,
    trained_embed,
    trained_norm,
    master_up,
    moment_up,
    master_down,
    moment_down,
    master_embed,
    moment_embed,
    master_norm,
    moment_norm,
    embed_basis,
):
    replicas = lax.axis_size("replica")
    shards = lax.axis_size("shard")
    tensors = lax.axis_size("tensor")
    width, rank = embed_basis.shape
    rows_up, half_cols = master_up.shape[0], trained_up.shape[2]
    rows_down, rows_embed = master_down.shape[1], master_embed.shape[1]
    tall = tensors * rows_up
    chunks = half_cols // width
    packed = jax.ShapeDtypeStruct((rows_down + chunks * tall, width), BF16)
    dma = pltpu.SemaphoreType.DMA

    basis_t = embed_basis.T
    rank_rows = jax.ShapeDtypeStruct((rank, rows_embed), F32)
    packet = jax.ShapeDtypeStruct((rank + 16, rows_embed), BF16)
    token_shape = jax.ShapeDtypeStruct((8, 128), F32)
    own_rows, *packets = call(
        project_kernel,
        "project_rows",
        [rank_rows] + [packet] * (replicas - 1),
        [VMEM] * 3,
        [VMEM] * replicas,
        [pltpu.VMEM((rank, replicas * rows_embed), F32)],
        pltpu.with_memory_space_constraint(trained_embed[0], pltpu.HBM),
        pltpu.with_memory_space_constraint(basis_t, pltpu.HBM),
        pltpu.with_memory_space_constraint(trained_norm[0], pltpu.HBM),
    )
    down = trained_down[0].reshape(replicas, shards, rows_down, width)
    up = trained_up[0].reshape(replicas, shards, tall, half_cols)
    own, near, middle, end = call(
        pack_kernel,
        "pack_blocks",
        [packed] * replicas,
        [HBM] * 2,
        [VMEM] * replicas,
        [dma((replicas * (1 + chunks),))],
        pltpu.with_memory_space_constraint(down, pltpu.HBM),
        pltpu.with_memory_space_constraint(up, pltpu.HBM),
    )
    packets_came = [swap(packets[0], "replica", 1), swap(packets[1], "replica", 2)]
    end = gate(end, packets_came[0])
    packets_came.append(swap(gate(packets[2], end), "replica", 3))
    from_end = [along(end, INWARD)]

    state = jax.ShapeDtypeStruct((2, rows_up, half_cols), F32)
    states = call(
        functools.partial(state_kernel, tensors),
        "up_state",
        [state] * (tensors - 1),
        [VMEM] * 2,
        [VMEM] * (tensors - 1),
        [],
        master_up,
        moment_up,
    )
    states = [
        lax.ppermute(x, "tensor", [(i, (i + shift) % tensors) for i in range(tensors)])
        for shift, x in enumerate(states, 1)
    ]

    base = lax.dot_general(
        basis_t, master_embed[0], (((1,), (1,)), ((), ())), precision=HIGHEST
    )
    norm_state = jax.ShapeDtypeStruct(master_norm.shape, F32)
    embed_rows = jax.ShapeDtypeStruct((rows_embed, width), BF16)
    stored_rows, recast_rows, velocity_rows, norm_cast, stored_norm, velocity_norm = call(
        functools.partial(embed_kernel, replicas, replicas - 1),
        "embed_update",
        [
            jax.ShapeDtypeStruct((rows_embed, width), F32),
            embed_rows,
            rank_rows,
            jax.ShapeDtypeStruct(master_norm.shape, BF16),
            norm_state,
            norm_state,
        ],
        [VMEM] * (7 + replicas),
        [VMEM] * 6,
        [],
        own_rows,
        base,
        master_embed[0],
        moment_embed[0].T,
        basis_t,
        trained_norm[0],
        master_norm,
        moment_norm,
        *packets_came,
    )

    embed_out = along(recast_rows, OUTWARD)
    embed_middle = along(recast_rows, ACROSS)
    end_sum = gate(add(end, from_end[0]), embed_out, embed_middle)
    end_partial = along(end_sum, ACROSS)
    from_end.append(along(middle, INWARD))
    middle_partial = along(add(middle, from_end[1]), ACROSS)
    from_near = along(join(near, recast_rows), INWARD)
    embed_middle_out = along(embed_middle, OUTWARD)
    to_end = along(add(near, end_partial, embed_middle_out), OUTWARD)
    came0 = [own, from_near, middle_partial, to_end]
    half_sum = jax.ShapeDtypeStruct((rows_up, half_cols), F32)
    down_state = jax.ShapeDtypeStruct((rows_down, width), F32)
    piece, stored_down, velocity_down, *sums = call(
        functools.partial(update_kernel, replicas, tensors, len(came0)),
        "update_rows",
        [packed, down_state, down_state] + [half_sum] * tensors,
        [VMEM] * (4 + len(came0) + len(states)),
        [VMEM] * (3 + tensors),
        [pltpu.VMEM((tall, half_cols), F32)] * 3,
        master_down[0],
        moment_down[0],
        master_up,
        moment_up,
        *came0,
        *states,
    )

    top = shards // 2
    came_near = swap(piece, "replica", 1)
    middle_piece = along(piece, ACROSS)
    far_piece = swap(piece, "shard", top)
    end_piece = along(came_near, ACROSS)
    second_out = along(middle_piece, OUTWARD)
    near_piece = gate(came_near, far_piece)
    far_near = swap(near_piece, "shard", top)
    sums = [sums[0]] + [
        lax.ppermute(
            gate(x, near_piece), "tensor", [(i, (i + shift) % tensors) for i in range(tensors)]
        )
        for shift, x in enumerate(sums[1:], 1)
    ]
    second = pick(middle_piece, second_out, far_near)
    far_second = swap(second, "shard", top)
    embed_in = tail(from_near, rows_embed, near_piece)
    embed_end = along(embed_in, ACROSS)
    third = pick(end_piece, along(end_piece, OUTWARD), far_second, embed_end, *sums[1:])
    far_third = swap(third, "shard", top)
    embed_last = along(embed_end, OUTWARD)
    bundles = [
        (
            [(0, 0), (0, top), (1, 0), (1, top)],
            spread_low(bundle([piece, far_piece, near_piece, far_near], third)),
        ),
        (
            [(2, 0), (2, top), (3, 0)],
            spread_low(bundle([second, far_second, third])),
        ),
    ]

    stored_up, velocity_up, token = call(
        functools.partial(up_kernel, replicas, tensors),
        "update_up",
        [jax.ShapeDtypeStruct(master_up.shape, F32)] * 2 + [token_shape],
        [VMEM] * (2 + tensors) + [ANY],
        [VMEM] * 3,
        [],
        master_up,
        moment_up,
        *sums,
        list(bundles[0][1].values())[-1],
    )

    embed_shape = jax.ShapeDtypeStruct((replicas, rows_embed, width), BF16)
    recast_embed, token = call(
        functools.partial(place_embed_kernel, [0, 1, 2]),
        "place_embed",
        [embed_shape, token_shape],
        [VMEM] * 4,
        [HBM, VMEM],
        [dma((3,))],
        recast_rows,
        pick(embed_in, embed_out),
        pick(embed_middle, embed_middle_out),
        token,
    )

    shapes = [jax.ShapeDtypeStruct(down.shape, BF16), jax.ShapeDtypeStruct(up.shape, BF16)]

    def place(slots, arrays, placed, *after):
        keys = [(low, slots) for low in arrays]
        count = len(keys) + len(after)
        return call(
            functools.partial(place_kernel, keys),
            "place_rows",
            shapes + [token_shape],
            [VMEM] * count + [HBM] * len(placed),
            [HBM] * 2 + [VMEM],
            [dma((len(keys) * len(slots) * (1 + chunks),))],
            *arrays.values(),
            *after,
            *placed,
            aliases={count: 0, count + 1: 1} if placed else {},
        )

    placed = []
    for slots, arrays in bundles:
        *placed, token = place(slots, arrays, placed, token)
    last = spread_low(bundle([far_third], token))
    recast_embed, token = call(
        functools.partial(place_embed_kernel, [3]),
        "place_embed",
        [embed_shape, token_shape],
        [VMEM] * 2 + [HBM],
        [HBM, VMEM],
        [dma((1,))],
        pick(embed_end, embed_last),
        last[0],
        recast_embed,
        aliases={2: 0},
    )
    recast_down, recast_up, _ = place([(3, top)], last, placed, token)

    return (
        recast_up.reshape(-1, half_cols),
        recast_down.reshape(-1, width),
        recast_embed.reshape(-1, width),
        norm_cast,
        stored_up,
        velocity_up,
        stored_down[None],
        velocity_down[None],
        stored_rows[None],
        velocity_rows.T[None],
        stored_norm,
        velocity_norm,
    )


def solution(mesh):
    in_specs = (
        P("replica", None, "tensor"),
        P("replica", "tensor", None),
        P("replica", ("shard", "tensor"), None),
        P("replica", None, None),
        P(("replica", "shard", "tensor"), None),
        P(("replica", "shard", "tensor"), None),
        P("tensor", ("replica", "shard"), None),
        P("tensor", ("replica", "shard"), None),
        P(("shard", "tensor"), "replica", None),
        P(("shard", "tensor"), "replica", None),
        P(),
        P(),
        P(),
    )
    out_specs = (
        P(None, "tensor"),
        P("tensor", None),
        P(("shard", "tensor"), None),
        P(),
        P(("replica", "shard", "tensor"), None),
        P(("replica", "shard", "tensor"), None),
        P("tensor", ("replica", "shard"), None),
        P("tensor", ("replica", "shard"), None),
        P(("shard", "tensor"), "replica", None),
        P(("shard", "tensor"), "replica", None),
        P(),
        P(),
    )
    return jax.shard_map(body, mesh=mesh, in_specs=in_specs, out_specs=out_specs, check_vma=False)
```

```python
import functools

import jax
import jax.numpy as jnp
from jax import lax
from jax.experimental import pallas as pl
from jax.experimental.pallas import tpu as pltpu
from jax.sharding import PartitionSpec as P

F32 = jnp.float32
BF16 = jnp.bfloat16
HIGHEST = lax.Precision.HIGHEST
HBM = pl.BlockSpec(memory_space=pltpu.HBM)
ANY = pl.BlockSpec(memory_space=pl.ANY)
VMEM = pl.BlockSpec(memory_space=pltpu.VMEM)


def outer_step(master, moment, summed, groups):
    difference = master - summed / groups
    velocity = 0.5 * moment + difference
    return (master - 0.7 * (difference + 0.5 * velocity), velocity)


def call(kernel, name, out_shape, in_specs, out_specs, scratch, *operands, limit=24, aliases={}):
    size = sum(x.size * x.dtype.itemsize for x in jax.tree.leaves(out_shape))
    return pl.pallas_call(
        kernel,
        name=name,
        out_shape=out_shape,
        in_specs=in_specs,
        out_specs=out_specs,
        scratch_shapes=scratch,
        input_output_aliases=aliases,
        compiler_params=pltpu.CompilerParams(vmem_limit_bytes=limit * 2**20),
        cost_estimate=pl.CostEstimate(flops=0, bytes_accessed=3 * size, transcendentals=0),
    )(*operands)


OUTER = (0, 3)
INWARD = ((0, 1), (3, 2))
ACROSS = ((1, 2), (2, 1))
OUTWARD = ((1, 0), (2, 3))


def owners():
    pos = lax.axis_index("replica")
    low = pos < 2
    return pos, jnp.bitwise_xor(pos, 1), jnp.where(low, 2, 1), jnp.where(low, 3, 0)


def along(x, pairs):
    return lax.ppermute(x, "replica", pairs)


def swap(x, axis, bit):
    return lax.ppermute(x, axis, [(i, i ^ bit) for i in range(lax.axis_size(axis))])


def bits_down(size):
    bit = size // 2
    while bit:
        yield bit
        bit //= 2


def project_kernel(trained, basis, norm, own, *refs):
    *outs, projected = refs
    rank, rows = basis.shape[0], own.shape[1]
    high = basis[...].astype(BF16)
    rest = basis[...] - high.astype(F32)
    middle = rest.astype(BF16)
    low = (rest - middle.astype(F32)).astype(BF16)
    split = jnp.concatenate([high, middle, low], axis=0)
    product = lax.dot_general(
        split, trained[...], (((1,), (1,)), ((), ())), preferred_element_type=F32
    )
    projected[...] = product[:rank] + (product[rank : 2 * rank] + product[2 * rank :])
    pos = lax.axis_index("replica")
    values = norm[...].astype(F32)
    per = norm.shape[1] // rows
    extra = outs[0].shape[0] - rank
    parts = [
        values[i // per : i // per + 1, (i % per) * rows : (i % per + 1) * rows]
        for i in range(norm.shape[0] * per)
    ]
    parts = jnp.concatenate((parts * extra)[:extra], axis=0).astype(BF16)
    own[...] = projected[:, pl.ds(pl.multiple_of(pos * rows, rows), rows)]
    for mask, out in enumerate(outs, 1):
        owner = jnp.bitwise_xor(pos, mask)
        block = projected[:, pl.ds(pl.multiple_of(owner * rows, rows), rows)]
        out[:rank, :] = block.astype(BF16)
        out[rank:, :] = parts


def embed_kernel(groups, n_came, *refs):
    refs = list(refs)
    own, base, master, moment, basis, norm, master_norm, moment_norm = refs[:8]
    came = refs[8 : 8 + n_came]
    stored, recast, velocity, norm_cast, norm_stored, norm_velocity = refs[-6:]
    rank, rows = own.shape
    total = own[...]
    for ref in came:
        total = total + ref[:rank, :].astype(F32)
    coefficient = base[...] - total / groups
    moved = 0.5 * moment[...] + coefficient
    velocity[...] = moved
    change = lax.dot_general(
        coefficient + 0.5 * moved,
        basis[...],
        (((0,), (0,)), ((), ())),
        precision=HIGHEST,
        preferred_element_type=F32,
    )
    new = master[...] - 0.7 * change
    stored[...] = new
    recast[...] = new.astype(BF16)
    per = norm.shape[1] // rows
    values = norm[...].astype(F32)
    tails = [ref[rank:, :].astype(F32) for ref in came]
    for i in range(norm.shape[0] * per):
        row, span = i // per, slice((i % per) * rows, (i % per + 1) * rows)
        summed = values[row : row + 1, span]
        for tail in tails:
            summed = summed + tail[i : i + 1, :]
        new_norm, moved_norm = outer_step(
            master_norm[row : row + 1, span], moment_norm[row : row + 1, span], summed, groups
        )
        norm_stored[row : row + 1, span] = new_norm
        norm_velocity[row : row + 1, span] = moved_norm
    norm_cast[...] = norm_stored[...].astype(BF16)


def pack_kernel(down, up, *refs):
    *outs, sems = refs
    shard = lax.axis_index("shard")
    rows, width = down.shape[2:]
    tall, cols = up.shape[2:]
    copies = []

    def bring(source, dest):
        copies.append(pltpu.make_async_copy(source, dest, sems.at[len(copies)]))
        copies[-1].start()

    for owner, out in reversed(list(zip(owners(), outs))):
        bring(down.at[owner, shard], out.at[pl.ds(0, rows)])
        for chunk in range(cols // width):
            bring(
                up.at[owner, shard, :, pl.ds(chunk * width, width)],
                out.at[pl.ds(rows + chunk * tall, tall)],
            )
    for copy in copies:
        copy.wait()


def add_kernel(block, came, *refs):
    refs[-1][...] = (block[...].astype(F32) + came[...].astype(F32)).astype(BF16)


def add(block, came, *after):
    return call(
        add_kernel,
        "add_block",
        jax.ShapeDtypeStruct(block.shape, BF16),
        [VMEM] * 2 + [ANY] * len(after),
        VMEM,
        [],
        block,
        came,
        *after,
    )


def pick_kernel(middle, end, *refs):
    out = refs[-1]
    pos = lax.axis_index("replica")
    outer = jnp.logical_or(pos == OUTER[0], pos == OUTER[1])

    @pl.when(outer)
    def _():
        out[...] = end[...]

    @pl.when(jnp.logical_not(outer))
    def _():
        out[...] = middle[...]


def pick(middle, end, *after):
    specs = [VMEM] * 2 + [ANY] * len(after)
    shape = jax.ShapeDtypeStruct(end.shape, end.dtype)
    return call(pick_kernel, "pick", shape, specs, VMEM, [], middle, end, *after)


def update_kernel(groups, tensors, n_came, *refs):
    refs = list(refs)
    master_down, moment_down, master_up, moment_up = refs[:4]
    came, state_came = refs[4 : 4 + n_came], refs[4 + n_came : 3 + n_came + tensors]
    piece, stored_down, velocity_down, *sums = refs[3 + n_came + tensors : -3]
    summed, master, moment = refs[-3:]
    me = lax.axis_index("tensor")
    rows_down, width = master_down.shape
    rows_up = master_up.shape[0]
    tall, cols = summed.shape

    def at(index):
        return pl.ds(pl.multiple_of(index * rows_up, rows_up), rows_up)

    own_cols = pl.ds(pl.multiple_of(me * cols, cols), cols)
    master[at(me), :] = master_up[:, own_cols]
    moment[at(me), :] = moment_up[:, own_cols]
    for shift in range(1, tensors):
        source = lax.rem(me + tensors - shift, tensors)
        master[at(source), :] = state_came[shift - 1][0]
        moment[at(source), :] = state_came[shift - 1][1]

    def total(lo, hi):
        value = came[0][lo:hi, :].astype(F32)
        for ref in came[1:]:
            value = value + ref[lo:hi, :].astype(F32)
        return value

    stored, velocity = outer_step(
        master_down[...], moment_down[...], total(0, rows_down), groups
    )
    stored_down[...] = stored
    velocity_down[...] = velocity
    piece[:rows_down, :] = stored.astype(BF16)
    for chunk in range(cols // width):
        lo = rows_down + chunk * tall
        part = total(lo, lo + tall)
        span = slice(chunk * width, (chunk + 1) * width)
        summed[:, span] = part
        stored, _ = outer_step(master[:, span], moment[:, span], part, groups)
        piece[lo : lo + tall, :] = stored.astype(BF16)
    for shift in range(tensors):
        sums[shift][...] = summed[at(lax.rem(me + shift, tensors)), :]


def up_kernel(groups, tensors, master_up, moment_up, *refs):
    sums, (stored_up, velocity_up, token) = refs[:tensors], refs[-3:]
    cols = sums[0].shape[1]
    me = lax.axis_index("tensor")
    for shift in range(tensors):
        source = lax.rem(me + tensors - shift, tensors)
        span = pl.ds(pl.multiple_of(source * cols, cols), cols)
        stored, velocity = outer_step(
            master_up[:, span], moment_up[:, span], sums[shift][...], groups
        )
        stored_up[:, span] = stored
        velocity_up[:, span] = velocity
    token[...] = jnp.zeros_like(token)


def state_kernel(tensors, master_up, moment_up, *outs):
    me = lax.axis_index("tensor")
    cols = outs[0].shape[2]
    for shift in range(1, tensors):
        target = lax.rem(me + shift, tensors)
        span = pl.ds(pl.multiple_of(target * cols, cols), cols)
        outs[shift - 1][0] = master_up[:, span]
        outs[shift - 1][1] = moment_up[:, span]


def gate_kernel(x, *refs):
    refs[-1][...] = x[...]


def gate(x, *after):
    return call(
        gate_kernel,
        "gate",
        jax.ShapeDtypeStruct(x.shape, x.dtype),
        [VMEM] + [ANY] * len(after),
        VMEM,
        [],
        x,
        *after,
    )


def stack_kernel(count, *refs):
    for i in range(count):
        refs[-1][i] = refs[i][...]


def bundle(pieces, *after):
    return call(
        functools.partial(stack_kernel, len(pieces)),
        "bundle",
        jax.ShapeDtypeStruct((len(pieces),) + pieces[0].shape, BF16),
        [VMEM] * len(pieces) + [ANY] * len(after),
        VMEM,
        [],
        *pieces,
        *after,
    )


def place_kernel(keys, *refs):
    bundles, (down, up, token, sems) = refs[: len(keys)], refs[-4:]
    token[...] = jnp.zeros_like(token)
    shard = lax.axis_index("shard")
    rows, width = down.shape[2:]
    tall, cols = up.shape[2:]
    copies = []

    def send(source, dest):
        copies.append(pltpu.make_async_copy(source, dest, sems.at[len(copies)]))
        copies[-1].start()

    for pieces, (low, slots) in zip(bundles, keys):
        for i, (slot, mask) in enumerate(slots):
            owner, place = owners()[slot], jnp.bitwise_xor(shard, mask ^ low)
            send(pieces.at[i, pl.ds(0, rows)], down.at[owner, place])
            for chunk in range(cols // width):
                send(
                    pieces.at[i, pl.ds(rows + chunk * tall, tall)],
                    up.at[owner, place, :, pl.ds(chunk * width, width)],
                )
    for copy in copies:
        copy.wait()


def place_embed_kernel(slots, *refs):
    pieces, (out, token, sems) = refs[: len(slots)], refs[-3:]
    token[...] = jnp.zeros_like(token)
    copies = [
        pltpu.make_async_copy(piece, out.at[owners()[slot]], sems.at[i])
        for i, (piece, slot) in enumerate(zip(pieces, slots))
    ]
    for copy in copies:
        copy.start()
    for copy in copies:
        copy.wait()


def spread_low(x):
    found = {0: x}
    for bit in bits_down(lax.axis_size("shard") // 2):
        found.update({mask ^ bit: swap(y, "shard", bit) for mask, y in list(found.items())})
    return found


def body(
    trained_up,
    trained_down,
    trained_embed,
    trained_norm,
    master_up,
    moment_up,
    master_down,
    moment_down,
    master_embed,
    moment_embed,
    master_norm,
    moment_norm,
    embed_basis,
):
    replicas = lax.axis_size("replica")
    shards = lax.axis_size("shard")
    tensors = lax.axis_size("tensor")
    width, rank = embed_basis.shape
    rows_up, half_cols = master_up.shape[0], trained_up.shape[2]
    rows_down, rows_embed = master_down.shape[1], master_embed.shape[1]
    tall = tensors * rows_up
    chunks = half_cols // width
    packed = jax.ShapeDtypeStruct((rows_down + chunks * tall, width), BF16)
    dma = pltpu.SemaphoreType.DMA

    basis_t = embed_basis.T
    rank_rows = jax.ShapeDtypeStruct((rank, rows_embed), F32)
    packet = jax.ShapeDtypeStruct((rank + 16, rows_embed), BF16)
    token_shape = jax.ShapeDtypeStruct((8, 128), F32)
    own_rows, *packets = call(
        project_kernel,
        "project_rows",
        [rank_rows] + [packet] * (replicas - 1),
        [VMEM] * 3,
        [VMEM] * replicas,
        [pltpu.VMEM((rank, replicas * rows_embed), F32)],
        pltpu.with_memory_space_constraint(trained_embed[0], pltpu.HBM),
        pltpu.with_memory_space_constraint(basis_t, pltpu.HBM),
        pltpu.with_memory_space_constraint(trained_norm[0], pltpu.HBM),
    )
    down = trained_down[0].reshape(replicas, shards, rows_down, width)
    up = trained_up[0].reshape(replicas, shards, tall, half_cols)
    own, near, middle, end = call(
        pack_kernel,
        "pack_blocks",
        [packed] * replicas,
        [HBM] * 2,
        [VMEM] * replicas,
        [dma((replicas * (1 + chunks),))],
        pltpu.with_memory_space_constraint(down, pltpu.HBM),
        pltpu.with_memory_space_constraint(up, pltpu.HBM),
    )
    packets_came = [swap(packets[0], "replica", 1), swap(packets[1], "replica", 2)]
    end = gate(end, packets_came[0])
    packets_came.append(swap(gate(packets[2], end), "replica", 3))
    from_end = along(end, INWARD)

    state = jax.ShapeDtypeStruct((2, rows_up, half_cols), F32)
    states = call(
        functools.partial(state_kernel, tensors),
        "up_state",
        [state] * (tensors - 1),
        [VMEM] * 2,
        [VMEM] * (tensors - 1),
        [],
        master_up,
        moment_up,
    )
    states = [
        lax.ppermute(x, "tensor", [(i, (i + shift) % tensors) for i in range(tensors)])
        for shift, x in enumerate(states, 1)
    ]

    base = lax.dot_general(
        basis_t, master_embed[0], (((1,), (1,)), ((), ())), precision=HIGHEST
    )
    norm_state = jax.ShapeDtypeStruct(master_norm.shape, F32)
    embed_rows = jax.ShapeDtypeStruct((rows_embed, width), BF16)
    stored_rows, recast_rows, velocity_rows, norm_cast, stored_norm, velocity_norm = call(
        functools.partial(embed_kernel, replicas, replicas - 1),
        "embed_update",
        [
            jax.ShapeDtypeStruct((rows_embed, width), F32),
            embed_rows,
            rank_rows,
            jax.ShapeDtypeStruct(master_norm.shape, BF16),
            norm_state,
            norm_state,
        ],
        [VMEM] * (7 + replicas),
        [VMEM] * 6,
        [],
        own_rows,
        base,
        master_embed[0],
        moment_embed[0].T,
        basis_t,
        trained_norm[0],
        master_norm,
        moment_norm,
        *packets_came,
    )

    embed_out = along(recast_rows, OUTWARD)
    embed_middle = along(recast_rows, ACROSS)
    end_sum = gate(add(end, from_end), embed_middle)
    end_partial = along(end_sum, ACROSS)
    middle_sum = add(middle, along(gate(middle, from_end), INWARD), embed_out)
    middle_partial = along(middle_sum, ACROSS)
    from_near = along(gate(near, middle_sum), INWARD)
    embed_middle_out = along(embed_middle, OUTWARD)
    to_end = along(add(near, end_partial, embed_middle_out), OUTWARD)
    came0 = [own, from_near, middle_partial, to_end]
    half_sum = jax.ShapeDtypeStruct((rows_up, half_cols), F32)
    down_state = jax.ShapeDtypeStruct((rows_down, width), F32)
    piece, stored_down, velocity_down, *sums = call(
        functools.partial(update_kernel, replicas, tensors, len(came0)),
        "update_rows",
        [packed, down_state, down_state] + [half_sum] * tensors,
        [VMEM] * (4 + len(came0) + len(states)),
        [VMEM] * (3 + tensors),
        [pltpu.VMEM((tall, half_cols), F32)] * 3,
        master_down[0],
        moment_down[0],
        master_up,
        moment_up,
        *came0,
        *states,
    )

    top = shards // 2
    came_near = swap(piece, "replica", 1)
    middle_piece = along(piece, ACROSS)
    far_piece = swap(piece, "shard", top)
    end_piece = along(came_near, ACROSS)
    second_out = along(middle_piece, OUTWARD)
    near_piece = gate(came_near, far_piece)
    far_near = swap(near_piece, "shard", top)
    sums = [sums[0]] + [
        lax.ppermute(
            gate(x, near_piece), "tensor", [(i, (i + shift) % tensors) for i in range(tensors)]
        )
        for shift, x in enumerate(sums[1:], 1)
    ]
    second = pick(middle_piece, second_out, far_near)
    far_second = swap(second, "shard", top)
    embed_in = along(gate(recast_rows, near_piece), INWARD)
    embed_end = along(embed_in, ACROSS)
    third = pick(end_piece, along(end_piece, OUTWARD), far_second, embed_end, *sums[1:])
    far_third = swap(third, "shard", top)
    embed_last = along(embed_end, OUTWARD)
    bundles = [
        (
            [(0, 0), (0, top), (1, 0), (1, top)],
            spread_low(bundle([piece, far_piece, near_piece, far_near], third)),
        ),
        (
            [(2, 0), (2, top), (3, 0)],
            spread_low(bundle([second, far_second, third])),
        ),
    ]

    stored_up, velocity_up, token = call(
        functools.partial(up_kernel, replicas, tensors),
        "update_up",
        [jax.ShapeDtypeStruct(master_up.shape, F32)] * 2 + [token_shape],
        [VMEM] * (2 + tensors) + [ANY],
        [VMEM] * 3,
        [],
        master_up,
        moment_up,
        *sums,
        list(bundles[0][1].values())[-1],
    )

    embed_shape = jax.ShapeDtypeStruct((replicas, rows_embed, width), BF16)
    recast_embed, token = call(
        functools.partial(place_embed_kernel, [0, 1, 2]),
        "place_embed",
        [embed_shape, token_shape],
        [VMEM] * 4,
        [HBM, VMEM],
        [dma((3,))],
        recast_rows,
        pick(embed_in, embed_out),
        pick(embed_middle, embed_middle_out),
        token,
    )

    shapes = [jax.ShapeDtypeStruct(down.shape, BF16), jax.ShapeDtypeStruct(up.shape, BF16)]

    def place(slots, arrays, placed, *after):
        keys = [(low, slots) for low in arrays]
        count = len(keys) + len(after)
        return call(
            functools.partial(place_kernel, keys),
            "place_rows",
            shapes + [token_shape],
            [VMEM] * count + [HBM] * len(placed),
            [HBM] * 2 + [VMEM],
            [dma((len(keys) * len(slots) * (1 + chunks),))],
            *arrays.values(),
            *after,
            *placed,
            aliases={count: 0, count + 1: 1} if placed else {},
        )

    placed = []
    for slots, arrays in bundles:
        *placed, token = place(slots, arrays, placed, token)
    last = spread_low(bundle([far_third], token))
    recast_embed, token = call(
        functools.partial(place_embed_kernel, [3]),
        "place_embed",
        [embed_shape, token_shape],
        [VMEM] * 2 + [HBM],
        [HBM, VMEM],
        [dma((1,))],
        pick(embed_end, embed_last),
        last[0],
        recast_embed,
        aliases={2: 0},
    )
    recast_down, recast_up, _ = place([(3, top)], last, placed, token)

    return (
        recast_up.reshape(-1, half_cols),
        recast_down.reshape(-1, width),
        recast_embed.reshape(-1, width),
        norm_cast,
        stored_up,
        velocity_up,
        stored_down[None],
        velocity_down[None],
        stored_rows[None],
        velocity_rows.T[None],
        stored_norm,
        velocity_norm,
    )


def solution(mesh):
    in_specs = (
        P("replica", None, "tensor"),
        P("replica", "tensor", None),
        P("replica", ("shard", "tensor"), None),
        P("replica", None, None),
        P(("replica", "shard", "tensor"), None),
        P(("replica", "shard", "tensor"), None),
        P("tensor", ("replica", "shard"), None),
        P("tensor", ("replica", "shard"), None),
        P(("shard", "tensor"), "replica", None),
        P(("shard", "tensor"), "replica", None),
        P(),
        P(),
        P(),
    )
    out_specs = (
        P(None, "tensor"),
        P("tensor", None),
        P(("shard", "tensor"), None),
        P(),
        P(("replica", "shard", "tensor"), None),
        P(("replica", "shard", "tensor"), None),
        P("tensor", ("replica", "shard"), None),
        P("tensor", ("replica", "shard"), None),
        P(("shard", "tensor"), "replica", None),
        P(("shard", "tensor"), "replica", None),
        P(),
        P(),
    )
    return jax.shard_map(body, mesh=mesh, in_specs=in_specs, out_specs=out_specs, check_vma=False)
```

```python
import functools

import jax
import jax.numpy as jnp
from jax import lax
from jax.experimental import pallas as pl
from jax.experimental.pallas import tpu as pltpu
from jax.sharding import PartitionSpec as P

F32 = jnp.float32
BF16 = jnp.bfloat16
HIGHEST = lax.Precision.HIGHEST
HBM = pl.BlockSpec(memory_space=pltpu.HBM)
ANY = pl.BlockSpec(memory_space=pl.ANY)
VMEM = pl.BlockSpec(memory_space=pltpu.VMEM)


def outer_step(master, moment, summed, groups):
    difference = master - summed / groups
    velocity = 0.5 * moment + difference
    return (master - 0.7 * (difference + 0.5 * velocity), velocity)


def call(
    kernel, name, out_shape, in_specs, out_specs, scratch, *operands, limit=24, aliases={}, weight=3
):
    size = sum(x.size * x.dtype.itemsize for x in jax.tree.leaves(out_shape))
    return pl.pallas_call(
        kernel,
        name=name,
        out_shape=out_shape,
        in_specs=in_specs,
        out_specs=out_specs,
        scratch_shapes=scratch,
        input_output_aliases=aliases,
        compiler_params=pltpu.CompilerParams(vmem_limit_bytes=limit * 2**20),
        cost_estimate=pl.CostEstimate(flops=0, bytes_accessed=weight * size, transcendentals=0),
    )(*operands)


OUTER = (0, 3)
INWARD = ((0, 1), (3, 2))
ACROSS = ((1, 2), (2, 1))
OUTWARD = ((1, 0), (2, 3))


def owners():
    pos = lax.axis_index("replica")
    low = pos < 2
    return pos, jnp.bitwise_xor(pos, 1), jnp.where(low, 2, 1), jnp.where(low, 3, 0)


def along(x, pairs):
    return lax.ppermute(x, "replica", pairs)


def swap(x, axis, bit):
    return lax.ppermute(x, axis, [(i, i ^ bit) for i in range(lax.axis_size(axis))])


def bits_down(size):
    bit = size // 2
    while bit:
        yield bit
        bit //= 2


def project_kernel(trained, basis, norm, own, *refs):
    *outs, projected = refs
    rank, rows = basis.shape[0], own.shape[1]
    high = basis[...].astype(BF16)
    rest = basis[...] - high.astype(F32)
    middle = rest.astype(BF16)
    low = (rest - middle.astype(F32)).astype(BF16)
    split = jnp.concatenate([high, middle, low], axis=0)
    product = lax.dot_general(
        split, trained[...], (((1,), (1,)), ((), ())), preferred_element_type=F32
    )
    projected[...] = product[:rank] + (product[rank : 2 * rank] + product[2 * rank :])
    pos = lax.axis_index("replica")
    values = norm[...].astype(F32)
    per = norm.shape[1] // rows
    extra = outs[0].shape[0] - rank
    parts = [
        values[i // per : i // per + 1, (i % per) * rows : (i % per + 1) * rows]
        for i in range(norm.shape[0] * per)
    ]
    parts = jnp.concatenate((parts * extra)[:extra], axis=0).astype(BF16)
    own[...] = projected[:, pl.ds(pl.multiple_of(pos * rows, rows), rows)]
    for mask, out in enumerate(outs, 1):
        owner = jnp.bitwise_xor(pos, mask)
        block = projected[:, pl.ds(pl.multiple_of(owner * rows, rows), rows)]
        out[:rank, :] = block.astype(BF16)
        out[rank:, :] = parts


def embed_kernel(groups, n_came, *refs):
    refs = list(refs)
    own, base, master, moment, basis, norm, master_norm, moment_norm = refs[:8]
    came = refs[8 : 8 + n_came]
    stored, recast, velocity, norm_cast, norm_stored, norm_velocity = refs[-6:]
    rank, rows = own.shape
    total = own[...]
    for ref in came:
        total = total + ref[:rank, :].astype(F32)
    coefficient = base[...] - total / groups
    moved = 0.5 * moment[...] + coefficient
    velocity[...] = moved
    change = lax.dot_general(
        coefficient + 0.5 * moved,
        basis[...],
        (((0,), (0,)), ((), ())),
        precision=HIGHEST,
        preferred_element_type=F32,
    )
    new = master[...] - 0.7 * change
    stored[...] = new
    recast[...] = new.astype(BF16)
    per = norm.shape[1] // rows
    values = norm[...].astype(F32)
    tails = [ref[rank:, :].astype(F32) for ref in came]
    for i in range(norm.shape[0] * per):
        row, span = i // per, slice((i % per) * rows, (i % per + 1) * rows)
        summed = values[row : row + 1, span]
        for tail in tails:
            summed = summed + tail[i : i + 1, :]
        new_norm, moved_norm = outer_step(
            master_norm[row : row + 1, span], moment_norm[row : row + 1, span], summed, groups
        )
        norm_stored[row : row + 1, span] = new_norm
        norm_velocity[row : row + 1, span] = moved_norm
    norm_cast[...] = norm_stored[...].astype(BF16)


def pack_kernel(down, up, *refs):
    *outs, sems = refs
    shard = lax.axis_index("shard")
    rows, width = down.shape[2:]
    tall, cols = up.shape[2:]
    copies = []

    def bring(source, dest):
        copies.append(pltpu.make_async_copy(source, dest, sems.at[len(copies)]))
        copies[-1].start()

    for owner, out in reversed(list(zip(owners(), outs))):
        bring(down.at[owner, shard], out.at[pl.ds(0, rows)])
        for chunk in range(cols // width):
            bring(
                up.at[owner, shard, :, pl.ds(chunk * width, width)],
                out.at[pl.ds(rows + chunk * tall, tall)],
            )
    for copy in copies:
        copy.wait()


def add_kernel(block, came, *refs):
    refs[-1][...] = (block[...].astype(F32) + came[...].astype(F32)).astype(BF16)


def add(block, came, *after):
    return call(
        add_kernel,
        "add_block",
        jax.ShapeDtypeStruct(block.shape, BF16),
        [VMEM] * 2 + [ANY] * len(after),
        VMEM,
        [],
        block,
        came,
        *after,
    )


def pick_kernel(middle, end, *refs):
    out = refs[-1]
    pos = lax.axis_index("replica")
    outer = jnp.logical_or(pos == OUTER[0], pos == OUTER[1])

    @pl.when(outer)
    def _():
        out[...] = end[...]

    @pl.when(jnp.logical_not(outer))
    def _():
        out[...] = middle[...]


def pick(middle, end, *after):
    specs = [VMEM] * 2 + [ANY] * len(after)
    shape = jax.ShapeDtypeStruct(end.shape, end.dtype)
    return call(pick_kernel, "pick", shape, specs, VMEM, [], middle, end, *after)


def update_kernel(groups, tensors, n_came, *refs):
    refs = list(refs)
    master_down, moment_down, master_up, moment_up = refs[:4]
    came, state_came = refs[4 : 4 + n_came], refs[4 + n_came : 3 + n_came + tensors]
    piece, token, stored_down, velocity_down, *sums = refs[3 + n_came + tensors : -3]
    token[...] = jnp.zeros_like(token)
    summed, master, moment = refs[-3:]
    me = lax.axis_index("tensor")
    rows_down, width = master_down.shape
    rows_up = master_up.shape[0]
    tall, cols = summed.shape

    def at(index):
        return pl.ds(pl.multiple_of(index * rows_up, rows_up), rows_up)

    own_cols = pl.ds(pl.multiple_of(me * cols, cols), cols)
    master[at(me), :] = master_up[:, own_cols]
    moment[at(me), :] = moment_up[:, own_cols]
    for shift in range(1, tensors):
        source = lax.rem(me + tensors - shift, tensors)
        master[at(source), :] = state_came[shift - 1][0]
        moment[at(source), :] = state_came[shift - 1][1]

    def total(lo, hi):
        value = came[0][lo:hi, :].astype(F32)
        for ref in came[1:]:
            value = value + ref[lo:hi, :].astype(F32)
        return value

    stored, velocity = outer_step(
        master_down[...], moment_down[...], total(0, rows_down), groups
    )
    stored_down[...] = stored
    velocity_down[...] = velocity
    piece[:rows_down, :] = stored.astype(BF16)
    for chunk in range(cols // width):
        lo = rows_down + chunk * tall
        part = total(lo, lo + tall)
        span = slice(chunk * width, (chunk + 1) * width)
        summed[:, span] = part
        stored, _ = outer_step(master[:, span], moment[:, span], part, groups)
        piece[lo : lo + tall, :] = stored.astype(BF16)
    for shift in range(tensors):
        sums[shift][...] = summed[at(lax.rem(me + shift, tensors)), :]


def up_kernel(groups, tensors, master_up, moment_up, *refs):
    sums, (stored_up, velocity_up, token) = refs[:tensors], refs[-3:]
    cols = sums[0].shape[1]
    me = lax.axis_index("tensor")
    for shift in range(tensors):
        source = lax.rem(me + tensors - shift, tensors)
        span = pl.ds(pl.multiple_of(source * cols, cols), cols)
        stored, velocity = outer_step(
            master_up[:, span], moment_up[:, span], sums[shift][...], groups
        )
        stored_up[:, span] = stored
        velocity_up[:, span] = velocity
    token[...] = jnp.zeros_like(token)


def state_kernel(tensors, master_up, moment_up, *outs):
    me = lax.axis_index("tensor")
    cols = outs[0].shape[2]
    for shift in range(1, tensors):
        target = lax.rem(me + shift, tensors)
        span = pl.ds(pl.multiple_of(target * cols, cols), cols)
        outs[shift - 1][0] = master_up[:, span]
        outs[shift - 1][1] = moment_up[:, span]


def gate_kernel(x, *refs):
    refs[-1][...] = x[...]


def gate(x, *after):
    return call(
        gate_kernel,
        "gate",
        jax.ShapeDtypeStruct(x.shape, x.dtype),
        [VMEM] + [ANY] * len(after),
        VMEM,
        [],
        x,
        *after,
    )


def stack_kernel(count, *refs):
    for i in range(count):
        refs[-1][i] = refs[i][...]


def bundle(pieces, *after):
    return call(
        functools.partial(stack_kernel, len(pieces)),
        "bundle",
        jax.ShapeDtypeStruct((len(pieces),) + pieces[0].shape, BF16),
        [VMEM] * len(pieces) + [ANY] * len(after),
        VMEM,
        [],
        *pieces,
        *after,
    )


def place_kernel(keys, *refs):
    bundles, (down, up, token, sems) = refs[: len(keys)], refs[-4:]
    token[...] = jnp.zeros_like(token)
    shard = lax.axis_index("shard")
    rows, width = down.shape[2:]
    tall, cols = up.shape[2:]
    copies = []

    def send(source, dest):
        copies.append(pltpu.make_async_copy(source, dest, sems.at[len(copies)]))
        copies[-1].start()

    for pieces, (low, slots) in zip(bundles, keys):
        for i, (slot, mask) in enumerate(slots):
            owner, place = owners()[slot], jnp.bitwise_xor(shard, mask ^ low)
            send(pieces.at[i, pl.ds(0, rows)], down.at[owner, place])
            for chunk in range(cols // width):
                send(
                    pieces.at[i, pl.ds(rows + chunk * tall, tall)],
                    up.at[owner, place, :, pl.ds(chunk * width, width)],
                )
    for copy in copies:
        copy.wait()


def place_embed_kernel(slots, *refs):
    pieces, (out, token, sems) = refs[: len(slots)], refs[-3:]
    token[...] = jnp.zeros_like(token)
    copies = [
        pltpu.make_async_copy(piece, out.at[owners()[slot]], sems.at[i])
        for i, (piece, slot) in enumerate(zip(pieces, slots))
    ]
    for copy in copies:
        copy.start()
    for copy in copies:
        copy.wait()


def spread_low(x):
    found = {0: x}
    for bit in bits_down(lax.axis_size("shard") // 2):
        found.update({mask ^ bit: swap(y, "shard", bit) for mask, y in list(found.items())})
    return found


def body(
    trained_up,
    trained_down,
    trained_embed,
    trained_norm,
    master_up,
    moment_up,
    master_down,
    moment_down,
    master_embed,
    moment_embed,
    master_norm,
    moment_norm,
    embed_basis,
):
    replicas = lax.axis_size("replica")
    shards = lax.axis_size("shard")
    tensors = lax.axis_size("tensor")
    width, rank = embed_basis.shape
    rows_up, half_cols = master_up.shape[0], trained_up.shape[2]
    rows_down, rows_embed = master_down.shape[1], master_embed.shape[1]
    tall = tensors * rows_up
    chunks = half_cols // width
    packed = jax.ShapeDtypeStruct((rows_down + chunks * tall, width), BF16)
    dma = pltpu.SemaphoreType.DMA

    basis_t = embed_basis.T
    rank_rows = jax.ShapeDtypeStruct((rank, rows_embed), F32)
    packet = jax.ShapeDtypeStruct((rank + 16, rows_embed), BF16)
    token_shape = jax.ShapeDtypeStruct((8, 128), F32)
    own_rows, *packets = call(
        project_kernel,
        "project_rows",
        [rank_rows] + [packet] * (replicas - 1),
        [VMEM] * 3,
        [VMEM] * replicas,
        [pltpu.VMEM((rank, replicas * rows_embed), F32)],
        pltpu.with_memory_space_constraint(trained_embed[0], pltpu.HBM),
        pltpu.with_memory_space_constraint(basis_t, pltpu.HBM),
        pltpu.with_memory_space_constraint(trained_norm[0], pltpu.HBM),
    )
    down = trained_down[0].reshape(replicas, shards, rows_down, width)
    up = trained_up[0].reshape(replicas, shards, tall, half_cols)
    own, near, middle, end = call(
        pack_kernel,
        "pack_blocks",
        [packed] * replicas,
        [HBM] * 2,
        [VMEM] * replicas,
        [dma((replicas * (1 + chunks),))],
        pltpu.with_memory_space_constraint(down, pltpu.HBM),
        pltpu.with_memory_space_constraint(up, pltpu.HBM),
    )
    packets_came = [swap(packets[0], "replica", 1), swap(packets[1], "replica", 2)]
    end = gate(end, packets_came[0])
    packets_came.append(swap(gate(packets[2], end), "replica", 3))
    from_end = along(end, INWARD)

    state = jax.ShapeDtypeStruct((2, rows_up, half_cols), F32)
    states = call(
        functools.partial(state_kernel, tensors),
        "up_state",
        [state] * (tensors - 1),
        [VMEM] * 2,
        [VMEM] * (tensors - 1),
        [],
        master_up,
        moment_up,
    )
    states = [
        lax.ppermute(x, "tensor", [(i, (i + shift) % tensors) for i in range(tensors)])
        for shift, x in enumerate(states, 1)
    ]

    base = lax.dot_general(
        basis_t, master_embed[0], (((1,), (1,)), ((), ())), precision=HIGHEST
    )
    norm_state = jax.ShapeDtypeStruct(master_norm.shape, F32)
    embed_rows = jax.ShapeDtypeStruct((rows_embed, width), BF16)
    stored_rows, recast_rows, velocity_rows, norm_cast, stored_norm, velocity_norm = call(
        functools.partial(embed_kernel, replicas, replicas - 1),
        "embed_update",
        [
            jax.ShapeDtypeStruct((rows_embed, width), F32),
            embed_rows,
            rank_rows,
            jax.ShapeDtypeStruct(master_norm.shape, BF16),
            norm_state,
            norm_state,
        ],
        [VMEM] * (7 + replicas),
        [VMEM] * 6,
        [],
        own_rows,
        base,
        master_embed[0],
        moment_embed[0].T,
        basis_t,
        trained_norm[0],
        master_norm,
        moment_norm,
        *packets_came,
    )

    embed_out = along(recast_rows, OUTWARD)
    embed_middle = along(recast_rows, ACROSS)
    end_sum = add(end, from_end)
    end_partial = along(end_sum, ACROSS)
    middle_sum = add(middle, along(gate(middle, from_end), INWARD), embed_out)
    middle_partial = along(middle_sum, ACROSS)
    from_near = along(gate(near, middle_sum), INWARD)
    embed_middle_out = along(embed_middle, OUTWARD)
    to_end = along(add(near, end_partial, embed_middle_out), OUTWARD)
    came0 = [own, from_near, middle_partial, to_end]
    half_sum = jax.ShapeDtypeStruct((rows_up, half_cols), F32)
    down_state = jax.ShapeDtypeStruct((rows_down, width), F32)
    piece, token, stored_down, velocity_down, *sums = call(
        functools.partial(update_kernel, replicas, tensors, len(came0)),
        "update_rows",
        [packed, token_shape, down_state, down_state] + [half_sum] * tensors,
        [VMEM] * (4 + len(came0) + len(states)),
        [VMEM] * (4 + tensors),
        [pltpu.VMEM((tall, half_cols), F32)] * 3,
        master_down[0],
        moment_down[0],
        master_up,
        moment_up,
        *came0,
        *states,
    )

    top = shards // 2
    came_near = swap(piece, "replica", 1)
    middle_piece = along(piece, ACROSS)
    far_piece = swap(gate(piece, swap(token, "shard", 1)), "shard", top)
    end_piece = along(came_near, ACROSS)
    second_out = along(middle_piece, OUTWARD)
    near_piece = came_near
    far_near = swap(near_piece, "shard", top)
    sums = [sums[0]] + [
        lax.ppermute(
            gate(x, near_piece), "tensor", [(i, (i + shift) % tensors) for i in range(tensors)]
        )
        for shift, x in enumerate(sums[1:], 1)
    ]
    second = pick(middle_piece, second_out, far_near, far_piece)
    far_second = swap(second, "shard", top)
    embed_in = along(gate(recast_rows, near_piece), INWARD)
    embed_end = along(embed_in, ACROSS)
    third = pick(end_piece, along(end_piece, OUTWARD), far_second, embed_end, *sums[1:])
    far_third = swap(third, "shard", top)
    embed_last = along(embed_end, OUTWARD)
    bundles = [
        (
            [(0, 0), (0, top), (1, 0), (1, top)],
            spread_low(bundle([piece, far_piece, near_piece, far_near], third)),
        ),
        (
            [(2, 0), (2, top), (3, 0)],
            spread_low(bundle([second, far_second, third])),
        ),
    ]

    stored_up, velocity_up, token = call(
        functools.partial(up_kernel, replicas, tensors),
        "update_up",
        [jax.ShapeDtypeStruct(master_up.shape, F32)] * 2 + [token_shape],
        [VMEM] * (2 + tensors) + [ANY],
        [VMEM] * 3,
        [],
        master_up,
        moment_up,
        *sums,
        list(bundles[0][1].values())[-1],
    )

    embed_shape = jax.ShapeDtypeStruct((replicas, rows_embed, width), BF16)
    recast_embed, token = call(
        functools.partial(place_embed_kernel, [0, 1, 2]),
        "place_embed",
        [embed_shape, token_shape],
        [VMEM] * 4,
        [HBM, VMEM],
        [dma((3,))],
        recast_rows,
        pick(embed_in, embed_out),
        pick(embed_middle, embed_middle_out),
        token,
    )

    shapes = [jax.ShapeDtypeStruct(down.shape, BF16), jax.ShapeDtypeStruct(up.shape, BF16)]

    def place(slots, arrays, placed, *after):
        keys = [(low, slots) for low in arrays]
        count = len(keys) + len(after)
        return call(
            functools.partial(place_kernel, keys),
            "place_rows",
            shapes + [token_shape],
            [VMEM] * count + [HBM] * len(placed),
            [HBM] * 2 + [VMEM],
            [dma((len(keys) * len(slots) * (1 + chunks),))],
            *arrays.values(),
            *after,
            *placed,
            aliases={count: 0, count + 1: 1} if placed else {},
        )

    placed = []
    for slots, arrays in bundles:
        *placed, token = place(slots, arrays, placed, token)
    last = spread_low(bundle([far_third], token))
    recast_embed, token = call(
        functools.partial(place_embed_kernel, [3]),
        "place_embed",
        [embed_shape, token_shape],
        [VMEM] * 2 + [HBM],
        [HBM, VMEM],
        [dma((1,))],
        pick(embed_end, embed_last),
        last[0],
        recast_embed,
        aliases={2: 0},
        weight=30,
    )
    recast_down, recast_up, _ = place([(3, top)], last, placed, token)

    return (
        recast_up.reshape(-1, half_cols),
        recast_down.reshape(-1, width),
        recast_embed.reshape(-1, width),
        norm_cast,
        stored_up,
        velocity_up,
        stored_down[None],
        velocity_down[None],
        stored_rows[None],
        velocity_rows.T[None],
        stored_norm,
        velocity_norm,
    )


def solution(mesh):
    in_specs = (
        P("replica", None, "tensor"),
        P("replica", "tensor", None),
        P("replica", ("shard", "tensor"), None),
        P("replica", None, None),
        P(("replica", "shard", "tensor"), None),
        P(("replica", "shard", "tensor"), None),
        P("tensor", ("replica", "shard"), None),
        P("tensor", ("replica", "shard"), None),
        P(("shard", "tensor"), "replica", None),
        P(("shard", "tensor"), "replica", None),
        P(),
        P(),
        P(),
    )
    out_specs = (
        P(None, "tensor"),
        P("tensor", None),
        P(("shard", "tensor"), None),
        P(),
        P(("replica", "shard", "tensor"), None),
        P(("replica", "shard", "tensor"), None),
        P("tensor", ("replica", "shard"), None),
        P("tensor", ("replica", "shard"), None),
        P(("shard", "tensor"), "replica", None),
        P(("shard", "tensor"), "replica", None),
        P(),
        P(),
    )
    return jax.shard_map(body, mesh=mesh, in_specs=in_specs, out_specs=out_specs, check_vma=False)
```

```python
import functools

import jax
import jax.numpy as jnp
from jax import lax
from jax.experimental import pallas as pl
from jax.experimental.pallas import tpu as pltpu
from jax.sharding import PartitionSpec as P

F32 = jnp.float32
BF16 = jnp.bfloat16
HIGHEST = lax.Precision.HIGHEST
HBM = pl.BlockSpec(memory_space=pltpu.HBM)
ANY = pl.BlockSpec(memory_space=pl.ANY)
VMEM = pl.BlockSpec(memory_space=pltpu.VMEM)


def outer_step(master, moment, summed, groups):
    difference = master - summed / groups
    velocity = 0.5 * moment + difference
    return (master - 0.7 * (difference + 0.5 * velocity), velocity)


def call(kernel, name, out_shape, in_specs, out_specs, scratch, *operands, limit=24, aliases={}):
    size = sum(x.size * x.dtype.itemsize for x in jax.tree.leaves(out_shape))
    return pl.pallas_call(
        kernel,
        name=name,
        out_shape=out_shape,
        in_specs=in_specs,
        out_specs=out_specs,
        scratch_shapes=scratch,
        input_output_aliases=aliases,
        compiler_params=pltpu.CompilerParams(vmem_limit_bytes=limit * 2**20),
        cost_estimate=pl.CostEstimate(flops=0, bytes_accessed=3 * size, transcendentals=0),
    )(*operands)


OUTER = (0, 3)
INWARD = ((0, 1), (3, 2))
ACROSS = ((1, 2), (2, 1))
OUTWARD = ((1, 0), (2, 3))


def owners():
    pos = lax.axis_index("replica")
    low = pos < 2
    return pos, jnp.bitwise_xor(pos, 1), jnp.where(low, 2, 1), jnp.where(low, 3, 0)


def along(x, pairs):
    return lax.ppermute(x, "replica", pairs)


def swap(x, axis, bit):
    return lax.ppermute(x, axis, [(i, i ^ bit) for i in range(lax.axis_size(axis))])


def bits_down(size):
    bit = size // 2
    while bit:
        yield bit
        bit //= 2


def project_kernel(trained, basis, norm, own, *refs):
    *outs, projected = refs
    rank, rows = basis.shape[0], own.shape[1]
    high = basis[...].astype(BF16)
    rest = basis[...] - high.astype(F32)
    middle = rest.astype(BF16)
    low = (rest - middle.astype(F32)).astype(BF16)
    split = jnp.concatenate([high, middle, low], axis=0)
    product = lax.dot_general(
        split, trained[...], (((1,), (1,)), ((), ())), preferred_element_type=F32
    )
    projected[...] = product[:rank] + (product[rank : 2 * rank] + product[2 * rank :])
    pos = lax.axis_index("replica")
    values = norm[...].astype(F32)
    per = norm.shape[1] // rows
    extra = outs[0].shape[0] - rank
    parts = [
        values[i // per : i // per + 1, (i % per) * rows : (i % per + 1) * rows]
        for i in range(norm.shape[0] * per)
    ]
    parts = jnp.concatenate((parts * extra)[:extra], axis=0).astype(BF16)
    own[...] = projected[:, pl.ds(pl.multiple_of(pos * rows, rows), rows)]
    for mask, out in enumerate(outs, 1):
        owner = jnp.bitwise_xor(pos, mask)
        block = projected[:, pl.ds(pl.multiple_of(owner * rows, rows), rows)]
        out[:rank, :] = block.astype(BF16)
        out[rank:, :] = parts


def embed_kernel(groups, n_came, *refs):
    refs = list(refs)
    own, base, master, moment, basis, norm, master_norm, moment_norm = refs[:8]
    came = refs[8 : 8 + n_came]
    stored, recast, velocity, norm_cast, norm_stored, norm_velocity = refs[-6:]
    rank, rows = own.shape
    total = own[...]
    for ref in came:
        total = total + ref[:rank, :].astype(F32)
    coefficient = base[...] - total / groups
    moved = 0.5 * moment[...] + coefficient
    velocity[...] = moved
    change = lax.dot_general(
        coefficient + 0.5 * moved,
        basis[...],
        (((0,), (0,)), ((), ())),
        precision=HIGHEST,
        preferred_element_type=F32,
    )
    new = master[...] - 0.7 * change
    stored[...] = new
    recast[...] = new.astype(BF16)
    per = norm.shape[1] // rows
    values = norm[...].astype(F32)
    tails = [ref[rank:, :].astype(F32) for ref in came]
    for i in range(norm.shape[0] * per):
        row, span = i // per, slice((i % per) * rows, (i % per + 1) * rows)
        summed = values[row : row + 1, span]
        for tail in tails:
            summed = summed + tail[i : i + 1, :]
        new_norm, moved_norm = outer_step(
            master_norm[row : row + 1, span], moment_norm[row : row + 1, span], summed, groups
        )
        norm_stored[row : row + 1, span] = new_norm
        norm_velocity[row : row + 1, span] = moved_norm
    norm_cast[...] = norm_stored[...].astype(BF16)


def pack_kernel(down, up, *refs):
    *outs, sems = refs
    shard = lax.axis_index("shard")
    rows, width = down.shape[2:]
    tall, cols = up.shape[2:]
    copies = []

    def bring(source, dest):
        copies.append(pltpu.make_async_copy(source, dest, sems.at[len(copies)]))
        copies[-1].start()

    for owner, out in reversed(list(zip(owners(), outs))):
        bring(down.at[owner, shard], out.at[pl.ds(0, rows)])
        for chunk in range(cols // width):
            bring(
                up.at[owner, shard, :, pl.ds(chunk * width, width)],
                out.at[pl.ds(rows + chunk * tall, tall)],
            )
    for copy in copies:
        copy.wait()


def add_kernel(block, came, *refs):
    refs[-1][...] = (block[...].astype(F32) + came[...].astype(F32)).astype(BF16)


def add(block, came, *after):
    return call(
        add_kernel,
        "add_block",
        jax.ShapeDtypeStruct(block.shape, BF16),
        [VMEM] * 2 + [ANY] * len(after),
        VMEM,
        [],
        block,
        came,
        *after,
    )


def pick_kernel(middle, end, *refs):
    out = refs[-1]
    pos = lax.axis_index("replica")
    outer = jnp.logical_or(pos == OUTER[0], pos == OUTER[1])

    @pl.when(outer)
    def _():
        out[...] = end[...]

    @pl.when(jnp.logical_not(outer))
    def _():
        out[...] = middle[...]


def pick(middle, end, *after):
    specs = [VMEM] * 2 + [ANY] * len(after)
    shape = jax.ShapeDtypeStruct(end.shape, end.dtype)
    return call(pick_kernel, "pick", shape, specs, VMEM, [], middle, end, *after)


def total(came, lo, hi):
    value = came[0][lo:hi, :].astype(F32)
    for ref in came[1:]:
        value = value + ref[lo:hi, :].astype(F32)
    return value


def rows_kernel(groups, tensors, n_came, *refs):
    refs = list(refs)
    master_down, moment_down, master_up, moment_up = refs[:4]
    came, state_came = refs[4 : 4 + n_came], refs[4 + n_came : 3 + n_came + tensors]
    piece, master, moment = refs[-3:]
    me = lax.axis_index("tensor")
    rows_down, width = master_down.shape
    rows_up = master_up.shape[0]
    tall, cols = master.shape

    def at(index):
        return pl.ds(pl.multiple_of(index * rows_up, rows_up), rows_up)

    own_cols = pl.ds(pl.multiple_of(me * cols, cols), cols)
    master[at(me), :] = master_up[:, own_cols]
    moment[at(me), :] = moment_up[:, own_cols]
    for shift in range(1, tensors):
        source = lax.rem(me + tensors - shift, tensors)
        master[at(source), :] = state_came[shift - 1][0]
        moment[at(source), :] = state_came[shift - 1][1]
    stored, _ = outer_step(
        master_down[...], moment_down[...], total(came, 0, rows_down), groups
    )
    piece[:rows_down, :] = stored.astype(BF16)
    for chunk in range(cols // width):
        lo = rows_down + chunk * tall
        span = slice(chunk * width, (chunk + 1) * width)
        stored, _ = outer_step(
            master[:, span], moment[:, span], total(came, lo, lo + tall), groups
        )
        piece[lo : lo + tall, :] = stored.astype(BF16)


def states_kernel(groups, tensors, n_came, *refs):
    master_down, moment_down = refs[:2]
    came = refs[2 : 2 + n_came]
    stored_down, velocity_down, *sums, summed = refs[-3 - tensors :]
    rows_down, width = master_down.shape
    rows_up = sums[0].shape[0]
    tall, cols = summed.shape
    me = lax.axis_index("tensor")
    stored, velocity = outer_step(
        master_down[...], moment_down[...], total(came, 0, rows_down), groups
    )
    stored_down[...] = stored
    velocity_down[...] = velocity
    for chunk in range(cols // width):
        lo = rows_down + chunk * tall
        summed[:, chunk * width : (chunk + 1) * width] = total(came, lo, lo + tall)
    for shift in range(tensors):
        owner = lax.rem(me + shift, tensors)
        sums[shift][...] = summed[pl.ds(pl.multiple_of(owner * rows_up, rows_up), rows_up), :]


def up_kernel(groups, tensors, master_up, moment_up, *refs):
    sums, (stored_up, velocity_up, token) = refs[:tensors], refs[-3:]
    cols = sums[0].shape[1]
    me = lax.axis_index("tensor")
    for shift in range(tensors):
        source = lax.rem(me + tensors - shift, tensors)
        span = pl.ds(pl.multiple_of(source * cols, cols), cols)
        stored, velocity = outer_step(
            master_up[:, span], moment_up[:, span], sums[shift][...], groups
        )
        stored_up[:, span] = stored
        velocity_up[:, span] = velocity
    token[...] = jnp.zeros_like(token)


def state_kernel(tensors, master_up, moment_up, *outs):
    me = lax.axis_index("tensor")
    cols = outs[0].shape[2]
    for shift in range(1, tensors):
        target = lax.rem(me + shift, tensors)
        span = pl.ds(pl.multiple_of(target * cols, cols), cols)
        outs[shift - 1][0] = master_up[:, span]
        outs[shift - 1][1] = moment_up[:, span]


def gate_kernel(x, *refs):
    refs[-1][...] = x[...]


def gate(x, *after):
    return call(
        gate_kernel,
        "gate",
        jax.ShapeDtypeStruct(x.shape, x.dtype),
        [VMEM] + [ANY] * len(after),
        VMEM,
        [],
        x,
        *after,
    )


def stack_kernel(count, *refs):
    for i in range(count):
        refs[-1][i] = refs[i][...]


def bundle(pieces, *after):
    return call(
        functools.partial(stack_kernel, len(pieces)),
        "bundle",
        jax.ShapeDtypeStruct((len(pieces),) + pieces[0].shape, BF16),
        [VMEM] * len(pieces) + [ANY] * len(after),
        VMEM,
        [],
        *pieces,
        *after,
    )


def place_kernel(keys, *refs):
    bundles, (down, up, token, sems) = refs[: len(keys)], refs[-4:]
    token[...] = jnp.zeros_like(token)
    shard = lax.axis_index("shard")
    rows, width = down.shape[2:]
    tall, cols = up.shape[2:]
    copies = []

    def send(source, dest):
        copies.append(pltpu.make_async_copy(source, dest, sems.at[len(copies)]))
        copies[-1].start()

    for pieces, (low, slots) in zip(bundles, keys):
        for i, (slot, mask) in enumerate(slots):
            owner, place = owners()[slot], jnp.bitwise_xor(shard, mask ^ low)
            send(pieces.at[i, pl.ds(0, rows)], down.at[owner, place])
            for chunk in range(cols // width):
                send(
                    pieces.at[i, pl.ds(rows + chunk * tall, tall)],
                    up.at[owner, place, :, pl.ds(chunk * width, width)],
                )
    for copy in copies:
        copy.wait()


def place_embed_kernel(slots, *refs):
    pieces, (out, token, sems) = refs[: len(slots)], refs[-3:]
    token[...] = jnp.zeros_like(token)
    copies = [
        pltpu.make_async_copy(piece, out.at[owners()[slot]], sems.at[i])
        for i, (piece, slot) in enumerate(zip(pieces, slots))
    ]
    for copy in copies:
        copy.start()
    for copy in copies:
        copy.wait()


def spread_low(x):
    found = {0: x}
    for bit in bits_down(lax.axis_size("shard") // 2):
        found.update({mask ^ bit: swap(y, "shard", bit) for mask, y in list(found.items())})
    return found


def body(
    trained_up,
    trained_down,
    trained_embed,
    trained_norm,
    master_up,
    moment_up,
    master_down,
    moment_down,
    master_embed,
    moment_embed,
    master_norm,
    moment_norm,
    embed_basis,
):
    replicas = lax.axis_size("replica")
    shards = lax.axis_size("shard")
    tensors = lax.axis_size("tensor")
    width, rank = embed_basis.shape
    rows_up, half_cols = master_up.shape[0], trained_up.shape[2]
    rows_down, rows_embed = master_down.shape[1], master_embed.shape[1]
    tall = tensors * rows_up
    chunks = half_cols // width
    packed = jax.ShapeDtypeStruct((rows_down + chunks * tall, width), BF16)
    dma = pltpu.SemaphoreType.DMA

    basis_t = embed_basis.T
    rank_rows = jax.ShapeDtypeStruct((rank, rows_embed), F32)
    packet = jax.ShapeDtypeStruct((rank + 16, rows_embed), BF16)
    token_shape = jax.ShapeDtypeStruct((8, 128), F32)
    own_rows, *packets = call(
        project_kernel,
        "project_rows",
        [rank_rows] + [packet] * (replicas - 1),
        [VMEM] * 3,
        [VMEM] * replicas,
        [pltpu.VMEM((rank, replicas * rows_embed), F32)],
        pltpu.with_memory_space_constraint(trained_embed[0], pltpu.HBM),
        pltpu.with_memory_space_constraint(basis_t, pltpu.HBM),
        pltpu.with_memory_space_constraint(trained_norm[0], pltpu.HBM),
    )
    down = trained_down[0].reshape(replicas, shards, rows_down, width)
    up = trained_up[0].reshape(replicas, shards, tall, half_cols)
    own, near, middle, end = call(
        pack_kernel,
        "pack_blocks",
        [packed] * replicas,
        [HBM] * 2,
        [VMEM] * replicas,
        [dma((replicas * (1 + chunks),))],
        pltpu.with_memory_space_constraint(down, pltpu.HBM),
        pltpu.with_memory_space_constraint(up, pltpu.HBM),
    )
    packets_came = [swap(packets[0], "replica", 1), swap(packets[1], "replica", 2)]
    end = gate(end, packets_came[0])
    packets_came.append(swap(gate(packets[2], end), "replica", 3))
    from_end = along(end, INWARD)

    state = jax.ShapeDtypeStruct((2, rows_up, half_cols), F32)
    states = call(
        functools.partial(state_kernel, tensors),
        "up_state",
        [state] * (tensors - 1),
        [VMEM] * 2,
        [VMEM] * (tensors - 1),
        [],
        master_up,
        moment_up,
    )
    states = [
        lax.ppermute(x, "tensor", [(i, (i + shift) % tensors) for i in range(tensors)])
        for shift, x in enumerate(states, 1)
    ]

    base = lax.dot_general(
        gate(basis_t, packets_came[1]), master_embed[0], (((1,), (1,)), ((), ())), precision=HIGHEST
    )
    norm_state = jax.ShapeDtypeStruct(master_norm.shape, F32)
    embed_rows = jax.ShapeDtypeStruct((rows_embed, width), BF16)
    stored_rows, recast_rows, velocity_rows, norm_cast, stored_norm, velocity_norm = call(
        functools.partial(embed_kernel, replicas, replicas - 1),
        "embed_update",
        [
            jax.ShapeDtypeStruct((rows_embed, width), F32),
            embed_rows,
            rank_rows,
            jax.ShapeDtypeStruct(master_norm.shape, BF16),
            norm_state,
            norm_state,
        ],
        [VMEM] * (7 + replicas),
        [VMEM] * 6,
        [],
        own_rows,
        base,
        master_embed[0],
        moment_embed[0].T,
        basis_t,
        trained_norm[0],
        master_norm,
        moment_norm,
        *packets_came,
    )

    embed_out = along(recast_rows, OUTWARD)
    embed_middle = along(recast_rows, ACROSS)
    end_sum = gate(add(end, from_end), embed_middle)
    end_partial = along(end_sum, ACROSS)
    middle_sum = add(middle, along(gate(middle, from_end), INWARD), embed_out)
    middle_partial = along(middle_sum, ACROSS)
    from_near = along(gate(near, middle_sum), INWARD)
    embed_middle_out = along(embed_middle, OUTWARD)
    to_end = along(add(near, end_partial, embed_middle_out), OUTWARD)
    came0 = [own, from_near, middle_partial, to_end]
    half_sum = jax.ShapeDtypeStruct((rows_up, half_cols), F32)
    down_state = jax.ShapeDtypeStruct((rows_down, width), F32)
    piece = call(
        functools.partial(rows_kernel, replicas, tensors, len(came0)),
        "update_rows",
        packed,
        [VMEM] * (4 + len(came0) + len(states)),
        VMEM,
        [pltpu.VMEM((tall, half_cols), F32)] * 2,
        master_down[0],
        moment_down[0],
        master_up,
        moment_up,
        *came0,
        *states,
    )

    top = shards // 2
    came_near = swap(piece, "replica", 1)
    middle_piece = along(piece, ACROSS)
    far_piece = swap(piece, "shard", top)
    end_piece = along(came_near, ACROSS)
    second_out = along(middle_piece, OUTWARD)
    near_piece = gate(came_near, far_piece)
    far_near = swap(near_piece, "shard", top)
    stored_down, velocity_down, *sums = call(
        functools.partial(states_kernel, replicas, tensors, len(came0)),
        "update_states",
        [down_state, down_state] + [half_sum] * tensors,
        [VMEM] * (2 + len(came0)) + [ANY],
        [VMEM] * (2 + tensors),
        [pltpu.VMEM((tall, half_cols), F32)],
        master_down[0],
        moment_down[0],
        *came0,
        near_piece,
    )
    sums = [sums[0]] + [
        lax.ppermute(x, "tensor", [(i, (i + shift) % tensors) for i in range(tensors)])
        for shift, x in enumerate(sums[1:], 1)
    ]
    second = pick(middle_piece, second_out, far_near, sums[0])
    far_second = swap(second, "shard", top)
    embed_in = along(gate(recast_rows, near_piece), INWARD)
    embed_end = along(embed_in, ACROSS)
    third = pick(end_piece, along(end_piece, OUTWARD), far_second, embed_end, *sums[1:])
    far_third = swap(third, "shard", top)
    embed_last = along(embed_end, OUTWARD)
    bundles = [
        (
            [(0, 0), (0, top), (1, 0), (1, top)],
            spread_low(bundle([piece, far_piece, near_piece, far_near], third)),
        ),
        (
            [(2, 0), (2, top), (3, 0)],
            spread_low(bundle([second, far_second, third])),
        ),
    ]

    stored_up, velocity_up, token = call(
        functools.partial(up_kernel, replicas, tensors),
        "update_up",
        [jax.ShapeDtypeStruct(master_up.shape, F32)] * 2 + [token_shape],
        [VMEM] * (2 + tensors) + [ANY],
        [VMEM] * 3,
        [],
        master_up,
        moment_up,
        *sums,
        list(bundles[0][1].values())[-1],
    )

    embed_shape = jax.ShapeDtypeStruct((replicas, rows_embed, width), BF16)
    recast_embed, token = call(
        functools.partial(place_embed_kernel, [0, 1, 2]),
        "place_embed",
        [embed_shape, token_shape],
        [VMEM] * 4,
        [HBM, VMEM],
        [dma((3,))],
        recast_rows,
        pick(embed_in, embed_out),
        pick(embed_middle, embed_middle_out),
        token,
    )

    shapes = [jax.ShapeDtypeStruct(down.shape, BF16), jax.ShapeDtypeStruct(up.shape, BF16)]

    def place(slots, arrays, placed, *after):
        keys = [(low, slots) for low in arrays]
        count = len(keys) + len(after)
        return call(
            functools.partial(place_kernel, keys),
            "place_rows",
            shapes + [token_shape],
            [VMEM] * count + [HBM] * len(placed),
            [HBM] * 2 + [VMEM],
            [dma((len(keys) * len(slots) * (1 + chunks),))],
            *arrays.values(),
            *after,
            *placed,
            aliases={count: 0, count + 1: 1} if placed else {},
        )

    placed = []
    for slots, arrays in bundles:
        *placed, token = place(slots, arrays, placed, token)
    last = spread_low(bundle([far_third], token))
    recast_down, recast_up, _ = place([(3, top)], last, placed)
    recast_embed, _ = call(
        functools.partial(place_embed_kernel, [3]),
        "place_embed",
        [embed_shape, token_shape],
        [VMEM] + [HBM],
        [HBM, VMEM],
        [dma((1,))],
        pick(embed_end, embed_last),
        recast_embed,
        aliases={1: 0},
    )

    return (
        recast_up.reshape(-1, half_cols),
        recast_down.reshape(-1, width),
        recast_embed.reshape(-1, width),
        norm_cast,
        stored_up,
        velocity_up,
        stored_down[None],
        velocity_down[None],
        stored_rows[None],
        velocity_rows.T[None],
        stored_norm,
        velocity_norm,
    )


def solution(mesh):
    in_specs = (
        P("replica", None, "tensor"),
        P("replica", "tensor", None),
        P("replica", ("shard", "tensor"), None),
        P("replica", None, None),
        P(("replica", "shard", "tensor"), None),
        P(("replica", "shard", "tensor"), None),
        P("tensor", ("replica", "shard"), None),
        P("tensor", ("replica", "shard"), None),
        P(("shard", "tensor"), "replica", None),
        P(("shard", "tensor"), "replica", None),
        P(),
        P(),
        P(),
    )
    out_specs = (
        P(None, "tensor"),
        P("tensor", None),
        P(("shard", "tensor"), None),
        P(),
        P(("replica", "shard", "tensor"), None),
        P(("replica", "shard", "tensor"), None),
        P("tensor", ("replica", "shard"), None),
        P("tensor", ("replica", "shard"), None),
        P(("shard", "tensor"), "replica", None),
        P(("shard", "tensor"), "replica", None),
        P(),
        P(),
    )
    return jax.shard_map(body, mesh=mesh, in_specs=in_specs, out_specs=out_specs, check_vma=False)
```

```python
import functools

import jax
import jax.numpy as jnp
from jax import lax
from jax.experimental import pallas as pl
from jax.experimental.pallas import tpu as pltpu
from jax.sharding import PartitionSpec as P

F32 = jnp.float32
BF16 = jnp.bfloat16
HIGHEST = lax.Precision.HIGHEST
HBM = pl.BlockSpec(memory_space=pltpu.HBM)
ANY = pl.BlockSpec(memory_space=pl.ANY)
VMEM = pl.BlockSpec(memory_space=pltpu.VMEM)


def outer_step(master, moment, summed, groups):
    difference = master - summed / groups
    velocity = 0.5 * moment + difference
    return (master - 0.7 * (difference + 0.5 * velocity), velocity)


def call(kernel, name, out_shape, in_specs, out_specs, scratch, *operands, limit=24, aliases={}):
    size = sum(x.size * x.dtype.itemsize for x in jax.tree.leaves(out_shape))
    return pl.pallas_call(
        kernel,
        name=name,
        out_shape=out_shape,
        in_specs=in_specs,
        out_specs=out_specs,
        scratch_shapes=scratch,
        input_output_aliases=aliases,
        compiler_params=pltpu.CompilerParams(vmem_limit_bytes=limit * 2**20),
        cost_estimate=pl.CostEstimate(flops=0, bytes_accessed=3 * size, transcendentals=0),
    )(*operands)


OUTER = (0, 3)
INWARD = ((0, 1), (3, 2))
ACROSS = ((1, 2), (2, 1))
OUTWARD = ((1, 0), (2, 3))


def owners():
    pos = lax.axis_index("replica")
    low = pos < 2
    return pos, jnp.bitwise_xor(pos, 1), jnp.where(low, 2, 1), jnp.where(low, 3, 0)


def along(x, pairs):
    return lax.ppermute(x, "replica", pairs)


def swap(x, axis, bit):
    return lax.ppermute(x, axis, [(i, i ^ bit) for i in range(lax.axis_size(axis))])


def bits_down(size):
    bit = size // 2
    while bit:
        yield bit
        bit //= 2


def project_kernel(trained, basis, norm, own, *refs):
    *outs, projected = refs
    rank, rows = basis.shape[0], own.shape[1]
    high = basis[...].astype(BF16)
    rest = basis[...] - high.astype(F32)
    middle = rest.astype(BF16)
    low = (rest - middle.astype(F32)).astype(BF16)
    split = jnp.concatenate([high, middle, low], axis=0)
    product = lax.dot_general(
        split, trained[...], (((1,), (1,)), ((), ())), preferred_element_type=F32
    )
    projected[...] = product[:rank] + (product[rank : 2 * rank] + product[2 * rank :])
    pos = lax.axis_index("replica")
    values = norm[...].astype(F32)
    per = norm.shape[1] // rows
    extra = outs[0].shape[0] - rank
    parts = [
        values[i // per : i // per + 1, (i % per) * rows : (i % per + 1) * rows]
        for i in range(norm.shape[0] * per)
    ]
    parts = jnp.concatenate((parts * extra)[:extra], axis=0).astype(BF16)
    own[...] = projected[:, pl.ds(pl.multiple_of(pos * rows, rows), rows)]
    for mask, out in enumerate(outs, 1):
        owner = jnp.bitwise_xor(pos, mask)
        block = projected[:, pl.ds(pl.multiple_of(owner * rows, rows), rows)]
        out[:rank, :] = block.astype(BF16)
        out[rank:, :] = parts


def embed_kernel(groups, n_came, *refs):
    refs = list(refs)
    own, base, master, moment, basis, norm, master_norm, moment_norm = refs[:8]
    came = refs[8 : 8 + n_came]
    stored, recast, velocity, norm_cast, norm_stored, norm_velocity = refs[-6:]
    rank, rows = own.shape
    total = own[...]
    for ref in came:
        total = total + ref[:rank, :].astype(F32)
    coefficient = base[...] - total / groups
    moved = 0.5 * moment[...] + coefficient
    velocity[...] = moved
    change = lax.dot_general(
        coefficient + 0.5 * moved,
        basis[...],
        (((0,), (0,)), ((), ())),
        precision=HIGHEST,
        preferred_element_type=F32,
    )
    new = master[...] - 0.7 * change
    stored[...] = new
    recast[...] = new.astype(BF16)
    per = norm.shape[1] // rows
    values = norm[...].astype(F32)
    tails = [ref[rank:, :].astype(F32) for ref in came]
    for i in range(norm.shape[0] * per):
        row, span = i // per, slice((i % per) * rows, (i % per + 1) * rows)
        summed = values[row : row + 1, span]
        for tail in tails:
            summed = summed + tail[i : i + 1, :]
        new_norm, moved_norm = outer_step(
            master_norm[row : row + 1, span], moment_norm[row : row + 1, span], summed, groups
        )
        norm_stored[row : row + 1, span] = new_norm
        norm_velocity[row : row + 1, span] = moved_norm
    norm_cast[...] = norm_stored[...].astype(BF16)


def pack_kernel(down, up, *refs):
    *outs, sems = refs
    shard = lax.axis_index("shard")
    rows, width = down.shape[2:]
    tall, cols = up.shape[2:]
    copies = []

    def bring(source, dest):
        copies.append(pltpu.make_async_copy(source, dest, sems.at[len(copies)]))
        copies[-1].start()

    for owner, out in reversed(list(zip(owners(), outs))):
        bring(down.at[owner, shard], out.at[pl.ds(0, rows)])
        for chunk in range(cols // width):
            bring(
                up.at[owner, shard, :, pl.ds(chunk * width, width)],
                out.at[pl.ds(rows + chunk * tall, tall)],
            )
    for copy in copies:
        copy.wait()


def add_kernel(block, came, *refs):
    refs[-1][...] = (block[...].astype(F32) + came[...].astype(F32)).astype(BF16)


def add(block, came, *after):
    return call(
        add_kernel,
        "add_block",
        jax.ShapeDtypeStruct(block.shape, BF16),
        [VMEM] * 2 + [ANY] * len(after),
        VMEM,
        [],
        block,
        came,
        *after,
    )


def pick_kernel(middle, end, *refs):
    out = refs[-1]
    pos = lax.axis_index("replica")
    outer = jnp.logical_or(pos == OUTER[0], pos == OUTER[1])

    @pl.when(outer)
    def _():
        out[...] = end[...]

    @pl.when(jnp.logical_not(outer))
    def _():
        out[...] = middle[...]


def pick(middle, end, *after):
    specs = [VMEM] * 2 + [ANY] * len(after)
    shape = jax.ShapeDtypeStruct(end.shape, end.dtype)
    return call(pick_kernel, "pick", shape, specs, VMEM, [], middle, end, *after)


def total(came, lo, hi):
    value = came[0][lo:hi, :].astype(F32)
    for ref in came[1:]:
        value = value + ref[lo:hi, :].astype(F32)
    return value


def rows_kernel(groups, tensors, n_came, *refs):
    refs = list(refs)
    master_down, moment_down, master_up, moment_up = refs[:4]
    came, state_came = refs[4 : 4 + n_came], refs[4 + n_came : 3 + n_came + tensors]
    piece, master, moment = refs[-3:]
    me = lax.axis_index("tensor")
    rows_down, width = master_down.shape
    rows_up = master_up.shape[0]
    tall, cols = master.shape

    def at(index):
        return pl.ds(pl.multiple_of(index * rows_up, rows_up), rows_up)

    own_cols = pl.ds(pl.multiple_of(me * cols, cols), cols)
    master[at(me), :] = master_up[:, own_cols]
    moment[at(me), :] = moment_up[:, own_cols]
    for shift in range(1, tensors):
        source = lax.rem(me + tensors - shift, tensors)
        master[at(source), :] = state_came[shift - 1][0]
        moment[at(source), :] = state_came[shift - 1][1]
    stored, _ = outer_step(
        master_down[...], moment_down[...], total(came, 0, rows_down), groups
    )
    piece[:rows_down, :] = stored.astype(BF16)
    for chunk in range(cols // width):
        lo = rows_down + chunk * tall
        span = slice(chunk * width, (chunk + 1) * width)
        stored, _ = outer_step(
            master[:, span], moment[:, span], total(came, lo, lo + tall), groups
        )
        piece[lo : lo + tall, :] = stored.astype(BF16)


def states_kernel(groups, tensors, n_came, *refs):
    master_down, moment_down = refs[:2]
    came = refs[2 : 2 + n_came]
    stored_down, velocity_down, *sums, summed = refs[-3 - tensors :]
    rows_down, width = master_down.shape
    rows_up = sums[0].shape[0]
    tall, cols = summed.shape
    me = lax.axis_index("tensor")
    stored, velocity = outer_step(
        master_down[...], moment_down[...], total(came, 0, rows_down), groups
    )
    stored_down[...] = stored
    velocity_down[...] = velocity
    for chunk in range(cols // width):
        lo = rows_down + chunk * tall
        summed[:, chunk * width : (chunk + 1) * width] = total(came, lo, lo + tall)
    for shift in range(tensors):
        owner = lax.rem(me + shift, tensors)
        sums[shift][...] = summed[pl.ds(pl.multiple_of(owner * rows_up, rows_up), rows_up), :]


def up_kernel(groups, tensors, master_up, moment_up, *refs):
    sums, (stored_up, velocity_up, token) = refs[:tensors], refs[-3:]
    cols = sums[0].shape[1]
    me = lax.axis_index("tensor")
    for shift in range(tensors):
        source = lax.rem(me + tensors - shift, tensors)
        span = pl.ds(pl.multiple_of(source * cols, cols), cols)
        stored, velocity = outer_step(
            master_up[:, span], moment_up[:, span], sums[shift][...], groups
        )
        stored_up[:, span] = stored
        velocity_up[:, span] = velocity
    token[...] = jnp.zeros_like(token)


def state_kernel(tensors, master_up, moment_up, *outs):
    me = lax.axis_index("tensor")
    cols = outs[0].shape[2]
    for shift in range(1, tensors):
        target = lax.rem(me + shift, tensors)
        span = pl.ds(pl.multiple_of(target * cols, cols), cols)
        outs[shift - 1][0] = master_up[:, span]
        outs[shift - 1][1] = moment_up[:, span]


def gate_kernel(x, *refs):
    refs[-1][...] = x[...]


def gate(x, *after):
    return call(
        gate_kernel,
        "gate",
        jax.ShapeDtypeStruct(x.shape, x.dtype),
        [VMEM] + [ANY] * len(after),
        VMEM,
        [],
        x,
        *after,
    )


def stack_kernel(count, *refs):
    for i in range(count):
        refs[-1][i] = refs[i][...]


def bundle(pieces, *after):
    return call(
        functools.partial(stack_kernel, len(pieces)),
        "bundle",
        jax.ShapeDtypeStruct((len(pieces),) + pieces[0].shape, BF16),
        [VMEM] * len(pieces) + [ANY] * len(after),
        VMEM,
        [],
        *pieces,
        *after,
    )


def place_kernel(keys, *refs):
    bundles, (down, up, token, sems) = refs[: len(keys)], refs[-4:]
    token[...] = jnp.zeros_like(token)
    shard = lax.axis_index("shard")
    rows, width = down.shape[2:]
    tall, cols = up.shape[2:]
    copies = []

    def send(source, dest):
        copies.append(pltpu.make_async_copy(source, dest, sems.at[len(copies)]))
        copies[-1].start()

    for pieces, (low, slots) in zip(bundles, keys):
        for i, (slot, mask) in enumerate(slots):
            owner, place = owners()[slot], jnp.bitwise_xor(shard, mask ^ low)
            send(pieces.at[i, pl.ds(0, rows)], down.at[owner, place])
            for chunk in range(cols // width):
                send(
                    pieces.at[i, pl.ds(rows + chunk * tall, tall)],
                    up.at[owner, place, :, pl.ds(chunk * width, width)],
                )
    for copy in copies:
        copy.wait()


def place_embed_kernel(slots, *refs):
    pieces, (out, token, sems) = refs[: len(slots)], refs[-3:]
    token[...] = jnp.zeros_like(token)
    copies = [
        pltpu.make_async_copy(piece, out.at[owners()[slot]], sems.at[i])
        for i, (piece, slot) in enumerate(zip(pieces, slots))
    ]
    for copy in copies:
        copy.start()
    for copy in copies:
        copy.wait()


def spread_low(x):
    found = {0: x}
    for bit in bits_down(lax.axis_size("shard") // 2):
        found.update({mask ^ bit: swap(y, "shard", bit) for mask, y in list(found.items())})
    return found


def body(
    trained_up,
    trained_down,
    trained_embed,
    trained_norm,
    master_up,
    moment_up,
    master_down,
    moment_down,
    master_embed,
    moment_embed,
    master_norm,
    moment_norm,
    embed_basis,
):
    replicas = lax.axis_size("replica")
    shards = lax.axis_size("shard")
    tensors = lax.axis_size("tensor")
    width, rank = embed_basis.shape
    rows_up, half_cols = master_up.shape[0], trained_up.shape[2]
    rows_down, rows_embed = master_down.shape[1], master_embed.shape[1]
    tall = tensors * rows_up
    chunks = half_cols // width
    packed = jax.ShapeDtypeStruct((rows_down + chunks * tall, width), BF16)
    dma = pltpu.SemaphoreType.DMA

    basis_t = embed_basis.T
    rank_rows = jax.ShapeDtypeStruct((rank, rows_embed), F32)
    packet = jax.ShapeDtypeStruct((rank + 16, rows_embed), BF16)
    token_shape = jax.ShapeDtypeStruct((8, 128), F32)
    own_rows, *packets = call(
        project_kernel,
        "project_rows",
        [rank_rows] + [packet] * (replicas - 1),
        [VMEM] * 3,
        [VMEM] * replicas,
        [pltpu.VMEM((rank, replicas * rows_embed), F32)],
        pltpu.with_memory_space_constraint(trained_embed[0], pltpu.HBM),
        pltpu.with_memory_space_constraint(basis_t, pltpu.HBM),
        pltpu.with_memory_space_constraint(trained_norm[0], pltpu.HBM),
    )
    down = trained_down[0].reshape(replicas, shards, rows_down, width)
    up = trained_up[0].reshape(replicas, shards, tall, half_cols)
    own, near, middle, end = call(
        pack_kernel,
        "pack_blocks",
        [packed] * replicas,
        [HBM] * 2,
        [VMEM] * replicas,
        [dma((replicas * (1 + chunks),))],
        pltpu.with_memory_space_constraint(down, pltpu.HBM),
        pltpu.with_memory_space_constraint(up, pltpu.HBM),
    )
    packets_came = [swap(packets[0], "replica", 1), swap(packets[1], "replica", 2)]
    end = gate(end, packets_came[0])
    packets_came.append(swap(gate(packets[2], end), "replica", 3))
    from_end = along(end, INWARD)

    state = jax.ShapeDtypeStruct((2, rows_up, half_cols), F32)
    states = call(
        functools.partial(state_kernel, tensors),
        "up_state",
        [state] * (tensors - 1),
        [VMEM] * 2,
        [VMEM] * (tensors - 1),
        [],
        master_up,
        moment_up,
    )
    states = [
        lax.ppermute(x, "tensor", [(i, (i + shift) % tensors) for i in range(tensors)])
        for shift, x in enumerate(states, 1)
    ]

    base = lax.dot_general(
        basis_t, master_embed[0], (((1,), (1,)), ((), ())), precision=HIGHEST
    )
    norm_state = jax.ShapeDtypeStruct(master_norm.shape, F32)
    embed_rows = jax.ShapeDtypeStruct((rows_embed, width), BF16)
    stored_rows, recast_rows, velocity_rows, norm_cast, stored_norm, velocity_norm = call(
        functools.partial(embed_kernel, replicas, replicas - 1),
        "embed_update",
        [
            jax.ShapeDtypeStruct((rows_embed, width), F32),
            embed_rows,
            rank_rows,
            jax.ShapeDtypeStruct(master_norm.shape, BF16),
            norm_state,
            norm_state,
        ],
        [VMEM] * (7 + replicas),
        [VMEM] * 6,
        [],
        own_rows,
        base,
        master_embed[0],
        moment_embed[0].T,
        basis_t,
        trained_norm[0],
        master_norm,
        moment_norm,
        *packets_came,
    )

    embed_out = along(recast_rows, OUTWARD)
    embed_middle = along(recast_rows, ACROSS)
    end_sum = gate(add(end, from_end), embed_middle)
    end_partial = along(end_sum, ACROSS)
    middle_sum = add(middle, along(gate(middle, from_end), INWARD), embed_out)
    middle_partial = along(middle_sum, ACROSS)
    from_near = along(gate(near, middle_sum), INWARD)
    embed_middle_out = along(embed_middle, OUTWARD)
    to_end = along(add(near, end_partial), OUTWARD)
    came0 = [own, from_near, middle_partial, to_end]
    half_sum = jax.ShapeDtypeStruct((rows_up, half_cols), F32)
    down_state = jax.ShapeDtypeStruct((rows_down, width), F32)
    piece = call(
        functools.partial(rows_kernel, replicas, tensors, len(came0)),
        "update_rows",
        packed,
        [VMEM] * (4 + len(came0) + len(states)) + [ANY],
        VMEM,
        [pltpu.VMEM((tall, half_cols), F32)] * 2,
        master_down[0],
        moment_down[0],
        master_up,
        moment_up,
        *came0,
        *states,
        embed_middle_out,
    )

    top = shards // 2
    came_near = swap(piece, "replica", 1)
    middle_piece = along(piece, ACROSS)
    far_piece = swap(piece, "shard", top)
    end_piece = along(came_near, ACROSS)
    second_out = along(middle_piece, OUTWARD)
    near_piece = gate(came_near, far_piece)
    far_near = swap(near_piece, "shard", top)
    stored_down, velocity_down, *sums = call(
        functools.partial(states_kernel, replicas, tensors, len(came0)),
        "update_states",
        [down_state, down_state] + [half_sum] * tensors,
        [VMEM] * (2 + len(came0)) + [ANY],
        [VMEM] * (2 + tensors),
        [pltpu.VMEM((tall, half_cols), F32)],
        master_down[0],
        moment_down[0],
        *came0,
        near_piece,
    )
    sums = [sums[0]] + [
        lax.ppermute(x, "tensor", [(i, (i + shift) % tensors) for i in range(tensors)])
        for shift, x in enumerate(sums[1:], 1)
    ]
    second = pick(middle_piece, second_out, far_near, sums[0])
    far_second = swap(second, "shard", top)
    embed_in = along(gate(recast_rows, near_piece), INWARD)
    embed_end = along(embed_in, ACROSS)
    third = pick(end_piece, along(end_piece, OUTWARD), far_second, embed_end, *sums[1:])
    far_third = swap(third, "shard", top)
    embed_last = along(embed_end, OUTWARD)
    bundles = [
        (
            [(0, 0), (0, top), (1, 0), (1, top)],
            spread_low(bundle([piece, far_piece, near_piece, far_near], third)),
        ),
        (
            [(2, 0), (2, top), (3, 0)],
            spread_low(bundle([second, far_second, third])),
        ),
    ]

    stored_up, velocity_up, token = call(
        functools.partial(up_kernel, replicas, tensors),
        "update_up",
        [jax.ShapeDtypeStruct(master_up.shape, F32)] * 2 + [token_shape],
        [VMEM] * (2 + tensors) + [ANY],
        [VMEM] * 3,
        [],
        master_up,
        moment_up,
        *sums,
        list(bundles[0][1].values())[-1],
    )

    embed_shape = jax.ShapeDtypeStruct((replicas, rows_embed, width), BF16)
    recast_embed, token = call(
        functools.partial(place_embed_kernel, [0, 1, 2]),
        "place_embed",
        [embed_shape, token_shape],
        [VMEM] * 4,
        [HBM, VMEM],
        [dma((3,))],
        recast_rows,
        pick(embed_in, embed_out),
        pick(embed_middle, embed_middle_out),
        token,
    )

    shapes = [jax.ShapeDtypeStruct(down.shape, BF16), jax.ShapeDtypeStruct(up.shape, BF16)]

    def place(slots, arrays, placed, *after):
        keys = [(low, slots) for low in arrays]
        count = len(keys) + len(after)
        return call(
            functools.partial(place_kernel, keys),
            "place_rows",
            shapes + [token_shape],
            [VMEM] * count + [HBM] * len(placed),
            [HBM] * 2 + [VMEM],
            [dma((len(keys) * len(slots) * (1 + chunks),))],
            *arrays.values(),
            *after,
            *placed,
            aliases={count: 0, count + 1: 1} if placed else {},
        )

    placed = []
    for slots, arrays in bundles:
        *placed, token = place(slots, arrays, placed, token)
    last = spread_low(bundle([far_third], token))
    recast_embed, token = call(
        functools.partial(place_embed_kernel, [3]),
        "place_embed",
        [embed_shape, token_shape],
        [VMEM] * 2 + [HBM],
        [HBM, VMEM],
        [dma((1,))],
        pick(embed_end, embed_last),
        last[0],
        recast_embed,
        aliases={2: 0},
    )
    recast_down, recast_up, _ = place([(3, top)], last, placed, token)

    return (
        recast_up.reshape(-1, half_cols),
        recast_down.reshape(-1, width),
        recast_embed.reshape(-1, width),
        norm_cast,
        stored_up,
        velocity_up,
        stored_down[None],
        velocity_down[None],
        stored_rows[None],
        velocity_rows.T[None],
        stored_norm,
        velocity_norm,
    )


def solution(mesh):
    in_specs = (
        P("replica", None, "tensor"),
        P("replica", "tensor", None),
        P("replica", ("shard", "tensor"), None),
        P("replica", None, None),
        P(("replica", "shard", "tensor"), None),
        P(("replica", "shard", "tensor"), None),
        P("tensor", ("replica", "shard"), None),
        P("tensor", ("replica", "shard"), None),
        P(("shard", "tensor"), "replica", None),
        P(("shard", "tensor"), "replica", None),
        P(),
        P(),
        P(),
    )
    out_specs = (
        P(None, "tensor"),
        P("tensor", None),
        P(("shard", "tensor"), None),
        P(),
        P(("replica", "shard", "tensor"), None),
        P(("replica", "shard", "tensor"), None),
        P("tensor", ("replica", "shard"), None),
        P("tensor", ("replica", "shard"), None),
        P(("shard", "tensor"), "replica", None),
        P(("shard", "tensor"), "replica", None),
        P(),
        P(),
    )
    return jax.shard_map(body, mesh=mesh, in_specs=in_specs, out_specs=out_specs, check_vma=False)
```

```python
import functools

import jax
import jax.numpy as jnp
from jax import lax
from jax.experimental import pallas as pl
from jax.experimental.pallas import tpu as pltpu
from jax.sharding import PartitionSpec as P

F32 = jnp.float32
BF16 = jnp.bfloat16
HIGHEST = lax.Precision.HIGHEST
HBM = pl.BlockSpec(memory_space=pltpu.HBM)
ANY = pl.BlockSpec(memory_space=pl.ANY)
VMEM = pl.BlockSpec(memory_space=pltpu.VMEM)


def outer_step(master, moment, summed, groups):
    difference = master - summed / groups
    velocity = 0.5 * moment + difference
    return (master - 0.7 * (difference + 0.5 * velocity), velocity)


def call(kernel, name, out_shape, in_specs, out_specs, scratch, *operands, limit=24, aliases={}):
    size = sum(x.size * x.dtype.itemsize for x in jax.tree.leaves(out_shape))
    return pl.pallas_call(
        kernel,
        name=name,
        out_shape=out_shape,
        in_specs=in_specs,
        out_specs=out_specs,
        scratch_shapes=scratch,
        input_output_aliases=aliases,
        compiler_params=pltpu.CompilerParams(vmem_limit_bytes=limit * 2**20),
        cost_estimate=pl.CostEstimate(flops=0, bytes_accessed=3 * size, transcendentals=0),
    )(*operands)


OUTER = (0, 3)
INWARD = ((0, 1), (3, 2))
ACROSS = ((1, 2), (2, 1))
OUTWARD = ((1, 0), (2, 3))


def owners():
    pos = lax.axis_index("replica")
    low = pos < 2
    return pos, jnp.bitwise_xor(pos, 1), jnp.where(low, 2, 1), jnp.where(low, 3, 0)


def along(x, pairs):
    return lax.ppermute(x, "replica", pairs)


def swap(x, axis, bit):
    return lax.ppermute(x, axis, [(i, i ^ bit) for i in range(lax.axis_size(axis))])


def bits_down(size):
    bit = size // 2
    while bit:
        yield bit
        bit //= 2


def project_kernel(trained, basis, norm, own, *refs):
    *outs, projected = refs
    rank, rows = basis.shape[0], own.shape[1]
    high = basis[...].astype(BF16)
    rest = basis[...] - high.astype(F32)
    middle = rest.astype(BF16)
    low = (rest - middle.astype(F32)).astype(BF16)
    split = jnp.concatenate([high, middle, low], axis=0)
    product = lax.dot_general(
        split, trained[...], (((1,), (1,)), ((), ())), preferred_element_type=F32
    )
    projected[...] = product[:rank] + (product[rank : 2 * rank] + product[2 * rank :])
    pos = lax.axis_index("replica")
    values = norm[...].astype(F32)
    per = norm.shape[1] // rows
    extra = outs[0].shape[0] - rank
    parts = [
        values[i // per : i // per + 1, (i % per) * rows : (i % per + 1) * rows]
        for i in range(norm.shape[0] * per)
    ]
    parts = jnp.concatenate((parts * extra)[:extra], axis=0).astype(BF16)
    own[...] = projected[:, pl.ds(pl.multiple_of(pos * rows, rows), rows)]
    for mask, out in enumerate(outs, 1):
        owner = jnp.bitwise_xor(pos, mask)
        block = projected[:, pl.ds(pl.multiple_of(owner * rows, rows), rows)]
        out[:rank, :] = block.astype(BF16)
        out[rank:, :] = parts


def embed_kernel(groups, n_came, *refs):
    refs = list(refs)
    own, base, master, moment, basis, norm, master_norm, moment_norm = refs[:8]
    came = refs[8 : 8 + n_came]
    stored, recast, velocity, norm_cast, norm_stored, norm_velocity, token = refs[-7:]
    token[...] = jnp.zeros_like(token)
    rank, rows = own.shape
    total = own[...]
    for ref in came:
        total = total + ref[:rank, :].astype(F32)
    coefficient = base[...] - total / groups
    moved = 0.5 * moment[...] + coefficient
    velocity[...] = moved
    change = lax.dot_general(
        coefficient + 0.5 * moved,
        basis[...],
        (((0,), (0,)), ((), ())),
        precision=HIGHEST,
        preferred_element_type=F32,
    )
    new = master[...] - 0.7 * change
    stored[...] = new
    recast[...] = new.astype(BF16)
    per = norm.shape[1] // rows
    values = norm[...].astype(F32)
    tails = [ref[rank:, :].astype(F32) for ref in came]
    for i in range(norm.shape[0] * per):
        row, span = i // per, slice((i % per) * rows, (i % per + 1) * rows)
        summed = values[row : row + 1, span]
        for tail in tails:
            summed = summed + tail[i : i + 1, :]
        new_norm, moved_norm = outer_step(
            master_norm[row : row + 1, span], moment_norm[row : row + 1, span], summed, groups
        )
        norm_stored[row : row + 1, span] = new_norm
        norm_velocity[row : row + 1, span] = moved_norm
    norm_cast[...] = norm_stored[...].astype(BF16)


def pack_kernel(down, up, *refs):
    *outs, sems = refs
    shard = lax.axis_index("shard")
    rows, width = down.shape[2:]
    tall, cols = up.shape[2:]
    copies = []

    def bring(source, dest):
        copies.append(pltpu.make_async_copy(source, dest, sems.at[len(copies)]))
        copies[-1].start()

    for owner, out in reversed(list(zip(owners(), outs))):
        bring(down.at[owner, shard], out.at[pl.ds(0, rows)])
        for chunk in range(cols // width):
            bring(
                up.at[owner, shard, :, pl.ds(chunk * width, width)],
                out.at[pl.ds(rows + chunk * tall, tall)],
            )
    for copy in copies:
        copy.wait()


def add_kernel(block, came, *refs):
    refs[-1][...] = (block[...].astype(F32) + came[...].astype(F32)).astype(BF16)


def add(block, came, *after):
    return call(
        add_kernel,
        "add_block",
        jax.ShapeDtypeStruct(block.shape, BF16),
        [VMEM] * 2 + [ANY] * len(after),
        VMEM,
        [],
        block,
        came,
        *after,
    )


def pick_kernel(middle, end, *refs):
    out = refs[-1]
    pos = lax.axis_index("replica")
    outer = jnp.logical_or(pos == OUTER[0], pos == OUTER[1])

    @pl.when(outer)
    def _():
        out[...] = end[...]

    @pl.when(jnp.logical_not(outer))
    def _():
        out[...] = middle[...]


def pick(middle, end, *after):
    specs = [VMEM] * 2 + [ANY] * len(after)
    shape = jax.ShapeDtypeStruct(end.shape, end.dtype)
    return call(pick_kernel, "pick", shape, specs, VMEM, [], middle, end, *after)


def total(came, lo, hi):
    value = came[0][lo:hi, :].astype(F32)
    for ref in came[1:]:
        value = value + ref[lo:hi, :].astype(F32)
    return value


def rows_kernel(groups, tensors, n_came, *refs):
    refs = list(refs)
    master_down, moment_down, master_up, moment_up = refs[:4]
    came, state_came = refs[4 : 4 + n_came], refs[4 + n_came : 3 + n_came + tensors]
    piece, master, moment = refs[-3:]
    me = lax.axis_index("tensor")
    rows_down, width = master_down.shape
    rows_up = master_up.shape[0]
    tall, cols = master.shape

    def at(index):
        return pl.ds(pl.multiple_of(index * rows_up, rows_up), rows_up)

    own_cols = pl.ds(pl.multiple_of(me * cols, cols), cols)
    master[at(me), :] = master_up[:, own_cols]
    moment[at(me), :] = moment_up[:, own_cols]
    for shift in range(1, tensors):
        source = lax.rem(me + tensors - shift, tensors)
        master[at(source), :] = state_came[shift - 1][0]
        moment[at(source), :] = state_came[shift - 1][1]
    stored, _ = outer_step(
        master_down[...], moment_down[...], total(came, 0, rows_down), groups
    )
    piece[:rows_down, :] = stored.astype(BF16)
    for chunk in range(cols // width):
        lo = rows_down + chunk * tall
        span = slice(chunk * width, (chunk + 1) * width)
        stored, _ = outer_step(
            master[:, span], moment[:, span], total(came, lo, lo + tall), groups
        )
        piece[lo : lo + tall, :] = stored.astype(BF16)


def states_kernel(groups, tensors, n_came, *refs):
    master_down, moment_down = refs[:2]
    came = refs[2 : 2 + n_came]
    stored_down, velocity_down, *sums, summed = refs[-3 - tensors :]
    rows_down, width = master_down.shape
    rows_up = sums[0].shape[0]
    tall, cols = summed.shape
    me = lax.axis_index("tensor")
    stored, velocity = outer_step(
        master_down[...], moment_down[...], total(came, 0, rows_down), groups
    )
    stored_down[...] = stored
    velocity_down[...] = velocity
    for chunk in range(cols // width):
        lo = rows_down + chunk * tall
        summed[:, chunk * width : (chunk + 1) * width] = total(came, lo, lo + tall)
    for shift in range(tensors):
        owner = lax.rem(me + shift, tensors)
        sums[shift][...] = summed[pl.ds(pl.multiple_of(owner * rows_up, rows_up), rows_up), :]


def up_kernel(groups, tensors, master_up, moment_up, *refs):
    sums, (stored_up, velocity_up, token) = refs[:tensors], refs[-3:]
    cols = sums[0].shape[1]
    me = lax.axis_index("tensor")
    for shift in range(tensors):
        source = lax.rem(me + tensors - shift, tensors)
        span = pl.ds(pl.multiple_of(source * cols, cols), cols)
        stored, velocity = outer_step(
            master_up[:, span], moment_up[:, span], sums[shift][...], groups
        )
        stored_up[:, span] = stored
        velocity_up[:, span] = velocity
    token[...] = jnp.zeros_like(token)


def state_kernel(tensors, master_up, moment_up, *outs):
    me = lax.axis_index("tensor")
    cols = outs[0].shape[2]
    for shift in range(1, tensors):
        target = lax.rem(me + shift, tensors)
        span = pl.ds(pl.multiple_of(target * cols, cols), cols)
        outs[shift - 1][0] = master_up[:, span]
        outs[shift - 1][1] = moment_up[:, span]


def gate_kernel(x, *refs):
    refs[-1][...] = x[...]


def gate(x, *after):
    return call(
        gate_kernel,
        "gate",
        jax.ShapeDtypeStruct(x.shape, x.dtype),
        [VMEM] + [ANY] * len(after),
        VMEM,
        [],
        x,
        *after,
    )


def stack_kernel(count, *refs):
    for i in range(count):
        refs[-1][i] = refs[i][...]


def bundle(pieces, *after):
    return call(
        functools.partial(stack_kernel, len(pieces)),
        "bundle",
        jax.ShapeDtypeStruct((len(pieces),) + pieces[0].shape, BF16),
        [VMEM] * len(pieces) + [ANY] * len(after),
        VMEM,
        [],
        *pieces,
        *after,
    )


def place_kernel(keys, *refs):
    bundles, (down, up, token, sems) = refs[: len(keys)], refs[-4:]
    token[...] = jnp.zeros_like(token)
    shard = lax.axis_index("shard")
    rows, width = down.shape[2:]
    tall, cols = up.shape[2:]
    copies = []

    def send(source, dest):
        copies.append(pltpu.make_async_copy(source, dest, sems.at[len(copies)]))
        copies[-1].start()

    for pieces, (low, slots) in zip(bundles, keys):
        for i, (slot, mask) in enumerate(slots):
            owner, place = owners()[slot], jnp.bitwise_xor(shard, mask ^ low)
            send(pieces.at[i, pl.ds(0, rows)], down.at[owner, place])
            for chunk in range(cols // width):
                send(
                    pieces.at[i, pl.ds(rows + chunk * tall, tall)],
                    up.at[owner, place, :, pl.ds(chunk * width, width)],
                )
    for copy in copies:
        copy.wait()


def place_embed_kernel(slots, *refs):
    pieces, (out, token, sems) = refs[: len(slots)], refs[-3:]
    token[...] = jnp.zeros_like(token)
    copies = [
        pltpu.make_async_copy(piece, out.at[owners()[slot]], sems.at[i])
        for i, (piece, slot) in enumerate(zip(pieces, slots))
    ]
    for copy in copies:
        copy.start()
    for copy in copies:
        copy.wait()


def spread_low(x):
    found = {0: x}
    for bit in bits_down(lax.axis_size("shard") // 2):
        found.update({mask ^ bit: swap(y, "shard", bit) for mask, y in list(found.items())})
    return found


def body(
    trained_up,
    trained_down,
    trained_embed,
    trained_norm,
    master_up,
    moment_up,
    master_down,
    moment_down,
    master_embed,
    moment_embed,
    master_norm,
    moment_norm,
    embed_basis,
):
    replicas = lax.axis_size("replica")
    shards = lax.axis_size("shard")
    tensors = lax.axis_size("tensor")
    width, rank = embed_basis.shape
    rows_up, half_cols = master_up.shape[0], trained_up.shape[2]
    rows_down, rows_embed = master_down.shape[1], master_embed.shape[1]
    tall = tensors * rows_up
    chunks = half_cols // width
    packed = jax.ShapeDtypeStruct((rows_down + chunks * tall, width), BF16)
    dma = pltpu.SemaphoreType.DMA

    basis_t = embed_basis.T
    rank_rows = jax.ShapeDtypeStruct((rank, rows_embed), F32)
    packet = jax.ShapeDtypeStruct((rank + 16, rows_embed), BF16)
    own_rows, *packets = call(
        project_kernel,
        "project_rows",
        [rank_rows] + [packet] * (replicas - 1),
        [VMEM] * 3,
        [VMEM] * replicas,
        [pltpu.VMEM((rank, replicas * rows_embed), F32)],
        pltpu.with_memory_space_constraint(trained_embed[0], pltpu.HBM),
        pltpu.with_memory_space_constraint(basis_t, pltpu.HBM),
        pltpu.with_memory_space_constraint(trained_norm[0], pltpu.HBM),
    )
    down = trained_down[0].reshape(replicas, shards, rows_down, width)
    up = trained_up[0].reshape(replicas, shards, tall, half_cols)
    own, near, middle, end = call(
        pack_kernel,
        "pack_blocks",
        [packed] * replicas,
        [HBM] * 2,
        [VMEM] * replicas,
        [dma((replicas * (1 + chunks),))],
        pltpu.with_memory_space_constraint(down, pltpu.HBM),
        pltpu.with_memory_space_constraint(up, pltpu.HBM),
    )
    packets_came = [swap(packets[0], "replica", 1), swap(packets[1], "replica", 2)]
    end = gate(end, packets_came[0])
    packets_came.append(swap(gate(packets[2], end), "replica", 3))
    from_end = along(end, INWARD)

    state = jax.ShapeDtypeStruct((2, rows_up, half_cols), F32)
    states = call(
        functools.partial(state_kernel, tensors),
        "up_state",
        [state] * (tensors - 1),
        [VMEM] * 2,
        [VMEM] * (tensors - 1),
        [],
        master_up,
        moment_up,
    )
    states = [
        lax.ppermute(x, "tensor", [(i, (i + shift) % tensors) for i in range(tensors)])
        for shift, x in enumerate(states, 1)
    ]

    base = lax.dot_general(
        basis_t, master_embed[0], (((1,), (1,)), ((), ())), precision=HIGHEST
    )
    norm_state = jax.ShapeDtypeStruct(master_norm.shape, F32)
    token_shape = jax.ShapeDtypeStruct((8, 128), F32)
    embed_rows = jax.ShapeDtypeStruct((rows_embed, width), BF16)
    stored_rows, recast_rows, velocity_rows, norm_cast, stored_norm, velocity_norm, token = call(
        functools.partial(embed_kernel, replicas, replicas - 1),
        "embed_update",
        [
            jax.ShapeDtypeStruct((rows_embed, width), F32),
            embed_rows,
            rank_rows,
            jax.ShapeDtypeStruct(master_norm.shape, BF16),
            norm_state,
            norm_state,
            token_shape,
        ],
        [VMEM] * (7 + replicas),
        [VMEM] * 7,
        [],
        own_rows,
        base,
        master_embed[0],
        moment_embed[0].T,
        basis_t,
        trained_norm[0],
        master_norm,
        moment_norm,
        *packets_came,
    )

    embed_out = along(recast_rows, OUTWARD)
    embed_middle = along(recast_rows, ACROSS)
    end_sum = gate(add(end, from_end), embed_middle)
    end_partial = along(end_sum, ACROSS)
    middle_sum = add(middle, along(gate(middle, swap(token, "shard", 1)), INWARD), embed_out)
    middle_partial = along(middle_sum, ACROSS)
    from_near = along(gate(near, middle_sum), INWARD)
    embed_middle_out = along(embed_middle, OUTWARD)
    to_end = along(add(near, end_partial, embed_middle_out), OUTWARD)
    came0 = [own, from_near, middle_partial, to_end]
    half_sum = jax.ShapeDtypeStruct((rows_up, half_cols), F32)
    down_state = jax.ShapeDtypeStruct((rows_down, width), F32)
    piece = call(
        functools.partial(rows_kernel, replicas, tensors, len(came0)),
        "update_rows",
        packed,
        [VMEM] * (4 + len(came0) + len(states)),
        VMEM,
        [pltpu.VMEM((tall, half_cols), F32)] * 2,
        master_down[0],
        moment_down[0],
        master_up,
        moment_up,
        *came0,
        *states,
    )

    top = shards // 2
    came_near = swap(piece, "replica", 1)
    middle_piece = along(piece, ACROSS)
    far_piece = swap(piece, "shard", top)
    end_piece = along(came_near, ACROSS)
    second_out = along(middle_piece, OUTWARD)
    near_piece = gate(came_near, far_piece)
    far_near = swap(near_piece, "shard", top)
    stored_down, velocity_down, *sums = call(
        functools.partial(states_kernel, replicas, tensors, len(came0)),
        "update_states",
        [down_state, down_state] + [half_sum] * tensors,
        [VMEM] * (2 + len(came0)) + [ANY],
        [VMEM] * (2 + tensors),
        [pltpu.VMEM((tall, half_cols), F32)],
        master_down[0],
        moment_down[0],
        *came0,
        near_piece,
    )
    sums = [sums[0]] + [
        lax.ppermute(x, "tensor", [(i, (i + shift) % tensors) for i in range(tensors)])
        for shift, x in enumerate(sums[1:], 1)
    ]
    second = pick(middle_piece, second_out, far_near, sums[0])
    far_second = swap(second, "shard", top)
    embed_in = along(gate(recast_rows, near_piece), INWARD)
    embed_end = along(embed_in, ACROSS)
    third = pick(end_piece, along(end_piece, OUTWARD), far_second, embed_end, *sums[1:])
    far_third = swap(third, "shard", top)
    embed_last = along(embed_end, OUTWARD)
    bundles = [
        (
            [(0, 0), (0, top), (1, 0), (1, top)],
            spread_low(bundle([piece, far_piece, near_piece, far_near], third)),
        ),
        (
            [(2, 0), (2, top), (3, 0)],
            spread_low(bundle([second, far_second, third])),
        ),
    ]

    stored_up, velocity_up, token = call(
        functools.partial(up_kernel, replicas, tensors),
        "update_up",
        [jax.ShapeDtypeStruct(master_up.shape, F32)] * 2 + [token_shape],
        [VMEM] * (2 + tensors) + [ANY],
        [VMEM] * 3,
        [],
        master_up,
        moment_up,
        *sums,
        list(bundles[0][1].values())[-1],
    )

    embed_shape = jax.ShapeDtypeStruct((replicas, rows_embed, width), BF16)
    recast_embed, token = call(
        functools.partial(place_embed_kernel, [0, 1, 2]),
        "place_embed",
        [embed_shape, token_shape],
        [VMEM] * 4,
        [HBM, VMEM],
        [dma((3,))],
        recast_rows,
        pick(embed_in, embed_out),
        pick(embed_middle, embed_middle_out),
        token,
    )

    shapes = [jax.ShapeDtypeStruct(down.shape, BF16), jax.ShapeDtypeStruct(up.shape, BF16)]

    def place(slots, arrays, placed, *after):
        keys = [(low, slots) for low in arrays]
        count = len(keys) + len(after)
        return call(
            functools.partial(place_kernel, keys),
            "place_rows",
            shapes + [token_shape],
            [VMEM] * count + [HBM] * len(placed),
            [HBM] * 2 + [VMEM],
            [dma((len(keys) * len(slots) * (1 + chunks),))],
            *arrays.values(),
            *after,
            *placed,
            aliases={count: 0, count + 1: 1} if placed else {},
        )

    placed = []
    for slots, arrays in bundles:
        *placed, token = place(slots, arrays, placed, token)
    last = spread_low(bundle([far_third], token))
    recast_down, recast_up, token = place([(3, top)], last, placed)
    recast_embed, _ = call(
        functools.partial(place_embed_kernel, [3]),
        "place_embed",
        [embed_shape, token_shape],
        [VMEM] * 2 + [HBM],
        [HBM, VMEM],
        [dma((1,))],
        pick(embed_end, embed_last),
        token,
        recast_embed,
        aliases={2: 0},
    )

    return (
        recast_up.reshape(-1, half_cols),
        recast_down.reshape(-1, width),
        recast_embed.reshape(-1, width),
        norm_cast,
        stored_up,
        velocity_up,
        stored_down[None],
        velocity_down[None],
        stored_rows[None],
        velocity_rows.T[None],
        stored_norm,
        velocity_norm,
    )


def solution(mesh):
    in_specs = (
        P("replica", None, "tensor"),
        P("replica", "tensor", None),
        P("replica", ("shard", "tensor"), None),
        P("replica", None, None),
        P(("replica", "shard", "tensor"), None),
        P(("replica", "shard", "tensor"), None),
        P("tensor", ("replica", "shard"), None),
        P("tensor", ("replica", "shard"), None),
        P(("shard", "tensor"), "replica", None),
        P(("shard", "tensor"), "replica", None),
        P(),
        P(),
        P(),
    )
    out_specs = (
        P(None, "tensor"),
        P("tensor", None),
        P(("shard", "tensor"), None),
        P(),
        P(("replica", "shard", "tensor"), None),
        P(("replica", "shard", "tensor"), None),
        P("tensor", ("replica", "shard"), None),
        P("tensor", ("replica", "shard"), None),
        P(("shard", "tensor"), "replica", None),
        P(("shard", "tensor"), "replica", None),
        P(),
        P(),
    )
    return jax.shard_map(body, mesh=mesh, in_specs=in_specs, out_specs=out_specs, check_vma=False)
```

```python
import functools

import jax
import jax.numpy as jnp
from jax import lax
from jax.experimental import pallas as pl
from jax.experimental.pallas import tpu as pltpu
from jax.sharding import PartitionSpec as P

F32 = jnp.float32
BF16 = jnp.bfloat16
HIGHEST = lax.Precision.HIGHEST
HBM = pl.BlockSpec(memory_space=pltpu.HBM)
ANY = pl.BlockSpec(memory_space=pl.ANY)
VMEM = pl.BlockSpec(memory_space=pltpu.VMEM)


def outer_step(master, moment, summed, groups):
    difference = master - summed / groups
    velocity = 0.5 * moment + difference
    return (master - 0.7 * (difference + 0.5 * velocity), velocity)


def call(kernel, name, out_shape, in_specs, out_specs, scratch, *operands, limit=24, aliases={}):
    size = sum(x.size * x.dtype.itemsize for x in jax.tree.leaves(out_shape))
    return pl.pallas_call(
        kernel,
        name=name,
        out_shape=out_shape,
        in_specs=in_specs,
        out_specs=out_specs,
        scratch_shapes=scratch,
        input_output_aliases=aliases,
        compiler_params=pltpu.CompilerParams(vmem_limit_bytes=limit * 2**20),
        cost_estimate=pl.CostEstimate(flops=0, bytes_accessed=3 * size, transcendentals=0),
    )(*operands)


OUTER = (0, 3)
INWARD = ((0, 1), (3, 2))
ACROSS = ((1, 2), (2, 1))
OUTWARD = ((1, 0), (2, 3))


def owners():
    pos = lax.axis_index("replica")
    low = pos < 2
    return pos, jnp.bitwise_xor(pos, 1), jnp.where(low, 2, 1), jnp.where(low, 3, 0)


def along(x, pairs):
    return lax.ppermute(x, "replica", pairs)


def swap(x, axis, bit):
    return lax.ppermute(x, axis, [(i, i ^ bit) for i in range(lax.axis_size(axis))])


def bits_down(size):
    bit = size // 2
    while bit:
        yield bit
        bit //= 2


def project_kernel(trained, basis, norm, own, *refs):
    *outs, projected, held, sems = refs
    rank, rows = basis.shape[0], own.shape[1]
    spans = [slice(i * rows, (i + 1) * rows) for i in range(len(outs) + 1)]
    loads = [
        pltpu.make_async_copy(trained.at[span], held.at[span], sems.at[i])
        for i, span in enumerate(spans)
    ]
    for load in loads:
        load.start()
    high = basis[...].astype(BF16)
    rest = basis[...] - high.astype(F32)
    middle = rest.astype(BF16)
    low = (rest - middle.astype(F32)).astype(BF16)
    split = jnp.concatenate([high, middle, low], axis=0)
    for load, span in zip(loads, spans):
        load.wait()
        product = lax.dot_general(
            split, held[span, :], (((1,), (1,)), ((), ())), preferred_element_type=F32
        )
        projected[:, span] = product[:rank] + (product[rank : 2 * rank] + product[2 * rank :])
    pos = lax.axis_index("replica")
    values = norm[...].astype(F32)
    per = norm.shape[1] // rows
    extra = outs[0].shape[0] - rank
    parts = [
        values[i // per : i // per + 1, (i % per) * rows : (i % per + 1) * rows]
        for i in range(norm.shape[0] * per)
    ]
    parts = jnp.concatenate((parts * extra)[:extra], axis=0).astype(BF16)
    own[...] = projected[:, pl.ds(pl.multiple_of(pos * rows, rows), rows)]
    for mask, out in enumerate(outs, 1):
        owner = jnp.bitwise_xor(pos, mask)
        block = projected[:, pl.ds(pl.multiple_of(owner * rows, rows), rows)]
        out[:rank, :] = block.astype(BF16)
        out[rank:, :] = parts


def embed_kernel(groups, n_came, *refs):
    refs = list(refs)
    own, base, master, moment, basis, norm, master_norm, moment_norm = refs[:8]
    came = refs[8 : 8 + n_came]
    stored, recast, velocity, norm_cast, norm_stored, norm_velocity = refs[-6:]
    rank, rows = own.shape
    total = own[...]
    for ref in came:
        total = total + ref[:rank, :].astype(F32)
    coefficient = base[...] - total / groups
    moved = 0.5 * moment[...] + coefficient
    velocity[...] = moved
    change = lax.dot_general(
        coefficient + 0.5 * moved,
        basis[...],
        (((0,), (0,)), ((), ())),
        precision=HIGHEST,
        preferred_element_type=F32,
    )
    new = master[...] - 0.7 * change
    stored[...] = new
    recast[...] = new.astype(BF16)
    per = norm.shape[1] // rows
    values = norm[...].astype(F32)
    tails = [ref[rank:, :].astype(F32) for ref in came]
    for i in range(norm.shape[0] * per):
        row, span = i // per, slice((i % per) * rows, (i % per + 1) * rows)
        summed = values[row : row + 1, span]
        for tail in tails:
            summed = summed + tail[i : i + 1, :]
        new_norm, moved_norm = outer_step(
            master_norm[row : row + 1, span], moment_norm[row : row + 1, span], summed, groups
        )
        norm_stored[row : row + 1, span] = new_norm
        norm_velocity[row : row + 1, span] = moved_norm
    norm_cast[...] = norm_stored[...].astype(BF16)


def pack_kernel(down, up, *refs):
    *outs, sems = refs
    shard = lax.axis_index("shard")
    rows, width = down.shape[2:]
    tall, cols = up.shape[2:]
    copies = []

    def bring(source, dest):
        copies.append(pltpu.make_async_copy(source, dest, sems.at[len(copies)]))
        copies[-1].start()

    for owner, out in reversed(list(zip(owners(), outs))):
        bring(down.at[owner, shard], out.at[pl.ds(0, rows)])
        for chunk in range(cols // width):
            bring(
                up.at[owner, shard, :, pl.ds(chunk * width, width)],
                out.at[pl.ds(rows + chunk * tall, tall)],
            )
    for copy in copies:
        copy.wait()


def add_kernel(block, came, *refs):
    refs[-1][...] = (block[...].astype(F32) + came[...].astype(F32)).astype(BF16)


def add(block, came, *after):
    return call(
        add_kernel,
        "add_block",
        jax.ShapeDtypeStruct(block.shape, BF16),
        [VMEM] * 2 + [ANY] * len(after),
        VMEM,
        [],
        block,
        came,
        *after,
    )


def pick_kernel(middle, end, *refs):
    out = refs[-1]
    pos = lax.axis_index("replica")
    outer = jnp.logical_or(pos == OUTER[0], pos == OUTER[1])

    @pl.when(outer)
    def _():
        out[...] = end[...]

    @pl.when(jnp.logical_not(outer))
    def _():
        out[...] = middle[...]


def pick(middle, end, *after):
    specs = [VMEM] * 2 + [ANY] * len(after)
    shape = jax.ShapeDtypeStruct(end.shape, end.dtype)
    return call(pick_kernel, "pick", shape, specs, VMEM, [], middle, end, *after)


def total(came, lo, hi):
    value = came[0][lo:hi, :].astype(F32)
    for ref in came[1:]:
        value = value + ref[lo:hi, :].astype(F32)
    return value


def rows_kernel(groups, tensors, n_came, *refs):
    refs = list(refs)
    master_down, moment_down, master_up, moment_up = refs[:4]
    came, state_came = refs[4 : 4 + n_came], refs[4 + n_came : 3 + n_came + tensors]
    piece, master, moment = refs[-3:]
    me = lax.axis_index("tensor")
    rows_down, width = master_down.shape
    rows_up = master_up.shape[0]
    tall, cols = master.shape

    def at(index):
        return pl.ds(pl.multiple_of(index * rows_up, rows_up), rows_up)

    own_cols = pl.ds(pl.multiple_of(me * cols, cols), cols)
    master[at(me), :] = master_up[:, own_cols]
    moment[at(me), :] = moment_up[:, own_cols]
    for shift in range(1, tensors):
        source = lax.rem(me + tensors - shift, tensors)
        master[at(source), :] = state_came[shift - 1][0]
        moment[at(source), :] = state_came[shift - 1][1]
    stored, _ = outer_step(
        master_down[...], moment_down[...], total(came, 0, rows_down), groups
    )
    piece[:rows_down, :] = stored.astype(BF16)
    for chunk in range(cols // width):
        lo = rows_down + chunk * tall
        span = slice(chunk * width, (chunk + 1) * width)
        stored, _ = outer_step(
            master[:, span], moment[:, span], total(came, lo, lo + tall), groups
        )
        piece[lo : lo + tall, :] = stored.astype(BF16)


def states_kernel(groups, tensors, n_came, *refs):
    master_down, moment_down = refs[:2]
    came = refs[2 : 2 + n_came]
    stored_down, velocity_down, *sums, summed = refs[-3 - tensors :]
    rows_down, width = master_down.shape
    rows_up = sums[0].shape[0]
    tall, cols = summed.shape
    me = lax.axis_index("tensor")
    stored, velocity = outer_step(
        master_down[...], moment_down[...], total(came, 0, rows_down), groups
    )
    stored_down[...] = stored
    velocity_down[...] = velocity
    for chunk in range(cols // width):
        lo = rows_down + chunk * tall
        summed[:, chunk * width : (chunk + 1) * width] = total(came, lo, lo + tall)
    for shift in range(tensors):
        owner = lax.rem(me + shift, tensors)
        sums[shift][...] = summed[pl.ds(pl.multiple_of(owner * rows_up, rows_up), rows_up), :]


def up_kernel(groups, tensors, master_up, moment_up, *refs):
    sums, (stored_up, velocity_up, token) = refs[:tensors], refs[-3:]
    cols = sums[0].shape[1]
    me = lax.axis_index("tensor")
    for shift in range(tensors):
        source = lax.rem(me + tensors - shift, tensors)
        span = pl.ds(pl.multiple_of(source * cols, cols), cols)
        stored, velocity = outer_step(
            master_up[:, span], moment_up[:, span], sums[shift][...], groups
        )
        stored_up[:, span] = stored
        velocity_up[:, span] = velocity
    token[...] = jnp.zeros_like(token)


def state_kernel(tensors, master_up, moment_up, *outs):
    me = lax.axis_index("tensor")
    cols = outs[0].shape[2]
    for shift in range(1, tensors):
        target = lax.rem(me + shift, tensors)
        span = pl.ds(pl.multiple_of(target * cols, cols), cols)
        outs[shift - 1][0] = master_up[:, span]
        outs[shift - 1][1] = moment_up[:, span]


def gate_kernel(x, *refs):
    refs[-1][...] = x[...]


def gate(x, *after):
    return call(
        gate_kernel,
        "gate",
        jax.ShapeDtypeStruct(x.shape, x.dtype),
        [VMEM] + [ANY] * len(after),
        VMEM,
        [],
        x,
        *after,
    )


def stack_kernel(count, *refs):
    for i in range(count):
        refs[-1][i] = refs[i][...]


def bundle(pieces, *after):
    return call(
        functools.partial(stack_kernel, len(pieces)),
        "bundle",
        jax.ShapeDtypeStruct((len(pieces),) + pieces[0].shape, BF16),
        [VMEM] * len(pieces) + [ANY] * len(after),
        VMEM,
        [],
        *pieces,
        *after,
    )


def place_kernel(keys, *refs):
    bundles, (down, up, token, sems) = refs[: len(keys)], refs[-4:]
    token[...] = jnp.zeros_like(token)
    shard = lax.axis_index("shard")
    rows, width = down.shape[2:]
    tall, cols = up.shape[2:]
    copies = []

    def send(source, dest):
        copies.append(pltpu.make_async_copy(source, dest, sems.at[len(copies)]))
        copies[-1].start()

    for pieces, (low, slots) in zip(bundles, keys):
        for i, (slot, mask) in enumerate(slots):
            owner, place = owners()[slot], jnp.bitwise_xor(shard, mask ^ low)
            send(pieces.at[i, pl.ds(0, rows)], down.at[owner, place])
            for chunk in range(cols // width):
                send(
                    pieces.at[i, pl.ds(rows + chunk * tall, tall)],
                    up.at[owner, place, :, pl.ds(chunk * width, width)],
                )
    for copy in copies:
        copy.wait()


def place_embed_kernel(slots, *refs):
    pieces, (out, token, sems) = refs[: len(slots)], refs[-3:]
    token[...] = jnp.zeros_like(token)
    copies = [
        pltpu.make_async_copy(piece, out.at[owners()[slot]], sems.at[i])
        for i, (piece, slot) in enumerate(zip(pieces, slots))
    ]
    for copy in copies:
        copy.start()
    for copy in copies:
        copy.wait()


def spread_low(x):
    found = {0: x}
    for bit in bits_down(lax.axis_size("shard") // 2):
        found.update({mask ^ bit: swap(y, "shard", bit) for mask, y in list(found.items())})
    return found


def body(
    trained_up,
    trained_down,
    trained_embed,
    trained_norm,
    master_up,
    moment_up,
    master_down,
    moment_down,
    master_embed,
    moment_embed,
    master_norm,
    moment_norm,
    embed_basis,
):
    replicas = lax.axis_size("replica")
    shards = lax.axis_size("shard")
    tensors = lax.axis_size("tensor")
    width, rank = embed_basis.shape
    rows_up, half_cols = master_up.shape[0], trained_up.shape[2]
    rows_down, rows_embed = master_down.shape[1], master_embed.shape[1]
    tall = tensors * rows_up
    chunks = half_cols // width
    packed = jax.ShapeDtypeStruct((rows_down + chunks * tall, width), BF16)
    dma = pltpu.SemaphoreType.DMA

    basis_t = embed_basis.T
    rank_rows = jax.ShapeDtypeStruct((rank, rows_embed), F32)
    packet = jax.ShapeDtypeStruct((rank + 16, rows_embed), BF16)
    token_shape = jax.ShapeDtypeStruct((8, 128), F32)
    own_rows, *packets = call(
        project_kernel,
        "project_rows",
        [rank_rows] + [packet] * (replicas - 1),
        [HBM] + [VMEM] * 2,
        [VMEM] * replicas,
        [
            pltpu.VMEM((rank, replicas * rows_embed), F32),
            pltpu.VMEM((replicas * rows_embed, width), BF16),
            dma((replicas,)),
        ],
        pltpu.with_memory_space_constraint(trained_embed[0], pltpu.HBM),
        pltpu.with_memory_space_constraint(basis_t, pltpu.HBM),
        pltpu.with_memory_space_constraint(trained_norm[0], pltpu.HBM),
    )
    down = trained_down[0].reshape(replicas, shards, rows_down, width)
    up = trained_up[0].reshape(replicas, shards, tall, half_cols)
    own, near, middle, end = call(
        pack_kernel,
        "pack_blocks",
        [packed] * replicas,
        [HBM] * 2,
        [VMEM] * replicas,
        [dma((replicas * (1 + chunks),))],
        pltpu.with_memory_space_constraint(down, pltpu.HBM),
        pltpu.with_memory_space_constraint(up, pltpu.HBM),
    )
    packets_came = [swap(packets[0], "replica", 1), swap(packets[1], "replica", 2)]
    end = gate(end, packets_came[0])
    packets_came.append(swap(gate(packets[2], end), "replica", 3))
    from_end = along(end, INWARD)

    state = jax.ShapeDtypeStruct((2, rows_up, half_cols), F32)
    states = call(
        functools.partial(state_kernel, tensors),
        "up_state",
        [state] * (tensors - 1),
        [VMEM] * 2,
        [VMEM] * (tensors - 1),
        [],
        master_up,
        moment_up,
    )
    states = [
        lax.ppermute(x, "tensor", [(i, (i + shift) % tensors) for i in range(tensors)])
        for shift, x in enumerate(states, 1)
    ]

    base = lax.dot_general(
        basis_t, master_embed[0], (((1,), (1,)), ((), ())), precision=HIGHEST
    )
    norm_state = jax.ShapeDtypeStruct(master_norm.shape, F32)
    embed_rows = jax.ShapeDtypeStruct((rows_embed, width), BF16)
    stored_rows, recast_rows, velocity_rows, norm_cast, stored_norm, velocity_norm = call(
        functools.partial(embed_kernel, replicas, replicas - 1),
        "embed_update",
        [
            jax.ShapeDtypeStruct((rows_embed, width), F32),
            embed_rows,
            rank_rows,
            jax.ShapeDtypeStruct(master_norm.shape, BF16),
            norm_state,
            norm_state,
        ],
        [VMEM] * (7 + replicas),
        [VMEM] * 6,
        [],
        own_rows,
        base,
        master_embed[0],
        moment_embed[0].T,
        basis_t,
        trained_norm[0],
        master_norm,
        moment_norm,
        *packets_came,
    )

    embed_out = along(recast_rows, OUTWARD)
    embed_middle = along(recast_rows, ACROSS)
    end_sum = gate(add(end, from_end), embed_middle)
    end_partial = along(end_sum, ACROSS)
    middle_sum = add(middle, along(gate(middle, from_end), INWARD), embed_out)
    middle_partial = along(middle_sum, ACROSS)
    from_near = along(gate(near, middle_sum), INWARD)
    embed_middle_out = along(embed_middle, OUTWARD)
    to_end = along(add(near, end_partial), OUTWARD)
    came0 = [own, from_near, middle_partial, to_end]
    half_sum = jax.ShapeDtypeStruct((rows_up, half_cols), F32)
    down_state = jax.ShapeDtypeStruct((rows_down, width), F32)
    piece = call(
        functools.partial(rows_kernel, replicas, tensors, len(came0)),
        "update_rows",
        packed,
        [VMEM] * (4 + len(came0) + len(states)) + [ANY],
        VMEM,
        [pltpu.VMEM((tall, half_cols), F32)] * 2,
        master_down[0],
        moment_down[0],
        master_up,
        moment_up,
        *came0,
        *states,
        embed_middle_out,
    )

    top = shards // 2
    came_near = swap(piece, "replica", 1)
    middle_piece = along(piece, ACROSS)
    far_piece = swap(piece, "shard", top)
    end_piece = along(came_near, ACROSS)
    second_out = along(middle_piece, OUTWARD)
    near_piece = gate(came_near, far_piece)
    far_near = swap(near_piece, "shard", top)
    stored_down, velocity_down, *sums = call(
        functools.partial(states_kernel, replicas, tensors, len(came0)),
        "update_states",
        [down_state, down_state] + [half_sum] * tensors,
        [VMEM] * (2 + len(came0)) + [ANY],
        [VMEM] * (2 + tensors),
        [pltpu.VMEM((tall, half_cols), F32)],
        master_down[0],
        moment_down[0],
        *came0,
        near_piece,
    )
    sums = [sums[0]] + [
        lax.ppermute(x, "tensor", [(i, (i + shift) % tensors) for i in range(tensors)])
        for shift, x in enumerate(sums[1:], 1)
    ]
    second = pick(middle_piece, second_out, far_near, sums[0])
    far_second = swap(second, "shard", top)
    embed_in = along(gate(recast_rows, near_piece), INWARD)
    embed_end = along(embed_in, ACROSS)
    third = pick(end_piece, along(end_piece, OUTWARD), far_second, embed_end, *sums[1:])
    far_third = swap(third, "shard", top)
    embed_last = along(embed_end, OUTWARD)
    bundles = [
        (
            [(0, 0), (0, top), (1, 0), (1, top)],
            spread_low(bundle([piece, far_piece, near_piece, far_near], third)),
        ),
        (
            [(2, 0), (2, top), (3, 0)],
            spread_low(bundle([second, far_second, third])),
        ),
    ]

    stored_up, velocity_up, token = call(
        functools.partial(up_kernel, replicas, tensors),
        "update_up",
        [jax.ShapeDtypeStruct(master_up.shape, F32)] * 2 + [token_shape],
        [VMEM] * (2 + tensors) + [ANY],
        [VMEM] * 3,
        [],
        master_up,
        moment_up,
        *sums,
        list(bundles[0][1].values())[-1],
    )

    embed_shape = jax.ShapeDtypeStruct((replicas, rows_embed, width), BF16)
    recast_embed, token = call(
        functools.partial(place_embed_kernel, [0, 1, 2]),
        "place_embed",
        [embed_shape, token_shape],
        [VMEM] * 4,
        [HBM, VMEM],
        [dma((3,))],
        recast_rows,
        pick(embed_in, embed_out),
        pick(embed_middle, embed_middle_out),
        token,
    )

    shapes = [jax.ShapeDtypeStruct(down.shape, BF16), jax.ShapeDtypeStruct(up.shape, BF16)]

    def place(slots, arrays, placed, *after):
        keys = [(low, slots) for low in arrays]
        count = len(keys) + len(after)
        return call(
            functools.partial(place_kernel, keys),
            "place_rows",
            shapes + [token_shape],
            [VMEM] * count + [HBM] * len(placed),
            [HBM] * 2 + [VMEM],
            [dma((len(keys) * len(slots) * (1 + chunks),))],
            *arrays.values(),
            *after,
            *placed,
            aliases={count: 0, count + 1: 1} if placed else {},
        )

    placed = []
    for slots, arrays in bundles:
        *placed, token = place(slots, arrays, placed, token)
    last = spread_low(bundle([far_third], token))
    recast_embed, token = call(
        functools.partial(place_embed_kernel, [3]),
        "place_embed",
        [embed_shape, token_shape],
        [VMEM] * 2 + [HBM],
        [HBM, VMEM],
        [dma((1,))],
        pick(embed_end, embed_last),
        last[0],
        recast_embed,
        aliases={2: 0},
    )
    recast_down, recast_up, _ = place([(3, top)], last, placed, token)

    return (
        recast_up.reshape(-1, half_cols),
        recast_down.reshape(-1, width),
        recast_embed.reshape(-1, width),
        norm_cast,
        stored_up,
        velocity_up,
        stored_down[None],
        velocity_down[None],
        stored_rows[None],
        velocity_rows.T[None],
        stored_norm,
        velocity_norm,
    )


def solution(mesh):
    in_specs = (
        P("replica", None, "tensor"),
        P("replica", "tensor", None),
        P("replica", ("shard", "tensor"), None),
        P("replica", None, None),
        P(("replica", "shard", "tensor"), None),
        P(("replica", "shard", "tensor"), None),
        P("tensor", ("replica", "shard"), None),
        P("tensor", ("replica", "shard"), None),
        P(("shard", "tensor"), "replica", None),
        P(("shard", "tensor"), "replica", None),
        P(),
        P(),
        P(),
    )
    out_specs = (
        P(None, "tensor"),
        P("tensor", None),
        P(("shard", "tensor"), None),
        P(),
        P(("replica", "shard", "tensor"), None),
        P(("replica", "shard", "tensor"), None),
        P("tensor", ("replica", "shard"), None),
        P("tensor", ("replica", "shard"), None),
        P(("shard", "tensor"), "replica", None),
        P(("shard", "tensor"), "replica", None),
        P(),
        P(),
    )
    return jax.shard_map(body, mesh=mesh, in_specs=in_specs, out_specs=out_specs, check_vma=False)
```

```python
import functools

import jax
import jax.numpy as jnp
from jax import lax
from jax.experimental import pallas as pl
from jax.experimental.pallas import tpu as pltpu
from jax.sharding import PartitionSpec as P

F32 = jnp.float32
BF16 = jnp.bfloat16
HIGHEST = lax.Precision.HIGHEST
HBM = pl.BlockSpec(memory_space=pltpu.HBM)
ANY = pl.BlockSpec(memory_space=pl.ANY)
VMEM = pl.BlockSpec(memory_space=pltpu.VMEM)


def outer_step(master, moment, summed, groups):
    difference = master - summed / groups
    velocity = 0.5 * moment + difference
    return (master - 0.7 * (difference + 0.5 * velocity), velocity)


def call(kernel, name, out_shape, in_specs, out_specs, scratch, *operands, limit=24, aliases={}):
    size = sum(x.size * x.dtype.itemsize for x in jax.tree.leaves(out_shape))
    return pl.pallas_call(
        kernel,
        name=name,
        out_shape=out_shape,
        in_specs=in_specs,
        out_specs=out_specs,
        scratch_shapes=scratch,
        input_output_aliases=aliases,
        compiler_params=pltpu.CompilerParams(vmem_limit_bytes=limit * 2**20),
        cost_estimate=pl.CostEstimate(flops=0, bytes_accessed=3 * size, transcendentals=0),
    )(*operands)


OUTER = (0, 3)
INWARD = ((0, 1), (3, 2))
ACROSS = ((1, 2), (2, 1))
OUTWARD = ((1, 0), (2, 3))


def owners():
    pos = lax.axis_index("replica")
    low = pos < 2
    return pos, jnp.bitwise_xor(pos, 1), jnp.where(low, 2, 1), jnp.where(low, 3, 0)


def along(x, pairs):
    return lax.ppermute(x, "replica", pairs)


def swap(x, axis, bit):
    return lax.ppermute(x, axis, [(i, i ^ bit) for i in range(lax.axis_size(axis))])


def bits_down(size):
    bit = size // 2
    while bit:
        yield bit
        bit //= 2


def project_kernel(trained, basis, norm, own, *refs):
    *outs, projected = refs
    rank, rows = basis.shape[0], own.shape[1]
    high = basis[...].astype(BF16)
    rest = basis[...] - high.astype(F32)
    middle = rest.astype(BF16)
    low = (rest - middle.astype(F32)).astype(BF16)
    split = jnp.concatenate([high, middle, low], axis=0)
    product = lax.dot_general(
        split, trained[...], (((1,), (1,)), ((), ())), preferred_element_type=F32
    )
    projected[...] = product[:rank] + (product[rank : 2 * rank] + product[2 * rank :])
    pos = lax.axis_index("replica")
    values = norm[...].astype(F32)
    per = norm.shape[1] // rows
    extra = outs[0].shape[0] - rank
    parts = [
        values[i // per : i // per + 1, (i % per) * rows : (i % per + 1) * rows]
        for i in range(norm.shape[0] * per)
    ]
    parts = jnp.concatenate((parts * extra)[:extra], axis=0).astype(BF16)
    own[...] = projected[:, pl.ds(pl.multiple_of(pos * rows, rows), rows)]
    for mask, out in enumerate(outs, 1):
        owner = jnp.bitwise_xor(pos, mask)
        block = projected[:, pl.ds(pl.multiple_of(owner * rows, rows), rows)]
        out[:rank, :] = block.astype(BF16)
        out[rank:, :] = parts


def embed_kernel(groups, n_came, *refs):
    refs = list(refs)
    own, base, master, moment, basis, norm, master_norm, moment_norm = refs[:8]
    came = refs[8 : 8 + n_came]
    stored, recast, velocity, norm_cast, norm_stored, norm_velocity = refs[-6:]
    rank, rows = own.shape
    total = own[...]
    for ref in came:
        total = total + ref[:rank, :].astype(F32)
    coefficient = base[...] - total / groups
    moved = 0.5 * moment[...] + coefficient
    velocity[...] = moved
    change = lax.dot_general(
        coefficient + 0.5 * moved,
        basis[...],
        (((0,), (0,)), ((), ())),
        precision=HIGHEST,
        preferred_element_type=F32,
    )
    new = master[...] - 0.7 * change
    stored[...] = new
    recast[...] = new.astype(BF16)
    per = norm.shape[1] // rows
    values = norm[...].astype(F32)
    tails = [ref[rank:, :].astype(F32) for ref in came]
    for i in range(norm.shape[0] * per):
        row, span = i // per, slice((i % per) * rows, (i % per + 1) * rows)
        summed = values[row : row + 1, span]
        for tail in tails:
            summed = summed + tail[i : i + 1, :]
        new_norm, moved_norm = outer_step(
            master_norm[row : row + 1, span], moment_norm[row : row + 1, span], summed, groups
        )
        norm_stored[row : row + 1, span] = new_norm
        norm_velocity[row : row + 1, span] = moved_norm
    norm_cast[...] = norm_stored[...].astype(BF16)


def pack_kernel(down, up, *refs):
    *outs, sems = refs
    shard = lax.axis_index("shard")
    rows, width = down.shape[2:]
    tall, cols = up.shape[2:]
    copies = []

    def bring(source, dest):
        copies.append(pltpu.make_async_copy(source, dest, sems.at[len(copies)]))
        copies[-1].start()

    for owner, out in reversed(list(zip(owners(), outs))):
        bring(down.at[owner, shard], out.at[pl.ds(0, rows)])
        for chunk in range(cols // width):
            bring(
                up.at[owner, shard, :, pl.ds(chunk * width, width)],
                out.at[pl.ds(rows + chunk * tall, tall)],
            )
    for copy in copies:
        copy.wait()


def add_kernel(block, came, *refs):
    refs[-1][...] = (block[...].astype(F32) + came[...].astype(F32)).astype(BF16)


def add(block, came, *after):
    return call(
        add_kernel,
        "add_block",
        jax.ShapeDtypeStruct(block.shape, BF16),
        [VMEM] * 2 + [ANY] * len(after),
        VMEM,
        [],
        block,
        came,
        *after,
    )


def pick_kernel(middle, end, *refs):
    out = refs[-1]
    pos = lax.axis_index("replica")
    outer = jnp.logical_or(pos == OUTER[0], pos == OUTER[1])

    @pl.when(outer)
    def _():
        out[...] = end[...]

    @pl.when(jnp.logical_not(outer))
    def _():
        out[...] = middle[...]


def pick(middle, end, *after):
    specs = [VMEM] * 2 + [ANY] * len(after)
    shape = jax.ShapeDtypeStruct(end.shape, end.dtype)
    return call(pick_kernel, "pick", shape, specs, VMEM, [], middle, end, *after)


def total(came, lo, hi):
    value = came[0][lo:hi, :].astype(F32)
    for ref in came[1:]:
        value = value + ref[lo:hi, :].astype(F32)
    return value


def rows_kernel(groups, tensors, n_came, *refs):
    refs = list(refs)
    master_down, moment_down, master_up, moment_up = refs[:4]
    came, state_came = refs[4 : 4 + n_came], refs[4 + n_came : 3 + n_came + tensors]
    piece, master, moment = refs[-3:]
    me = lax.axis_index("tensor")
    rows_down, width = master_down.shape
    rows_up = master_up.shape[0]
    tall, cols = master.shape

    def at(index):
        return pl.ds(pl.multiple_of(index * rows_up, rows_up), rows_up)

    own_cols = pl.ds(pl.multiple_of(me * cols, cols), cols)
    master[at(me), :] = master_up[:, own_cols]
    moment[at(me), :] = moment_up[:, own_cols]
    for shift in range(1, tensors):
        source = lax.rem(me + tensors - shift, tensors)
        master[at(source), :] = state_came[shift - 1][0]
        moment[at(source), :] = state_came[shift - 1][1]
    stored, _ = outer_step(
        master_down[...], moment_down[...], total(came, 0, rows_down), groups
    )
    piece[:rows_down, :] = stored.astype(BF16)
    for chunk in range(cols // width):
        lo = rows_down + chunk * tall
        span = slice(chunk * width, (chunk + 1) * width)
        stored, _ = outer_step(
            master[:, span], moment[:, span], total(came, lo, lo + tall), groups
        )
        piece[lo : lo + tall, :] = stored.astype(BF16)


def states_kernel(groups, tensors, n_came, *refs):
    master_down, moment_down = refs[:2]
    came = refs[2 : 2 + n_came]
    stored_down, velocity_down, *sums, summed = refs[-3 - tensors :]
    rows_down, width = master_down.shape
    rows_up = sums[0].shape[0]
    tall, cols = summed.shape
    me = lax.axis_index("tensor")
    stored, velocity = outer_step(
        master_down[...], moment_down[...], total(came, 0, rows_down), groups
    )
    stored_down[...] = stored
    velocity_down[...] = velocity
    for chunk in range(cols // width):
        lo = rows_down + chunk * tall
        summed[:, chunk * width : (chunk + 1) * width] = total(came, lo, lo + tall)
    for shift in range(tensors):
        owner = lax.rem(me + shift, tensors)
        sums[shift][...] = summed[pl.ds(pl.multiple_of(owner * rows_up, rows_up), rows_up), :]


def up_kernel(groups, tensors, master_up, moment_up, *refs):
    sums, (stored_up, velocity_up, token) = refs[:tensors], refs[-3:]
    cols = sums[0].shape[1]
    me = lax.axis_index("tensor")
    for shift in range(tensors):
        source = lax.rem(me + tensors - shift, tensors)
        span = pl.ds(pl.multiple_of(source * cols, cols), cols)
        stored, velocity = outer_step(
            master_up[:, span], moment_up[:, span], sums[shift][...], groups
        )
        stored_up[:, span] = stored
        velocity_up[:, span] = velocity
    token[...] = jnp.zeros_like(token)


def state_kernel(tensors, master_up, moment_up, *outs):
    me = lax.axis_index("tensor")
    cols = outs[0].shape[2]
    for shift in range(1, tensors):
        target = lax.rem(me + shift, tensors)
        span = pl.ds(pl.multiple_of(target * cols, cols), cols)
        outs[shift - 1][0] = master_up[:, span]
        outs[shift - 1][1] = moment_up[:, span]


def gate_kernel(x, *refs):
    refs[-1][...] = x[...]


def gate(x, *after):
    return call(
        gate_kernel,
        "gate",
        jax.ShapeDtypeStruct(x.shape, x.dtype),
        [VMEM] + [ANY] * len(after),
        VMEM,
        [],
        x,
        *after,
    )


def stack_kernel(count, *refs):
    for i in range(count):
        refs[-1][i] = refs[i][...]


def bundle(pieces, *after):
    return call(
        functools.partial(stack_kernel, len(pieces)),
        "bundle",
        jax.ShapeDtypeStruct((len(pieces),) + pieces[0].shape, BF16),
        [VMEM] * len(pieces) + [ANY] * len(after),
        VMEM,
        [],
        *pieces,
        *after,
    )


def place_kernel(keys, *refs):
    bundles, (down, up, token, sems) = refs[: len(keys)], refs[-4:]
    token[...] = jnp.zeros_like(token)
    shard = lax.axis_index("shard")
    rows, width = down.shape[2:]
    tall, cols = up.shape[2:]
    copies = []

    def send(source, dest):
        copies.append(pltpu.make_async_copy(source, dest, sems.at[len(copies)]))
        copies[-1].start()

    for pieces, (low, slots) in zip(bundles, keys):
        for i, (slot, mask) in enumerate(slots):
            owner, place = owners()[slot], jnp.bitwise_xor(shard, mask ^ low)
            send(pieces.at[i, pl.ds(0, rows)], down.at[owner, place])
            for chunk in range(cols // width):
                send(
                    pieces.at[i, pl.ds(rows + chunk * tall, tall)],
                    up.at[owner, place, :, pl.ds(chunk * width, width)],
                )
    for copy in copies:
        copy.wait()


def place_embed_kernel(slots, *refs):
    pieces, (out, token, sems) = refs[: len(slots)], refs[-3:]
    token[...] = jnp.zeros_like(token)
    copies = [
        pltpu.make_async_copy(piece, out.at[owners()[slot]], sems.at[i])
        for i, (piece, slot) in enumerate(zip(pieces, slots))
    ]
    for copy in copies:
        copy.start()
    for copy in copies:
        copy.wait()


def spread_low(x):
    found = {0: x}
    for bit in bits_down(lax.axis_size("shard") // 2):
        found.update({mask ^ bit: swap(y, "shard", bit) for mask, y in list(found.items())})
    return found


def body(
    trained_up,
    trained_down,
    trained_embed,
    trained_norm,
    master_up,
    moment_up,
    master_down,
    moment_down,
    master_embed,
    moment_embed,
    master_norm,
    moment_norm,
    embed_basis,
):
    replicas = lax.axis_size("replica")
    shards = lax.axis_size("shard")
    tensors = lax.axis_size("tensor")
    width, rank = embed_basis.shape
    rows_up, half_cols = master_up.shape[0], trained_up.shape[2]
    rows_down, rows_embed = master_down.shape[1], master_embed.shape[1]
    tall = tensors * rows_up
    chunks = half_cols // width
    packed = jax.ShapeDtypeStruct((rows_down + chunks * tall, width), BF16)
    dma = pltpu.SemaphoreType.DMA

    basis_t = embed_basis.T
    rank_rows = jax.ShapeDtypeStruct((rank, rows_embed), F32)
    packet = jax.ShapeDtypeStruct((rank + 16, rows_embed), BF16)
    token_shape = jax.ShapeDtypeStruct((8, 128), F32)
    own_rows, *packets = call(
        project_kernel,
        "project_rows",
        [rank_rows] + [packet] * (replicas - 1),
        [VMEM] * 3,
        [VMEM] * replicas,
        [pltpu.VMEM((rank, replicas * rows_embed), F32)],
        pltpu.with_memory_space_constraint(trained_embed[0], pltpu.HBM),
        pltpu.with_memory_space_constraint(basis_t, pltpu.HBM),
        pltpu.with_memory_space_constraint(trained_norm[0], pltpu.HBM),
    )
    down = trained_down[0].reshape(replicas, shards, rows_down, width)
    up = trained_up[0].reshape(replicas, shards, tall, half_cols)
    own, near, middle, end = call(
        pack_kernel,
        "pack_blocks",
        [packed] * replicas,
        [HBM] * 2,
        [VMEM] * replicas,
        [dma((replicas * (1 + chunks),))],
        pltpu.with_memory_space_constraint(down, pltpu.HBM),
        pltpu.with_memory_space_constraint(up, pltpu.HBM),
    )
    packets_came = [swap(packets[0], "replica", 1), swap(packets[1], "replica", 2)]
    end = gate(end, packets_came[0])
    packets_came.append(swap(gate(packets[2], end), "replica", 3))
    from_end = along(end, INWARD)

    state = jax.ShapeDtypeStruct((2, rows_up, half_cols), F32)
    states = call(
        functools.partial(state_kernel, tensors),
        "up_state",
        [state] * (tensors - 1),
        [VMEM] * 2,
        [VMEM] * (tensors - 1),
        [],
        master_up,
        moment_up,
    )
    states = [
        lax.ppermute(x, "tensor", [(i, (i + shift) % tensors) for i in range(tensors)])
        for shift, x in enumerate(states, 1)
    ]

    base = lax.dot_general(
        basis_t, master_embed[0], (((1,), (1,)), ((), ())), precision=HIGHEST
    )
    norm_state = jax.ShapeDtypeStruct(master_norm.shape, F32)
    embed_rows = jax.ShapeDtypeStruct((rows_embed, width), BF16)
    stored_rows, recast_rows, velocity_rows, norm_cast, stored_norm, velocity_norm = call(
        functools.partial(embed_kernel, replicas, replicas - 1),
        "embed_update",
        [
            jax.ShapeDtypeStruct((rows_embed, width), F32),
            embed_rows,
            rank_rows,
            jax.ShapeDtypeStruct(master_norm.shape, BF16),
            norm_state,
            norm_state,
        ],
        [VMEM] * (7 + replicas),
        [VMEM] * 6,
        [],
        own_rows,
        base,
        master_embed[0],
        moment_embed[0].T,
        basis_t,
        trained_norm[0],
        master_norm,
        moment_norm,
        *packets_came,
    )

    embed_out = along(recast_rows, OUTWARD)
    embed_middle = along(recast_rows, ACROSS)
    end_sum = gate(add(end, from_end), embed_middle)
    end_partial = along(end_sum, ACROSS)
    middle_sum = add(middle, along(gate(middle, from_end), INWARD), embed_out)
    middle_partial = along(middle_sum, ACROSS)
    from_near = along(gate(near, middle_sum), INWARD)
    embed_middle_out = along(embed_middle, OUTWARD)
    to_end = along(add(near, end_partial), OUTWARD)
    came0 = [own, from_near, middle_partial, to_end]
    half_sum = jax.ShapeDtypeStruct((rows_up, half_cols), F32)
    down_state = jax.ShapeDtypeStruct((rows_down, width), F32)
    piece = call(
        functools.partial(rows_kernel, replicas, tensors, len(came0)),
        "update_rows",
        packed,
        [VMEM] * (4 + len(came0) + len(states)) + [ANY],
        VMEM,
        [pltpu.VMEM((tall, half_cols), F32)] * 2,
        master_down[0],
        moment_down[0],
        master_up,
        moment_up,
        *came0,
        *states,
        embed_middle_out,
    )

    top = shards // 2
    came_near = swap(piece, "replica", 1)
    middle_piece = along(piece, ACROSS)
    far_piece = swap(piece, "shard", top)
    end_piece = along(came_near, ACROSS)
    second_out = along(middle_piece, OUTWARD)
    near_piece = gate(came_near, far_piece)
    far_near = swap(near_piece, "shard", top)
    stored_down, velocity_down, *sums = call(
        functools.partial(states_kernel, replicas, tensors, len(came0)),
        "update_states",
        [down_state, down_state] + [half_sum] * tensors,
        [VMEM] * (2 + len(came0)) + [ANY],
        [VMEM] * (2 + tensors),
        [pltpu.VMEM((tall, half_cols), F32)],
        master_down[0],
        moment_down[0],
        *came0,
        near_piece,
    )
    sums = [sums[0]] + [
        lax.ppermute(x, "tensor", [(i, (i + shift) % tensors) for i in range(tensors)])
        for shift, x in enumerate(sums[1:], 1)
    ]
    second = pick(middle_piece, second_out, far_near, sums[0])
    far_second = swap(second, "shard", top)
    embed_in = along(gate(recast_rows, near_piece), INWARD)
    embed_end = along(embed_in, ACROSS)
    third = pick(end_piece, along(end_piece, OUTWARD), far_second, embed_end, *sums[1:])
    far_third = swap(third, "shard", top)
    embed_last = along(embed_end, OUTWARD)
    bundles = [
        (
            [(0, 0), (0, top), (1, 0), (1, top), (2, 0), (2, top), (3, 0)],
            spread_low(
                bundle([piece, far_piece, near_piece, far_near, second, far_second, third])
            ),
        ),
    ]

    stored_up, velocity_up, token = call(
        functools.partial(up_kernel, replicas, tensors),
        "update_up",
        [jax.ShapeDtypeStruct(master_up.shape, F32)] * 2 + [token_shape],
        [VMEM] * (2 + tensors) + [ANY],
        [VMEM] * 3,
        [],
        master_up,
        moment_up,
        *sums,
        list(bundles[0][1].values())[-1],
    )

    embed_shape = jax.ShapeDtypeStruct((replicas, rows_embed, width), BF16)
    recast_embed, token = call(
        functools.partial(place_embed_kernel, [0, 1, 2]),
        "place_embed",
        [embed_shape, token_shape],
        [VMEM] * 4,
        [HBM, VMEM],
        [dma((3,))],
        recast_rows,
        pick(embed_in, embed_out),
        pick(embed_middle, embed_middle_out),
        token,
    )

    shapes = [jax.ShapeDtypeStruct(down.shape, BF16), jax.ShapeDtypeStruct(up.shape, BF16)]

    def place(slots, arrays, placed, *after):
        keys = [(low, slots) for low in arrays]
        count = len(keys) + len(after)
        return call(
            functools.partial(place_kernel, keys),
            "place_rows",
            shapes + [token_shape],
            [VMEM] * count + [HBM] * len(placed),
            [HBM] * 2 + [VMEM],
            [dma((len(keys) * len(slots) * (1 + chunks),))],
            *arrays.values(),
            *after,
            *placed,
            aliases={count: 0, count + 1: 1} if placed else {},
        )

    placed = []
    for slots, arrays in bundles:
        *placed, token = place(slots, arrays, placed, token)
    last = spread_low(bundle([far_third], token))
    recast_embed, token = call(
        functools.partial(place_embed_kernel, [3]),
        "place_embed",
        [embed_shape, token_shape],
        [VMEM] * 2 + [HBM],
        [HBM, VMEM],
        [dma((1,))],
        pick(embed_end, embed_last),
        last[0],
        recast_embed,
        aliases={2: 0},
    )
    recast_down, recast_up, _ = place([(3, top)], last, placed, token)

    return (
        recast_up.reshape(-1, half_cols),
        recast_down.reshape(-1, width),
        recast_embed.reshape(-1, width),
        norm_cast,
        stored_up,
        velocity_up,
        stored_down[None],
        velocity_down[None],
        stored_rows[None],
        velocity_rows.T[None],
        stored_norm,
        velocity_norm,
    )


def solution(mesh):
    in_specs = (
        P("replica", None, "tensor"),
        P("replica", "tensor", None),
        P("replica", ("shard", "tensor"), None),
        P("replica", None, None),
        P(("replica", "shard", "tensor"), None),
        P(("replica", "shard", "tensor"), None),
        P("tensor", ("replica", "shard"), None),
        P("tensor", ("replica", "shard"), None),
        P(("shard", "tensor"), "replica", None),
        P(("shard", "tensor"), "replica", None),
        P(),
        P(),
        P(),
    )
    out_specs = (
        P(None, "tensor"),
        P("tensor", None),
        P(("shard", "tensor"), None),
        P(),
        P(("replica", "shard", "tensor"), None),
        P(("replica", "shard", "tensor"), None),
        P("tensor", ("replica", "shard"), None),
        P("tensor", ("replica", "shard"), None),
        P(("shard", "tensor"), "replica", None),
        P(("shard", "tensor"), "replica", None),
        P(),
        P(),
    )
    return jax.shard_map(body, mesh=mesh, in_specs=in_specs, out_specs=out_specs, check_vma=False)
```

```python
import functools

import jax
import jax.numpy as jnp
from jax import lax
from jax.experimental import pallas as pl
from jax.experimental.pallas import tpu as pltpu
from jax.sharding import PartitionSpec as P

F32 = jnp.float32
BF16 = jnp.bfloat16
HIGHEST = lax.Precision.HIGHEST
HBM = pl.BlockSpec(memory_space=pltpu.HBM)
ANY = pl.BlockSpec(memory_space=pl.ANY)
VMEM = pl.BlockSpec(memory_space=pltpu.VMEM)


def outer_step(master, moment, summed, groups):
    difference = master - summed / groups
    velocity = 0.5 * moment + difference
    return (master - 0.7 * (difference + 0.5 * velocity), velocity)


def call(kernel, name, out_shape, in_specs, out_specs, scratch, *operands, limit=24, aliases={}):
    size = sum(x.size * x.dtype.itemsize for x in jax.tree.leaves(out_shape))
    return pl.pallas_call(
        kernel,
        name=name,
        out_shape=out_shape,
        in_specs=in_specs,
        out_specs=out_specs,
        scratch_shapes=scratch,
        input_output_aliases=aliases,
        compiler_params=pltpu.CompilerParams(vmem_limit_bytes=limit * 2**20),
        cost_estimate=pl.CostEstimate(flops=0, bytes_accessed=3 * size, transcendentals=0),
    )(*operands)


OUTER = (0, 3)
INWARD = ((0, 1), (3, 2))
ACROSS = ((1, 2), (2, 1))
OUTWARD = ((1, 0), (2, 3))


def owners():
    pos = lax.axis_index("replica")
    low = pos < 2
    return pos, jnp.bitwise_xor(pos, 1), jnp.where(low, 2, 1), jnp.where(low, 3, 0)


def along(x, pairs):
    return lax.ppermute(x, "replica", pairs)


def swap(x, axis, bit):
    return lax.ppermute(x, axis, [(i, i ^ bit) for i in range(lax.axis_size(axis))])


def bits_down(size):
    bit = size // 2
    while bit:
        yield bit
        bit //= 2


def project_kernel(trained, basis, norm, own, *refs):
    *outs, projected = refs
    rank, rows = basis.shape[0], own.shape[1]
    high = basis[...].astype(BF16)
    rest = basis[...] - high.astype(F32)
    middle = rest.astype(BF16)
    low = (rest - middle.astype(F32)).astype(BF16)
    split = jnp.concatenate([high, middle, low], axis=0)
    product = lax.dot_general(
        split, trained[...], (((1,), (1,)), ((), ())), preferred_element_type=F32
    )
    projected[...] = product[:rank] + (product[rank : 2 * rank] + product[2 * rank :])
    pos = lax.axis_index("replica")
    values = norm[...].astype(F32)
    per = norm.shape[1] // rows
    extra = outs[0].shape[0] - rank
    parts = [
        values[i // per : i // per + 1, (i % per) * rows : (i % per + 1) * rows]
        for i in range(norm.shape[0] * per)
    ]
    parts = jnp.concatenate((parts * extra)[:extra], axis=0).astype(BF16)
    own[...] = projected[:, pl.ds(pl.multiple_of(pos * rows, rows), rows)]
    for mask, out in enumerate(outs, 1):
        owner = jnp.bitwise_xor(pos, mask)
        block = projected[:, pl.ds(pl.multiple_of(owner * rows, rows), rows)]
        out[:rank, :] = block.astype(BF16)
        out[rank:, :] = parts


def embed_kernel(groups, n_came, *refs):
    refs = list(refs)
    own, base, master, moment, basis, norm, master_norm, moment_norm = refs[:8]
    came = refs[8 : 8 + n_came]
    stored, recast, velocity, norm_cast, norm_stored, norm_velocity = refs[-6:]
    rank, rows = own.shape
    total = own[...]
    for ref in came:
        total = total + ref[:rank, :].astype(F32)
    coefficient = base[...] - total / groups
    moved = 0.5 * moment[...] + coefficient
    velocity[...] = moved
    change = lax.dot_general(
        coefficient + 0.5 * moved,
        basis[...],
        (((0,), (0,)), ((), ())),
        precision=HIGHEST,
        preferred_element_type=F32,
    )
    new = master[...] - 0.7 * change
    stored[...] = new
    recast[...] = new.astype(BF16)
    per = norm.shape[1] // rows
    values = norm[...].astype(F32)
    tails = [ref[rank:, :].astype(F32) for ref in came]
    for i in range(norm.shape[0] * per):
        row, span = i // per, slice((i % per) * rows, (i % per + 1) * rows)
        summed = values[row : row + 1, span]
        for tail in tails:
            summed = summed + tail[i : i + 1, :]
        new_norm, moved_norm = outer_step(
            master_norm[row : row + 1, span], moment_norm[row : row + 1, span], summed, groups
        )
        norm_stored[row : row + 1, span] = new_norm
        norm_velocity[row : row + 1, span] = moved_norm
    norm_cast[...] = norm_stored[...].astype(BF16)


def pack_kernel(down, up, *refs):
    *outs, sems = refs
    shard = lax.axis_index("shard")
    rows, width = down.shape[2:]
    tall, cols = up.shape[2:]
    copies = []

    def bring(source, dest):
        copies.append(pltpu.make_async_copy(source, dest, sems.at[len(copies)]))
        copies[-1].start()

    for owner, out in reversed(list(zip(owners(), outs))):
        bring(down.at[owner, shard], out.at[pl.ds(0, rows)])
        for chunk in range(cols // width):
            bring(
                up.at[owner, shard, :, pl.ds(chunk * width, width)],
                out.at[pl.ds(rows + chunk * tall, tall)],
            )
    for copy in copies:
        copy.wait()


def add_kernel(block, came, *refs):
    refs[-1][...] = (block[...].astype(F32) + came[...].astype(F32)).astype(BF16)


def add(block, came, *after):
    return call(
        add_kernel,
        "add_block",
        jax.ShapeDtypeStruct(block.shape, BF16),
        [VMEM] * 2 + [ANY] * len(after),
        VMEM,
        [],
        block,
        came,
        *after,
    )


def pick_kernel(middle, end, *refs):
    out = refs[-1]
    pos = lax.axis_index("replica")
    outer = jnp.logical_or(pos == OUTER[0], pos == OUTER[1])

    @pl.when(outer)
    def _():
        out[...] = end[...]

    @pl.when(jnp.logical_not(outer))
    def _():
        out[...] = middle[...]


def pick(middle, end, *after):
    specs = [VMEM] * 2 + [ANY] * len(after)
    shape = jax.ShapeDtypeStruct(end.shape, end.dtype)
    return call(pick_kernel, "pick", shape, specs, VMEM, [], middle, end, *after)


def total(came, lo, hi):
    value = came[0][lo:hi, :].astype(F32)
    for ref in came[1:]:
        value = value + ref[lo:hi, :].astype(F32)
    return value


def rows_kernel(groups, tensors, n_came, *refs):
    refs = list(refs)
    master_down, moment_down, master_up, moment_up = refs[:4]
    came, state_came = refs[4 : 4 + n_came], refs[4 + n_came : 3 + n_came + tensors]
    piece, master, moment = refs[-3:]
    me = lax.axis_index("tensor")
    rows_down, width = master_down.shape
    rows_up = master_up.shape[0]
    tall, cols = master.shape

    def at(index):
        return pl.ds(pl.multiple_of(index * rows_up, rows_up), rows_up)

    own_cols = pl.ds(pl.multiple_of(me * cols, cols), cols)
    master[at(me), :] = master_up[:, own_cols]
    moment[at(me), :] = moment_up[:, own_cols]
    for shift in range(1, tensors):
        source = lax.rem(me + tensors - shift, tensors)
        master[at(source), :] = state_came[shift - 1][0]
        moment[at(source), :] = state_came[shift - 1][1]
    stored, _ = outer_step(
        master_down[...], moment_down[...], total(came, 0, rows_down), groups
    )
    piece[:rows_down, :] = stored.astype(BF16)
    for chunk in range(cols // width):
        lo = rows_down + chunk * tall
        span = slice(chunk * width, (chunk + 1) * width)
        stored, _ = outer_step(
            master[:, span], moment[:, span], total(came, lo, lo + tall), groups
        )
        piece[lo : lo + tall, :] = stored.astype(BF16)


def states_kernel(groups, tensors, n_came, *refs):
    master_down, moment_down = refs[:2]
    came = refs[2 : 2 + n_came]
    stored_down, velocity_down, *sums, summed = refs[-3 - tensors :]
    rows_down, width = master_down.shape
    rows_up = sums[0].shape[0]
    tall, cols = summed.shape
    me = lax.axis_index("tensor")
    stored, velocity = outer_step(
        master_down[...], moment_down[...], total(came, 0, rows_down), groups
    )
    stored_down[...] = stored
    velocity_down[...] = velocity
    for chunk in range(cols // width):
        lo = rows_down + chunk * tall
        summed[:, chunk * width : (chunk + 1) * width] = total(came, lo, lo + tall)
    for shift in range(tensors):
        owner = lax.rem(me + shift, tensors)
        sums[shift][...] = summed[pl.ds(pl.multiple_of(owner * rows_up, rows_up), rows_up), :]


def up_kernel(groups, tensors, master_up, moment_up, *refs):
    sums, (stored_up, velocity_up, token) = refs[:tensors], refs[-3:]
    cols = sums[0].shape[1]
    me = lax.axis_index("tensor")
    for shift in range(tensors):
        source = lax.rem(me + tensors - shift, tensors)
        span = pl.ds(pl.multiple_of(source * cols, cols), cols)
        stored, velocity = outer_step(
            master_up[:, span], moment_up[:, span], sums[shift][...], groups
        )
        stored_up[:, span] = stored
        velocity_up[:, span] = velocity
    token[...] = jnp.zeros_like(token)


def state_kernel(tensors, master_up, moment_up, *outs):
    me = lax.axis_index("tensor")
    cols = outs[0].shape[2]
    for shift in range(1, tensors):
        target = lax.rem(me + shift, tensors)
        span = pl.ds(pl.multiple_of(target * cols, cols), cols)
        outs[shift - 1][0] = master_up[:, span]
        outs[shift - 1][1] = moment_up[:, span]


def gate_kernel(x, *refs):
    refs[-1][...] = x[...]


def gate(x, *after):
    return call(
        gate_kernel,
        "gate",
        jax.ShapeDtypeStruct(x.shape, x.dtype),
        [VMEM] + [ANY] * len(after),
        VMEM,
        [],
        x,
        *after,
    )


def stack_kernel(count, *refs):
    for i in range(count):
        refs[-1][i] = refs[i][...]


def bundle(pieces, *after):
    return call(
        functools.partial(stack_kernel, len(pieces)),
        "bundle",
        jax.ShapeDtypeStruct((len(pieces),) + pieces[0].shape, BF16),
        [VMEM] * len(pieces) + [ANY] * len(after),
        VMEM,
        [],
        *pieces,
        *after,
    )


def place_kernel(keys, *refs):
    bundles, (down, up, token, sems) = refs[: len(keys)], refs[-4:]
    token[...] = jnp.zeros_like(token)
    shard = lax.axis_index("shard")
    rows, width = down.shape[2:]
    tall, cols = up.shape[2:]
    copies = []

    def send(source, dest):
        copies.append(pltpu.make_async_copy(source, dest, sems.at[len(copies)]))
        copies[-1].start()

    for pieces, (low, slots) in zip(bundles, keys):
        for i, (slot, mask) in enumerate(slots):
            owner, place = owners()[slot], jnp.bitwise_xor(shard, mask ^ low)
            send(pieces.at[i, pl.ds(0, rows)], down.at[owner, place])
            for chunk in range(cols // width):
                send(
                    pieces.at[i, pl.ds(rows + chunk * tall, tall)],
                    up.at[owner, place, :, pl.ds(chunk * width, width)],
                )
    for copy in copies:
        copy.wait()


def place_embed_kernel(slots, *refs):
    pieces, (out, token, sems) = refs[: len(slots)], refs[-3:]
    token[...] = jnp.zeros_like(token)
    copies = [
        pltpu.make_async_copy(piece, out.at[owners()[slot]], sems.at[i])
        for i, (piece, slot) in enumerate(zip(pieces, slots))
    ]
    for copy in copies:
        copy.start()
    for copy in copies:
        copy.wait()


def spread_low(x):
    found = {0: x}
    for bit in bits_down(lax.axis_size("shard") // 2):
        found.update({mask ^ bit: swap(y, "shard", bit) for mask, y in list(found.items())})
    return found


def body(
    trained_up,
    trained_down,
    trained_embed,
    trained_norm,
    master_up,
    moment_up,
    master_down,
    moment_down,
    master_embed,
    moment_embed,
    master_norm,
    moment_norm,
    embed_basis,
):
    replicas = lax.axis_size("replica")
    shards = lax.axis_size("shard")
    tensors = lax.axis_size("tensor")
    width, rank = embed_basis.shape
    rows_up, half_cols = master_up.shape[0], trained_up.shape[2]
    rows_down, rows_embed = master_down.shape[1], master_embed.shape[1]
    tall = tensors * rows_up
    chunks = half_cols // width
    packed = jax.ShapeDtypeStruct((rows_down + chunks * tall, width), BF16)
    dma = pltpu.SemaphoreType.DMA

    basis_t = embed_basis.T
    rank_rows = jax.ShapeDtypeStruct((rank, rows_embed), F32)
    packet = jax.ShapeDtypeStruct((rank + 16, rows_embed), BF16)
    token_shape = jax.ShapeDtypeStruct((8, 128), F32)
    own_rows, *packets = call(
        project_kernel,
        "project_rows",
        [rank_rows] + [packet] * (replicas - 1),
        [VMEM] * 3,
        [VMEM] * replicas,
        [pltpu.VMEM((rank, replicas * rows_embed), F32)],
        pltpu.with_memory_space_constraint(trained_embed[0], pltpu.HBM),
        pltpu.with_memory_space_constraint(basis_t, pltpu.HBM),
        pltpu.with_memory_space_constraint(trained_norm[0], pltpu.HBM),
    )
    down = trained_down[0].reshape(replicas, shards, rows_down, width)
    up = trained_up[0].reshape(replicas, shards, tall, half_cols)
    own, near, middle, end = call(
        pack_kernel,
        "pack_blocks",
        [packed] * replicas,
        [HBM] * 2,
        [VMEM] * replicas,
        [dma((replicas * (1 + chunks),))],
        pltpu.with_memory_space_constraint(down, pltpu.HBM),
        pltpu.with_memory_space_constraint(up, pltpu.HBM),
    )
    packets_came = [swap(packets[0], "replica", 1), swap(packets[1], "replica", 2)]
    end = gate(end, packets_came[0])
    packets_came.append(swap(gate(packets[2], end), "replica", 3))
    from_end = along(end, INWARD)

    state = jax.ShapeDtypeStruct((2, rows_up, half_cols), F32)
    states = call(
        functools.partial(state_kernel, tensors),
        "up_state",
        [state] * (tensors - 1),
        [VMEM] * 2,
        [VMEM] * (tensors - 1),
        [],
        master_up,
        moment_up,
    )
    states = [
        lax.ppermute(x, "tensor", [(i, (i + shift) % tensors) for i in range(tensors)])
        for shift, x in enumerate(states, 1)
    ]

    base = lax.dot_general(
        basis_t, master_embed[0], (((1,), (1,)), ((), ())), precision=HIGHEST
    )
    norm_state = jax.ShapeDtypeStruct(master_norm.shape, F32)
    embed_rows = jax.ShapeDtypeStruct((rows_embed, width), BF16)
    stored_rows, recast_rows, velocity_rows, norm_cast, stored_norm, velocity_norm = call(
        functools.partial(embed_kernel, replicas, replicas - 1),
        "embed_update",
        [
            jax.ShapeDtypeStruct((rows_embed, width), F32),
            embed_rows,
            rank_rows,
            jax.ShapeDtypeStruct(master_norm.shape, BF16),
            norm_state,
            norm_state,
        ],
        [VMEM] * (7 + replicas),
        [VMEM] * 6,
        [],
        own_rows,
        base,
        master_embed[0],
        moment_embed[0].T,
        basis_t,
        trained_norm[0],
        master_norm,
        moment_norm,
        *packets_came,
    )

    embed_out = along(recast_rows, OUTWARD)
    embed_middle = along(recast_rows, ACROSS)
    end_sum = gate(add(end, from_end), embed_middle)
    end_partial = along(end_sum, ACROSS)
    from_middle = along(gate(middle, from_end), INWARD)
    middle_sum = add(middle, from_middle, embed_out)
    middle_partial = along(middle_sum, ACROSS)
    from_near = along(gate(near, embed_out, from_middle), INWARD)
    embed_middle_out = along(embed_middle, OUTWARD)
    to_end = along(add(near, end_partial), OUTWARD)
    came0 = [own, from_near, middle_partial, to_end]
    half_sum = jax.ShapeDtypeStruct((rows_up, half_cols), F32)
    down_state = jax.ShapeDtypeStruct((rows_down, width), F32)
    piece = call(
        functools.partial(rows_kernel, replicas, tensors, len(came0)),
        "update_rows",
        packed,
        [VMEM] * (4 + len(came0) + len(states)) + [ANY],
        VMEM,
        [pltpu.VMEM((tall, half_cols), F32)] * 2,
        master_down[0],
        moment_down[0],
        master_up,
        moment_up,
        *came0,
        *states,
        embed_middle_out,
    )

    top = shards // 2
    came_near = swap(piece, "replica", 1)
    middle_piece = along(piece, ACROSS)
    far_piece = swap(piece, "shard", top)
    end_piece = along(came_near, ACROSS)
    second_out = along(middle_piece, OUTWARD)
    near_piece = gate(came_near, far_piece)
    far_near = swap(near_piece, "shard", top)
    stored_down, velocity_down, *sums = call(
        functools.partial(states_kernel, replicas, tensors, len(came0)),
        "update_states",
        [down_state, down_state] + [half_sum] * tensors,
        [VMEM] * (2 + len(came0)) + [ANY],
        [VMEM] * (2 + tensors),
        [pltpu.VMEM((tall, half_cols), F32)],
        master_down[0],
        moment_down[0],
        *came0,
        near_piece,
    )
    sums = [sums[0]] + [
        lax.ppermute(x, "tensor", [(i, (i + shift) % tensors) for i in range(tensors)])
        for shift, x in enumerate(sums[1:], 1)
    ]
    second = pick(middle_piece, second_out, far_near, sums[0])
    far_second = swap(second, "shard", top)
    embed_in = along(gate(recast_rows, near_piece), INWARD)
    embed_end = along(embed_in, ACROSS)
    third = pick(end_piece, along(end_piece, OUTWARD), far_second, embed_end, *sums[1:])
    far_third = swap(third, "shard", top)
    embed_last = along(embed_end, OUTWARD)
    bundles = [
        (
            [(0, 0), (0, top), (1, 0), (1, top), (2, 0), (2, top), (3, 0)],
            spread_low(
                bundle([piece, far_piece, near_piece, far_near, second, far_second, third])
            ),
        ),
    ]

    stored_up, velocity_up, token = call(
        functools.partial(up_kernel, replicas, tensors),
        "update_up",
        [jax.ShapeDtypeStruct(master_up.shape, F32)] * 2 + [token_shape],
        [VMEM] * (2 + tensors) + [ANY],
        [VMEM] * 3,
        [],
        master_up,
        moment_up,
        *sums,
        list(bundles[0][1].values())[-1],
    )

    embed_shape = jax.ShapeDtypeStruct((replicas, rows_embed, width), BF16)
    recast_embed, token = call(
        functools.partial(place_embed_kernel, [0, 1, 2]),
        "place_embed",
        [embed_shape, token_shape],
        [VMEM] * 4,
        [HBM, VMEM],
        [dma((3,))],
        recast_rows,
        pick(embed_in, embed_out),
        pick(embed_middle, embed_middle_out),
        token,
    )

    shapes = [jax.ShapeDtypeStruct(down.shape, BF16), jax.ShapeDtypeStruct(up.shape, BF16)]

    def place(slots, arrays, placed, *after):
        keys = [(low, slots) for low in arrays]
        count = len(keys) + len(after)
        return call(
            functools.partial(place_kernel, keys),
            "place_rows",
            shapes + [token_shape],
            [VMEM] * count + [HBM] * len(placed),
            [HBM] * 2 + [VMEM],
            [dma((len(keys) * len(slots) * (1 + chunks),))],
            *arrays.values(),
            *after,
            *placed,
            aliases={count: 0, count + 1: 1} if placed else {},
        )

    placed = []
    for slots, arrays in bundles:
        *placed, token = place(slots, arrays, placed, token)
    last = spread_low(bundle([far_third], token))
    recast_embed, token = call(
        functools.partial(place_embed_kernel, [3]),
        "place_embed",
        [embed_shape, token_shape],
        [VMEM] * 2 + [HBM],
        [HBM, VMEM],
        [dma((1,))],
        pick(embed_end, embed_last),
        last[0],
        recast_embed,
        aliases={2: 0},
    )
    recast_down, recast_up, _ = place([(3, top)], last, placed, token)

    return (
        recast_up.reshape(-1, half_cols),
        recast_down.reshape(-1, width),
        recast_embed.reshape(-1, width),
        norm_cast,
        stored_up,
        velocity_up,
        stored_down[None],
        velocity_down[None],
        stored_rows[None],
        velocity_rows.T[None],
        stored_norm,
        velocity_norm,
    )


def solution(mesh):
    in_specs = (
        P("replica", None, "tensor"),
        P("replica", "tensor", None),
        P("replica", ("shard", "tensor"), None),
        P("replica", None, None),
        P(("replica", "shard", "tensor"), None),
        P(("replica", "shard", "tensor"), None),
        P("tensor", ("replica", "shard"), None),
        P("tensor", ("replica", "shard"), None),
        P(("shard", "tensor"), "replica", None),
        P(("shard", "tensor"), "replica", None),
        P(),
        P(),
        P(),
    )
    out_specs = (
        P(None, "tensor"),
        P("tensor", None),
        P(("shard", "tensor"), None),
        P(),
        P(("replica", "shard", "tensor"), None),
        P(("replica", "shard", "tensor"), None),
        P("tensor", ("replica", "shard"), None),
        P("tensor", ("replica", "shard"), None),
        P(("shard", "tensor"), "replica", None),
        P(("shard", "tensor"), "replica", None),
        P(),
        P(),
    )
    return jax.shard_map(body, mesh=mesh, in_specs=in_specs, out_specs=out_specs, check_vma=False)
```
